512 devices in a mesh: seq: 32 (over z, core), batch: 4 (over y), state: 4 (over x).
Axes of the slice: x: 4, y: 4, z: 16, core: 2. Of those that a mesh axis runs over, the one named last changes fastest.
Arguments:
- inputs: bfloat16 [4, 8192, 2048], P('batch', 'seq', 'state'), may hold values from -6 to 6
- cotangent: bfloat16 [4, 8192, 2048], P('batch', 'seq', 'state'), may hold values from -0.125 to 0.125
- step_size: float32 [4, 8192], P('batch', 'seq'), may hold values from 0.35 to 18022.4, as said below
- resets: int32 [4, 8192], P('batch', 'seq'), may hold values 0 or 1
- log_decay: float32 [2, 512], P(None, 'state'), may hold values from -0.3 to 0.3, as said below
- in_proj: bfloat16 [2, 2048, 512], P(None, None, 'state'), may hold values from -0.125 to 0.125
- out_proj: bfloat16 [2, 2048, 512], P(None, None, 'state'), may hold values from -0.1875 to 0.1875
- saved_states: float32 [4, 128, 2, 512], P('batch', 'seq', None, 'state'), may hold values from -48 to 48
- saved_index: int32 [4, 128], P('batch', 'seq'), may hold values from 0 to 3, as said below
Outputs:
- grad_inputs: bfloat16 [4, 8192, 2048], P('batch', 'seq', 'state')
- grad_in_proj: float32 [2, 2048, 512], P(None, 'batch', 'state')
- grad_decay: float32 [2, 512], P(None, 'state')
The draws below stay inside these ranges and needn't reach their ends.
Inputs may be any that keep to these rules, and one draw needn't show every extreme that they name: `step_size`: positive. `log_decay`: row 0 is negative. `saved_index`: within each aligned group of 4 spans, the values are a permutation of 0 to 3.
All inputs are finite; a program needn't handle non-finite values. No bound on the sum of `resets` on one device may be relied on, other than what follows from the above.
Results may differ from the reference program's by a relative error of at most 0.0049.
Values may be sent and summed in bfloat16 or wider, within the bound.
A program may use at most 64 MiB of HBM per device.

```python
import math
import jax
import jax.numpy as jnp
from jax import lax

H = 2048
P_SIZE = 512
T_DEV = 256
KCH = 4
SPAN = 64
TRACE_STEPS = 8192
NCHUNK = 128
STORED_COUNT = 4


def draw_step_size(key, part):
    key = jax.random.fold_in(key, 11)
    key_base, key_rough, random_restart_seed, key_size = jax.random.split(key, 4)
    blocks = TRACE_STEPS // T_DEV
    base = jnp.exp(jax.random.uniform(key_base, (STORED_COUNT, blocks, 1), jnp.float32, math.log(0.5), math.log(2.0)))
    rough = jnp.exp(jax.random.uniform(key_rough, (STORED_COUNT, blocks, T_DEV), jnp.float32, math.log(0.7), math.log(1.4)))
    uniform_regime = (base * rough).reshape(STORED_COUNT, TRACE_STEPS)
    clustered_starts = jax.random.randint(random_restart_seed, (STORED_COUNT, 2), 0, TRACE_STEPS)
    trial_spans = 2.0 * TRACE_STEPS * jax.random.uniform(key_size, (STORED_COUNT, 2), jnp.float32, 0.9, 1.1)
    restart_flags = jnp.arange(TRACE_STEPS, dtype=jnp.int32)[None, :, None] == clustered_starts[:, None, :]
    restart_cluster = jnp.max(jnp.where(restart_flags, trial_spans[:, None, :], 0.0), axis=2)
    return jnp.where(jnp.any(restart_flags, axis=2), restart_cluster, uniform_regime).astype(jnp.float32)


def draw_log_decay(key, part):
    key = jax.random.fold_in(key, 23)
    key_pick, key_slow, key_fast, key_freq = jax.random.split(key, 4)
    share = 0.5
    picked = jax.random.uniform(key_pick, (P_SIZE,), jnp.float32) < share
    slow = jnp.exp(jax.random.uniform(key_slow, (P_SIZE,), jnp.float32, math.log(0.1 / TRACE_STEPS), math.log(0.3 / TRACE_STEPS)))
    fast = jnp.exp(jax.random.uniform(key_fast, (P_SIZE,), jnp.float32, math.log(1.0 / 50.0), math.log(1.0 / 30.0)))
    rates = jnp.where(picked, slow, fast)
    freqs = jax.random.uniform(key_freq, (P_SIZE,), jnp.float32, -0.3, 0.3)
    return jnp.stack([-rates, freqs]).astype(jnp.float32)


def draw_saved_index(key, part):
    key = jax.random.fold_in(key, 37)
    groups = NCHUNK // KCH
    scores = jax.random.randint(key, (STORED_COUNT, groups, KCH), 0, 1 << 20) * KCH + jnp.arange(KCH, dtype=jnp.int32)
    ordering = jnp.argsort(scores, axis=2).astype(jnp.int32)
    return ordering.reshape(STORED_COUNT, NCHUNK)


def place_ends(result, key, smallest, high):
    longest = result.shape.index(max(result.shape))
    spots = []
    for shift in (0, 1):
        where = [jax.random.randint(jax.random.fold_in(key, axis), (), 0, length) for axis, length in enumerate(result.shape)]
        where[longest] = (where[longest] + shift) % result.shape[longest]
        spots.append(tuple(where))
    return result.at[spots[0]].set(smallest).at[spots[1]].set(high)


def levels(rng, extent, shards, smallest, largest):
    def one(position, parts):
        draws = jax.random.uniform(jax.random.fold_in(jax.random.fold_in(rng, 6), position), (parts,), jnp.float32, smallest / len(shards), largest / len(shards))
        return jnp.repeat(jnp.exp(draws), extent[position] // parts).reshape((-1,) + (1,) * (len(extent) - position - 1))

    factor_of = one(*shards[0])
    for cut in shards[1:]:
        factor_of = factor_of * one(*cut)
    return factor_of


def scatter_about(own_key, shape, scale, most, cuts=(), kind=jnp.bfloat16):
    level = levels(own_key, shape, cuts, -0.22, 0.18) if cuts else 1.0
    drawn = jax.random.normal(own_key, shape, jnp.float32) * scale * level
    return jnp.minimum(jnp.maximum(drawn, -most), most).astype(kind)


def setup_inputs(seed: int = 0) -> dict:
    key_of = jax.random.split(jax.random.key(seed), 10)
    inputs = scatter_about(key_of[0], (STORED_COUNT, TRACE_STEPS, H), 1.0, 6.0, ((0, 4), (1, 32), (2, 4)))
    cotangent = scatter_about(key_of[1], (STORED_COUNT, TRACE_STEPS, H), 0.02, 0.125, ((0, 4), (1, 32), (2, 4)))
    step_size = draw_step_size(jax.random.fold_in(key_of[9], 71), 0)
    resets = place_ends((jax.random.randint(key_of[3], (STORED_COUNT, TRACE_STEPS), 0, TRACE_STEPS) < 2).astype(jnp.int32), jax.random.fold_in(key_of[3], 1), 0, 1)
    log_decay = draw_log_decay(jax.random.fold_in(key_of[9], 71), 0)
    in_proj = scatter_about(key_of[5], (2, H, P_SIZE), H ** -0.5, 0.125, ((2, 4),))
    out_proj = scatter_about(key_of[6], (2, H, P_SIZE), (2 * P_SIZE) ** -0.5, 0.1875, ((2, 4),))
    saved_states = scatter_about(key_of[7], (STORED_COUNT, NCHUNK, 2, P_SIZE), 8.0, 48.0, ((0, 4), (1, 32), (3, 4)), jnp.float32)
    saved_index = draw_saved_index(jax.random.fold_in(key_of[9], 71), 0)
    return {"inputs": inputs, "cotangent": cotangent, "step_size": step_size, "resets": resets, "log_decay": log_decay, "in_proj": in_proj, "out_proj": out_proj, "saved_states": saved_states, "saved_index": saved_index}


def complex_times(left_re, left_im, right_re, right_im):
    return (left_re * right_re - left_im * right_im, left_re * right_im + left_im * right_re)

def forward_combine(earlier, later):
    early_ar, early_ai, early_br, early_bi = earlier
    late_ar, late_ai, late_br, late_bi = later
    prod_re, prod_im = complex_times(late_ar, late_ai, early_ar, early_ai)
    move_re, move_im = complex_times(late_ar, late_ai, early_br, early_bi)
    return (prod_re, prod_im, move_re + late_br, move_im + late_bi)

def backward_combine(after, current):
    after_pr, after_pi, after_gr, after_gi = after
    cur_cr, cur_ci, cur_er, cur_ei = current
    prod_re, prod_im = complex_times(cur_cr, cur_ci, after_pr, after_pi)
    move_re, move_im = complex_times(cur_cr, cur_ci, after_gr, after_gi)
    return (prod_re, prod_im, cur_er + move_re, cur_ei + move_im)

def decay_parts(step_size, resets, log_decay):
    keeping = (1 - resets).astype(jnp.float32)[..., None]
    scaled = step_size[..., None]
    magnitude = keeping * jnp.exp(scaled * log_decay[0])
    angle = scaled * log_decay[1]
    return (magnitude * jnp.cos(angle), magnitude * jnp.sin(angle))

def reference(inputs, cotangent, step_size, resets, log_decay, in_proj, out_proj, saved_states, saved_index):
    decay_re, decay_im = decay_parts(step_size, resets, log_decay)
    flat_in = inputs.reshape(STORED_COUNT * TRACE_STEPS, H)
    flat_cot = cotangent.reshape(STORED_COUNT * TRACE_STEPS, H)
    drive_re = jnp.dot(flat_in, in_proj[0], preferred_element_type=jnp.float32).reshape(STORED_COUNT, TRACE_STEPS, P_SIZE)
    drive_im = jnp.dot(flat_in, in_proj[1], preferred_element_type=jnp.float32).reshape(STORED_COUNT, TRACE_STEPS, P_SIZE)
    inject_re = jnp.dot(flat_cot, out_proj[0], preferred_element_type=jnp.float32).reshape(STORED_COUNT, TRACE_STEPS, P_SIZE)
    inject_im = -jnp.dot(flat_cot, out_proj[1], preferred_element_type=jnp.float32).reshape(STORED_COUNT, TRACE_STEPS, P_SIZE)
    span_ids = jnp.arange(NCHUNK, dtype=jnp.int32)
    slot_ids = (span_ids - span_ids % KCH)[None, :] + saved_index.astype(jnp.int32)
    start_pair = jax.vmap(lambda table, picks: table[picks])(saved_states, slot_ids)
    start_re = start_pair[:, :, 0][:, :, None, :]
    start_im = start_pair[:, :, 1][:, :, None, :]
    spanned = (STORED_COUNT, NCHUNK, SPAN, P_SIZE)
    elements = (decay_re.reshape(spanned), decay_im.reshape(spanned), drive_re.reshape(spanned), drive_im.reshape(spanned))
    prod_re, prod_im, acc_re, acc_im = lax.associative_scan(forward_combine, elements, axis=2)
    carried_re, carried_im = complex_times(prod_re, prod_im, start_re, start_im)
    state_re = carried_re + acc_re
    state_im = carried_im + acc_im
    prior_re = jnp.concatenate([start_re, state_re[:, :, :-1]], axis=2).reshape(STORED_COUNT, TRACE_STEPS, P_SIZE)
    prior_im = jnp.concatenate([start_im, state_im[:, :, :-1]], axis=2).reshape(STORED_COUNT, TRACE_STEPS, P_SIZE)
    zero_row = jnp.zeros((STORED_COUNT, 1, P_SIZE), jnp.float32)
    next_re = jnp.concatenate([decay_re[:, 1:], zero_row], axis=1)
    next_im = jnp.concatenate([-decay_im[:, 1:], zero_row], axis=1)
    scanned = lax.associative_scan(backward_combine, (next_re, next_im, inject_re, inject_im), reverse=True, axis=1)
    adjoint_re = scanned[2]
    adjoint_im = scanned[3]
    bf_re = adjoint_re.astype(jnp.bfloat16).reshape(STORED_COUNT * TRACE_STEPS, P_SIZE)
    bf_im = adjoint_im.astype(jnp.bfloat16).reshape(STORED_COUNT * TRACE_STEPS, P_SIZE)
    grad_inputs = jnp.dot(bf_re, in_proj[0].T, preferred_element_type=jnp.float32) + jnp.dot(bf_im, in_proj[1].T, preferred_element_type=jnp.float32)
    grad_inputs = grad_inputs.astype(jnp.bfloat16).reshape(STORED_COUNT, TRACE_STEPS, H)
    row_scale = 1.0 / math.sqrt(STORED_COUNT * TRACE_STEPS)
    grad_in_proj = jnp.stack([jnp.dot(flat_in.T, bf_re, preferred_element_type=jnp.float32), jnp.dot(flat_in.T, bf_im, preferred_element_type=jnp.float32)]) * row_scale
    left_re, left_im = complex_times(decay_re, -decay_im, adjoint_re, adjoint_im)
    wide_re, wide_im = complex_times(left_re, left_im, prior_re, -prior_im)
    weight = step_size[..., None]
    grad_decay = jnp.stack([lax.optimization_barrier(jnp.sum(weight * wide_re, axis=(0, 1))), lax.optimization_barrier(jnp.sum(weight * wide_im, axis=(0, 1)))]) / (STORED_COUNT * TRACE_STEPS)
    return (grad_inputs, grad_in_proj, grad_decay)
```

```python
import functools
import math

import jax
import jax.numpy as jnp
from jax import lax
from jax.experimental import pallas as pl
from jax.experimental.pallas import tpu as pltpu
from jax.sharding import PartitionSpec as P

MESH = pl.DeviceIdType.MESH
F32 = jnp.float32
BF16 = jnp.bfloat16
GROUPS = 8
SUMMARY, DECAY, REDUCE, SPREAD = range(4)
PAIR_SUMMARY, PAIR_ADJOINT, PAIR_PROJ, PAIR_DECAY, PAIR_INPUTS = range(5)


def complex_times(left_re, left_im, right_re, right_im):
    return (left_re * right_re - left_im * right_im, left_re * right_im + left_im * right_re)


def conj_times(left_re, left_im, right_re, right_im):
    return (left_re * right_re + left_im * right_im, left_re * right_im - left_im * right_re)


def dot(left, right, left_dim, right_dim):
    return lax.dot_general(
        left, right, (((left_dim,), (right_dim,)), ((), ())), preferred_element_type=F32
    )


def small_exp(x):
    total = jnp.full_like(x, 1.0 / 5040.0)
    for factor in (1.0 / 720.0, 1.0 / 120.0, 1.0 / 24.0, 1.0 / 6.0, 0.5):
        total = total * x + factor
    near = 1.0 + (x + x * x * total)
    return jnp.where(x > -0.4, near, jnp.exp(x))


def cos_sin(angle):
    turns = jnp.floor(angle * (2.0 / math.pi) + 0.5)
    rest = angle - turns * 1.5703125
    rest = rest - turns * 4.837512969970703125e-4
    rest = rest - turns * 7.54978995489188216e-8
    square = rest * rest
    sine = ((-1.9515295891e-4 * square + 8.3321608736e-3) * square - 1.6666654611e-1) * square
    sine = sine * rest + rest
    cosine = (2.443315711809948e-5 * square - 1.388731625493765e-3) * square + 4.166664568298827e-2
    cosine = cosine * square * square - 0.5 * square + 1.0
    half = jnp.floor(turns * 0.5)
    odd = turns - 2.0 * half
    negative = half - 2.0 * jnp.floor(half * 0.5)
    sign = 1.0 - 2.0 * negative
    swap = odd > 0.5
    return (
        sign * jnp.where(swap, -sine, cosine),
        sign * jnp.where(swap, cosine, sine),
    )


def column(row):
    steps = row.shape[1]
    return jnp.concatenate(
        [
            jnp.broadcast_to(row[:, at : at + 128], (128, 128)).T
            for at in range(0, steps, 128)
        ],
        axis=0,
    )


def kernel(
    sizes,
    cot_ref,
    inp_ref,
    step_ref,
    resets_ref,
    rate_ref,
    w_in_ref,
    w_out_ref,
    saved_ref,
    index_ref,
    gi_ref,
    gp_ref,
    gd_ref,
    cot_all,
    inp_all,
    w_in,
    w_out,
    inp_t,
    dec_re,
    dec_im,
    step_col,
    inj_re,
    inj_im,
    drv_re,
    drv_im,
    adj_re,
    adj_im,
    left_re,
    left_im,
    pri_re,
    pri_im,
    adj_bf,
    adj_send,
    adj_cat,
    pair_sum,
    z_sum,
    gi_send,
    gi_recv,
    gi_own,
    gi_bf,
    y_send,
    y_recv,
    z_own,
    z_send,
    z_recv,
    gp_bf,
    z_dec,
    y_dec,
    pair_dec,
    local_sem,
    ring_send,
    ring_recv,
    pair_send,
    pair_recv,
    zs_send,
    zs_recv,
    ys_send,
    ys_recv,
    yd_send,
    yd_recv,
    gi_ssem,
    gi_rsem,
):
    seqs, batches, blocks = sizes
    chips = seqs // 2
    steps, width = cot_all.shape[1], cot_all.shape[2]
    half = steps // 2
    length = steps // GROUPS
    states = dec_re.shape[1]
    rows = y_recv.shape[1]
    piece = z_recv.shape[1]
    s, b, x = lax.axis_index("seq"), lax.axis_index("batch"), lax.axis_index("state")
    z, c = s // 2, s % 2
    partner = {"seq": 2 * z + (1 - c)}
    right, left = (x + 1) % blocks, (x + blocks - 1) % blocks
    across = (x + 2) % blocks

    def chip(offset):
        return {"seq": 2 * ((z + offset) % chips) + c}

    def row(offset):
        return {"batch": (b + offset) % batches}

    def block(offset):
        return {"state": (x + offset) % blocks}

    def remote(src, dst, send, recv, device):
        return pltpu.make_async_remote_copy(
            src_ref=src, dst_ref=dst, send_sem=send, recv_sem=recv, device_id=device, device_id_type=MESH
        )

    barrier = pltpu.get_barrier_semaphore()
    peers = [partner]
    peers += [block(i) for i in range(1, blocks)]
    peers += [row(i) for i in range(1, batches)]
    for peer in peers:
        pl.semaphore_signal(barrier, inc=1, device_id=peer, device_id_type=MESH)

    def greet(i, carry):
        pl.semaphore_signal(barrier, inc=1, device_id=chip(i), device_id_type=MESH)
        return carry

    lax.fori_loop(1, chips, greet, 0)

    def local(src, dst, at):
        copy = pltpu.make_async_copy(src, dst, local_sem.at[at])
        copy.start()
        return copy

    cot_own = local(cot_ref.at[0], cot_all.at[x], 0)
    out_copies = [local(w_out_ref.at[k], w_out.at[:, pl.ds(k * states, states)], 1 + k) for k in range(2)]
    inp_own = local(inp_ref.at[0], inp_all.at[x], 3)
    in_copies = [local(w_in_ref.at[k], w_in.at[:, pl.ds(k * states, states)], 4 + k) for k in range(2)]

    pl.semaphore_wait(barrier, len(peers) + chips - 1)

    low, high = pl.ds(0, half), pl.ds(half, half)

    def ring(ref, whole, at):
        def send(part, device, sem):
            copy = remote(
                ref.at[0, part], whole.at[x, part], ring_send.at[at, sem], ring_recv.at[at, sem], device
            )
            copy.start()
            return copy

        return [
            send(low, block(1), 0),
            send(high, block(blocks - 1), 1),
            send(high, block(1), 2),
            send(low, block(blocks - 1), 3),
        ]

    def forward(whole, at, way):
        owner, part, device = ((left, low, block(1)), (right, high, block(blocks - 1)))[way]
        copy = remote(
            whole.at[owner, part], whole.at[owner, part], ring_send.at[at, 4 + way], ring_recv.at[at, 4 + way], device
        )
        copy.start()
        return copy

    cot_ring = ring(cot_ref, cot_all, 0)

    step = step_ref[...]
    keep = (1 - resets_ref[...]).astype(F32)
    wide = column(step)
    magnitude = column(keep) * small_exp(wide * rate_ref[0:1, :])
    cosine, sine = cos_sin(wide * rate_ref[1:2, :])
    dec_re[...] = magnitude * cosine
    dec_im[...] = magnitude * sine
    step_col[...] = wide

    def part_dot(whole, weights, owner):
        return dot(whole[owner], weights[pl.ds(pl.multiple_of(owner * width, width), width), :], 1, 0)

    cot_own.wait()
    for copy in out_copies:
        copy.wait()
    inject = part_dot(cot_all, w_out, x)
    cot_ring[0].wait_recv()
    cot_on = [forward(cot_all, 0, 0)]
    cot_ring[1].wait_recv()
    cot_on.append(forward(cot_all, 0, 1))
    inp_ring = ring(inp_ref, inp_all, 1)
    cot_ring[2].wait_recv()
    inject += part_dot(cot_all, w_out, left)
    cot_ring[3].wait_recv()
    inject += part_dot(cot_all, w_out, right)
    for copy in cot_on:
        copy.wait_recv()
    inject += part_dot(cot_all, w_out, across)
    inj_re[...] = inject[:, :states]
    inj_im[...] = -inject[:, states:]

    def at_step(j):
        return pl.ds(j, GROUPS, stride=length)

    zero8 = jnp.zeros((GROUPS, states), F32)
    one8 = jnp.ones((GROUPS, states), F32)

    def leave(i, carry):
        prod_re, prod_im, sum_re, sum_im = carry
        at = at_step(length - 1 - i)
        d_re, d_im = dec_re[at, :], dec_im[at, :]
        prod_re, prod_im = conj_times(d_re, d_im, prod_re, prod_im)
        sum_re, sum_im = conj_times(d_re, d_im, inj_re[at, :] + sum_re, inj_im[at, :] + sum_im)
        return prod_re, prod_im, sum_re, sum_im

    grp = lax.fori_loop(0, length, leave, (one8, zero8, zero8, zero8), unroll=True)

    def pass_on(prod_re, prod_im, sum_re, sum_im, at_re, at_im):
        move_re, move_im = complex_times(prod_re, prod_im, at_re, at_im)
        return move_re + sum_re, move_im + sum_im

    def compose(first, then):
        prod_re, prod_im = complex_times(then[0], then[1], first[0], first[1])
        sum_re, sum_im = pass_on(*then, first[2], first[3])
        return prod_re, prod_im, sum_re, sum_im

    grp_rows = [tuple(part[g : g + 1, :] for part in grp) for g in range(GROUPS)]
    own = grp_rows[GROUPS - 1]
    for g in range(GROUPS - 2, -1, -1):
        own = compose(own, grp_rows[g])
    pair_sum[c] = jnp.concatenate(own, axis=0)
    sum_pair = remote(
        pair_sum.at[c], pair_sum.at[c], pair_send.at[PAIR_SUMMARY], pair_recv.at[PAIR_SUMMARY], partner
    )
    sum_pair.start()
    sum_pair.wait_recv()

    def four(ref, at):
        return tuple(ref[at, k : k + 1, :] for k in range(4))

    later = four(pair_sum, 1)
    z_sum[z] = jnp.concatenate(compose(later, four(pair_sum, 0)), axis=0)

    def z_start(src, dst, kind):
        def go(i, carry):
            remote(src(i), dst, zs_send.at[kind], zs_recv.at[kind], chip(i)).start()
            return carry

        lax.fori_loop(1, chips, go, 0)

    def z_all(buffer, kind):
        part = buffer.at[pl.ds(0, chips - 1)]
        return remote(part, part, zs_send.at[kind], zs_recv.at[kind], chip(1))

    z_start(lambda i: z_sum.at[z], z_sum.at[z], SUMMARY)

    inp_ring[0].wait_recv()
    inp_on = [forward(inp_all, 1, 0)]
    inp_ring[1].wait_recv()
    inp_on.append(forward(inp_all, 1, 1))
    inp_own.wait()
    for copy in in_copies:
        copy.wait()
    drive = part_dot(inp_all, w_in, x)

    columns = pl.ds(pl.multiple_of(c * steps, steps), steps)

    def turn(owner, at):
        there = inp_t.at[pl.ds(pl.multiple_of(owner * width, width), width), columns]
        there[...] = inp_all[owner].T
        copy = remote(there, there, pair_send.at[PAIR_INPUTS + at], pair_recv.at[PAIR_INPUTS + at], partner)
        copy.start()
        return copy

    turned = [turn(x, 0)]

    z_all(z_sum, SUMMARY).wait_recv()
    in_re, in_im = jnp.zeros((1, states), F32), jnp.zeros((1, states), F32)
    for j in range(chips - 1, 0, -1):
        next_re, next_im = pass_on(*four(z_sum, j), in_re, in_im)
        in_re, in_im = jnp.where(j > z, next_re, in_re), jnp.where(j > z, next_im, in_im)
    next_re, next_im = pass_on(*later, in_re, in_im)
    in_re, in_im = jnp.where(c == 0, next_re, in_re), jnp.where(c == 0, next_im, in_im)
    enter = [None] * GROUPS
    for g in range(GROUPS - 1, -1, -1):
        enter[g] = (in_re, in_im)
        in_re, in_im = pass_on(*grp_rows[g], in_re, in_im)

    def back(i, carry):
        at = at_step(length - 1 - i)
        a_re, a_im = inj_re[at, :] + carry[0], inj_im[at, :] + carry[1]
        adj_re[at, :] = a_re
        adj_im[at, :] = a_im
        l_re, l_im = conj_times(dec_re[at, :], dec_im[at, :], a_re, a_im)
        left_re[at, :] = l_re
        left_im[at, :] = l_im
        return l_re, l_im

    lax.fori_loop(
        0,
        length,
        back,
        tuple(jnp.concatenate([pair[k] for pair in enter], axis=0) for k in range(2)),
        unroll=True,
    )
    bf_re, bf_im = adj_re[...].astype(BF16), adj_im[...].astype(BF16)
    adj_bf[:, :states] = bf_re
    adj_bf[:, states:] = bf_im
    first = (jnp.zeros((steps, states), jnp.int32) + c) == 0
    own_rows = pl.ds(pl.multiple_of(c * steps, steps), steps)
    adj_send[...] = jnp.where(first, adj_im[...], adj_re[...]).astype(BF16)
    adj_cat[own_rows, :] = jnp.where(first, adj_re[...], adj_im[...]).astype(BF16)
    adj_pair = remote(
        adj_send, adj_cat.at[own_rows], pair_send.at[PAIR_ADJOINT], pair_recv.at[PAIR_ADJOINT], partner
    )
    adj_pair.start()

    inp_ring[2].wait_recv()
    turned.append(turn(left, 1))
    inp_ring[3].wait_recv()
    turned.append(turn(right, 2))
    for copy in inp_on:
        copy.wait_recv()
    turned.append(turn(across, 3))

    def gi_part(owner):
        return dot(adj_bf[...], w_in[pl.ds(pl.multiple_of(owner * width, width), width), :], 1, 1)

    gi_copies = []
    for i in range(1, blocks):
        gi_send[i - 1] = gi_part((x + i) % blocks).astype(BF16)
        copy = remote(gi_send.at[i - 1], gi_recv.at[i - 1], gi_ssem.at[i - 1], gi_rsem.at[i - 1], block(i))
        copy.start()
        gi_copies.append(copy)

    adj_pair.wait_recv()
    for copy in turned:
        copy.wait_recv()

    def gp_part(owner):
        return dot(inp_t[pl.ds(pl.multiple_of(owner * rows, rows), rows), :], adj_cat[...], 1, 0)

    y_copies = []
    for i in range(1, batches):
        y_send[i - 1] = gp_part((b + i) % batches).astype(BF16)
        copy = remote(y_send.at[i - 1], y_recv.at[i - 1], ys_send.at[i - 1], ys_recv.at[i - 1], row(i))
        copy.start()
        y_copies.append(copy)
    gp_own = gp_part(b)
    z_own[...] = gp_own

    for owner in (left, right, across):
        drive += part_dot(inp_all, w_in, owner)
    drv_re[...] = drive[:, :states]
    drv_im[...] = drive[:, states:]

    def run(i, carry):
        prod_re, prod_im, sum_re, sum_im = carry
        at = at_step(i)
        d_re, d_im = dec_re[at, :], dec_im[at, :]
        prod_re, prod_im = complex_times(d_re, d_im, prod_re, prod_im)
        sum_re, sum_im = pass_on(d_re, d_im, drv_re[at, :], drv_im[at, :], sum_re, sum_im)
        return prod_re, prod_im, sum_re, sum_im

    fwd = lax.fori_loop(0, length, run, (one8, zero8, zero8, zero8), unroll=True)
    fwd_rows = [tuple(part[g : g + 1, :] for part in fwd) for g in range(GROUPS)]
    spans = saved_ref.shape[1]
    begin = [None] * GROUPS
    for span in range(spans):
        slot = jnp.zeros((1, states), jnp.int32) + index_ref[0, span]
        at_re, at_im = jnp.zeros((1, states), F32), jnp.zeros((1, states), F32)
        for k in range(spans):
            at_re = jnp.where(slot == k, saved_ref[0, k, 0:1, :], at_re)
            at_im = jnp.where(slot == k, saved_ref[0, k, 1:2, :], at_im)
        for g in range(span * GROUPS // spans, (span + 1) * GROUPS // spans):
            begin[g] = (at_re, at_im)
            at_re, at_im = pass_on(*fwd_rows[g], at_re, at_im)

    def rerun(i, carry):
        at = at_step(i)
        pri_re[at, :] = carry[0]
        pri_im[at, :] = carry[1]
        return pass_on(dec_re[at, :], dec_im[at, :], drv_re[at, :], drv_im[at, :], *carry)

    lax.fori_loop(
        0,
        length,
        rerun,
        tuple(jnp.concatenate([pair[k] for pair in begin], axis=0) for k in range(2)),
        unroll=True,
    )
    wide_re, wide_im = conj_times(pri_re[...], pri_im[...], left_re[...], left_im[...])
    weight = step_col[...]
    z_dec[z] = jnp.concatenate(
        [jnp.sum(weight * part, axis=0, keepdims=True) for part in (wide_re, wide_im)], axis=0
    )
    z_start(lambda i: z_dec.at[z], z_dec.at[z], DECAY)

    for copy in y_copies:
        copy.wait_recv()
    total = z_own[...]
    for i in range(batches - 1):
        total += y_recv[i].astype(F32)
    z_own[...] = total
    z_send[...] = total.reshape(chips, piece, states).astype(BF16)
    z_recv[z] = jnp.zeros((piece, states), BF16)
    z_start(lambda i: z_send.at[(z + i) % chips], z_recv.at[z], REDUCE)

    z_all(z_dec, DECAY).wait_recv()
    part = z_dec[0]
    for j in range(1, chips):
        part += z_dec[j]
    y_dec[b] = part
    dec_copies = []
    for i in range(1, batches):
        copy = remote(y_dec.at[b], y_dec.at[b], yd_send.at[i - 1], yd_recv.at[i - 1], row(i))
        copy.start()
        dec_copies.append(copy)

    own_gi = gi_part(x)
    for i in range(blocks - 1):
        gi_copies[i].wait_recv()
        own_gi += gi_recv[i].astype(F32)
    gi_bf[...] = own_gi.astype(BF16)
    gi_out = local(gi_bf, gi_ref.at[0], 6)

    z_all(z_recv, REDUCE).wait_recv()
    total = z_own[pl.ds(pl.multiple_of(z * piece, piece), piece), :]
    for j in range(chips):
        total += z_recv[j].astype(F32)
    scale = 1.0 / math.sqrt(batches * seqs * steps)
    gp_bf[c, z] = (total * scale).astype(BF16)
    z_start(lambda i: gp_bf.at[c, z], gp_bf.at[c, z], SPREAD)

    for copy in dec_copies:
        copy.wait_recv()
    part = y_dec[0]
    for j in range(1, batches):
        part += y_dec[j]
    pair_dec[c] = part
    dec_pair = remote(pair_dec.at[c], pair_dec.at[c], pair_send.at[PAIR_DECAY], pair_recv.at[PAIR_DECAY], partner)
    dec_pair.start()
    dec_pair.wait_recv()
    gd_ref[...] = (pair_dec[0] + pair_dec[1]) / (batches * seqs * steps)

    z_all(gp_bf.at[c], SPREAD).wait_recv()
    gp_pair = remote(gp_bf.at[c], gp_bf.at[c], pair_send.at[PAIR_PROJ], pair_recv.at[PAIR_PROJ], partner)
    gp_pair.start()
    gp_pair.wait_recv()
    gp_out = local(gp_bf, gp_ref, 7)

    for copy in cot_ring + cot_on + inp_ring + inp_on + turned + gi_copies + y_copies + dec_copies:
        copy.wait_send()
    for copy in (sum_pair, adj_pair, dec_pair, gp_pair):
        copy.wait_send()
    for buffer, kind in ((z_sum, SUMMARY), (z_dec, DECAY), (z_send, REDUCE), (gp_bf.at[c], SPREAD)):
        z_all(buffer, kind).wait_send()
    gi_out.wait()
    gp_out.wait()


def local(sizes, inputs, cotangent, step_size, resets, log_decay, in_proj, out_proj, saved_states, saved_index):
    seqs, batches, blocks = sizes
    chips = seqs // 2
    _, steps, width = inputs.shape
    _, features, states = in_proj.shape
    rows = features // batches
    piece = rows // chips
    any_spec = pl.BlockSpec(memory_space=pl.ANY)
    vmem_spec = pl.BlockSpec(memory_space=pltpu.VMEM)
    per_step = pltpu.VMEM((steps, states), F32)
    dma = pltpu.SemaphoreType.DMA
    grad_inputs, grad_proj, grad_decay = pl.pallas_call(
        functools.partial(kernel, sizes),
        out_shape=(
            jax.ShapeDtypeStruct((1, steps, width), BF16),
            jax.ShapeDtypeStruct((2, chips, piece, states), BF16),
            jax.ShapeDtypeStruct((2, states), F32),
        ),
        in_specs=[
            any_spec,
            any_spec,
            vmem_spec,
            vmem_spec,
            vmem_spec,
            any_spec,
            any_spec,
            vmem_spec,
            pl.BlockSpec(memory_space=pltpu.SMEM),
        ],
        out_specs=(any_spec, any_spec, vmem_spec),
        scratch_shapes=[
            pltpu.VMEM((blocks, steps, width), BF16),
            pltpu.VMEM((blocks, steps, width), BF16),
            pltpu.VMEM((features, 2 * states), BF16),
            pltpu.VMEM((features, 2 * states), BF16),
            pltpu.VMEM((features, 2 * steps), BF16),
            *([per_step] * 13),
            pltpu.VMEM((steps, 2 * states), BF16),
            pltpu.VMEM((steps, states), BF16),
            pltpu.VMEM((2 * steps, states), BF16),
            pltpu.VMEM((2, 4, states), F32),
            pltpu.VMEM((chips, 4, states), F32),
            pltpu.VMEM((blocks - 1, steps, width), BF16),
            pltpu.VMEM((blocks - 1, steps, width), BF16),
            pltpu.VMEM((steps, width), F32),
            pltpu.VMEM((steps, width), BF16),
            pltpu.VMEM((batches - 1, rows, states), BF16),
            pltpu.VMEM((batches - 1, rows, states), BF16),
            pltpu.VMEM((rows, states), F32),
            pltpu.VMEM((chips, piece, states), BF16),
            pltpu.VMEM((chips, piece, states), BF16),
            pltpu.VMEM((2, chips, piece, states), BF16),
            pltpu.VMEM((chips, 2, states), F32),
            pltpu.VMEM((batches, 2, states), F32),
            pltpu.VMEM((2, 2, states), F32),
            dma((8,)),
            dma((2, 6)),
            dma((2, 6)),
            dma((PAIR_INPUTS + blocks,)),
            dma((PAIR_INPUTS + blocks,)),
            dma((4,)),
            dma((4,)),
            dma((batches - 1,)),
            dma((batches - 1,)),
            dma((batches - 1,)),
            dma((batches - 1,)),
            dma((blocks - 1,)),
            dma((blocks - 1,)),
        ],
        compiler_params=pltpu.CompilerParams(
            collective_id=0, has_side_effects=True, vmem_limit_bytes=40 * 1024 * 1024
        ),
    )(cotangent, inputs, step_size, resets, log_decay, in_proj, out_proj, saved_states, saved_index)
    return (grad_inputs, grad_proj.reshape(2, rows, states).astype(F32), grad_decay)


def solution(mesh):
    in_specs = (
        P("batch", "seq", "state"),
        P("batch", "seq", "state"),
        P("batch", "seq"),
        P("batch", "seq"),
        P(None, "state"),
        P(None, None, "state"),
        P(None, None, "state"),
        P("batch", "seq", None, "state"),
        P("batch", "seq"),
    )
    out_specs = (P("batch", "seq", "state"), P(None, "batch", "state"), P(None, "state"))
    sizes = (mesh.shape["seq"], mesh.shape["batch"], mesh.shape["state"])
    return jax.shard_map(
        functools.partial(local, sizes), mesh=mesh, in_specs=in_specs, out_specs=out_specs, check_vma=False
    )
```

```python
import functools
import math

import jax
import jax.numpy as jnp
from jax import lax
from jax.experimental import pallas as pl
from jax.experimental.pallas import tpu as pltpu
from jax.sharding import PartitionSpec as P

MESH = pl.DeviceIdType.MESH
F32 = jnp.float32
BF16 = jnp.bfloat16
GROUPS = 8
SUMMARY, DECAY, REDUCE, SPREAD = range(4)
PAIR_ADJOINT, PAIR_PROJ, PAIR_DECAY, PAIR_INPUTS = range(4)


def complex_times(left_re, left_im, right_re, right_im):
    return (left_re * right_re - left_im * right_im, left_re * right_im + left_im * right_re)


def conj_times(left_re, left_im, right_re, right_im):
    return (left_re * right_re + left_im * right_im, left_re * right_im - left_im * right_re)


def dot(left, right, left_dim, right_dim):
    return lax.dot_general(
        left, right, (((left_dim,), (right_dim,)), ((), ())), preferred_element_type=F32
    )


def small_exp(x):
    total = jnp.full_like(x, 1.0 / 5040.0)
    for factor in (1.0 / 720.0, 1.0 / 120.0, 1.0 / 24.0, 1.0 / 6.0, 0.5):
        total = total * x + factor
    near = 1.0 + (x + x * x * total)
    return jnp.where(x > -0.4, near, jnp.exp(x))


def cos_sin(angle):
    turns = jnp.floor(angle * (2.0 / math.pi) + 0.5)
    rest = angle - turns * 1.5703125
    rest = rest - turns * 4.837512969970703125e-4
    rest = rest - turns * 7.54978995489188216e-8
    square = rest * rest
    sine = ((-1.9515295891e-4 * square + 8.3321608736e-3) * square - 1.6666654611e-1) * square
    sine = sine * rest + rest
    cosine = (2.443315711809948e-5 * square - 1.388731625493765e-3) * square + 4.166664568298827e-2
    cosine = cosine * square * square - 0.5 * square + 1.0
    half = jnp.floor(turns * 0.5)
    odd = turns - 2.0 * half
    negative = half - 2.0 * jnp.floor(half * 0.5)
    sign = 1.0 - 2.0 * negative
    swap = odd > 0.5
    return (
        sign * jnp.where(swap, -sine, cosine),
        sign * jnp.where(swap, cosine, sine),
    )


def column(row):
    steps = row.shape[1]
    return jnp.concatenate(
        [
            jnp.broadcast_to(row[:, at : at + 128], (128, 128)).T
            for at in range(0, steps, 128)
        ],
        axis=0,
    )


def kernel(
    sizes,
    cot_ref,
    inp_ref,
    step_hbm,
    resets_hbm,
    rate_hbm,
    w_in_ref,
    w_out_ref,
    saved_hbm,
    index_hbm,
    gi_ref,
    gp_ref,
    gd_ref,
    cot_all,
    inp_all,
    w_in,
    w_out,
    inp_t,
    dec_re,
    dec_im,
    step_col,
    inj_re,
    inj_im,
    drv_re,
    drv_im,
    adj_re,
    adj_im,
    left_re,
    left_im,
    pri_re,
    pri_im,
    adj_bf,
    adj_send,
    adj_cat,
    z_sum,
    gi_send,
    gi_recv,
    gi_bf,
    y_send,
    y_recv,
    z_own,
    z_send,
    z_recv,
    gp_bf,
    z_dec,
    y_dec,
    pair_dec,
    step_ref,
    resets_ref,
    rate_ref,
    saved_ref,
    index_ref,
    gd_own,
    known_sem,
    local_sem,
    ring_send,
    ring_recv,
    pair_send,
    pair_recv,
    zs_send,
    zs_recv,
    ys_send,
    ys_recv,
    yd_send,
    yd_recv,
    gi_ssem,
    gi_rsem,
):
    seqs, batches, blocks = sizes
    chips = seqs // 2
    steps, width = cot_all.shape[1], cot_all.shape[2]
    half = steps // 2
    length = steps // GROUPS
    states = dec_re.shape[1]
    rows = y_recv.shape[1]
    piece = z_recv.shape[1]
    s, b, x = lax.axis_index("seq"), lax.axis_index("batch"), lax.axis_index("state")
    z, c = s // 2, s % 2
    partner = {"seq": 2 * z + (1 - c)}
    right, left = (x + 1) % blocks, (x + blocks - 1) % blocks
    across = (x + 2) % blocks

    def chip(offset, core=c):
        return {"seq": 2 * ((z + offset) % chips) + core}

    def row(offset):
        return {"batch": (b + offset) % batches}

    def block(offset):
        return {"state": (x + offset) % blocks}

    def remote(src, dst, send, recv, device):
        return pltpu.make_async_remote_copy(
            src_ref=src, dst_ref=dst, send_sem=send, recv_sem=recv, device_id=device, device_id_type=MESH
        )

    barrier = pltpu.get_barrier_semaphore()
    peers = [partner]
    peers += [block(i) for i in range(1, blocks)]
    peers += [row(i) for i in range(1, batches)]
    peers += [chip(1), chip(chips - 1)]

    def greet(semaphore, devices):
        for device in devices:
            pl.semaphore_signal(semaphore, inc=1, device_id=device, device_id_type=MESH)

    greet(barrier, peers)

    rounds = [1 << i for i in range(chips.bit_length() - 2)]

    def round_start(at):
        if at < len(rounds):
            greet(known_sem.at[at], [chip(rounds[at]), chip(chips - rounds[at])])

    def round_end(at):
        if at < len(rounds):
            pl.semaphore_wait(known_sem.at[at], 2)

    def local(src, dst, at):
        copy = pltpu.make_async_copy(src, dst, local_sem.at[at])
        copy.start()
        return copy

    cot_own = local(cot_ref.at[0], cot_all.at[x], 0)
    out_copies = [local(w_out_ref.at[k], w_out.at[:, pl.ds(k * states, states)], 1 + k) for k in range(2)]
    inp_own = local(inp_ref.at[0], inp_all.at[x], 3)
    small = ((step_hbm, step_ref), (resets_hbm, resets_ref), (rate_hbm, rate_ref))
    small_copies = [local(*pair, 8 + k) for k, pair in enumerate(small)]
    saved_copies = [local(saved_hbm, saved_ref, 11), local(index_hbm, index_ref, 12)]
    in_copies = [local(w_in_ref.at[k], w_in.at[:, pl.ds(k * states, states)], 4 + k) for k in range(2)]

    pl.semaphore_wait(barrier, len(peers))
    round_start(0)

    low, high = pl.ds(0, half), pl.ds(half, half)

    def ring(ref, whole, at):
        def send(part, device, sem):
            copy = remote(
                ref.at[0, part], whole.at[x, part], ring_send.at[at, sem], ring_recv.at[at, sem], device
            )
            copy.start()
            return copy

        return [
            send(low, block(1), 0),
            send(high, block(blocks - 1), 1),
            send(high, block(1), 2),
            send(low, block(blocks - 1), 3),
        ]

    def forward(whole, at, way):
        owner, part, device = ((left, low, block(1)), (right, high, block(blocks - 1)))[way]
        copy = remote(
            whole.at[owner, part], whole.at[owner, part], ring_send.at[at, 4 + way], ring_recv.at[at, 4 + way], device
        )
        copy.start()
        return copy

    cot_ring = ring(cot_ref, cot_all, 0)

    for copy in small_copies:
        copy.wait()
    step = step_ref[...]
    keep = (1 - resets_ref[...]).astype(F32)
    wide = column(step)
    magnitude = column(keep) * small_exp(wide * rate_ref[0:1, :])
    cosine, sine = cos_sin(wide * rate_ref[1:2, :])
    dec_re[...] = magnitude * cosine
    dec_im[...] = magnitude * sine
    step_col[...] = wide

    def part_dot(whole, weights, owner):
        return dot(whole[owner], weights[pl.ds(pl.multiple_of(owner * width, width), width), :], 1, 0)

    cot_own.wait()
    for copy in out_copies:
        copy.wait()
    inject = part_dot(cot_all, w_out, x)
    round_end(0)
    round_start(1)
    cot_ring[0].wait_recv()
    cot_on = [forward(cot_all, 0, 0)]
    cot_ring[1].wait_recv()
    cot_on.append(forward(cot_all, 0, 1))
    inp_ring = ring(inp_ref, inp_all, 1)
    round_end(1)
    round_start(2)
    cot_ring[2].wait_recv()
    inject += part_dot(cot_all, w_out, left)
    cot_ring[3].wait_recv()
    inject += part_dot(cot_all, w_out, right)
    round_end(2)
    greet(known_sem.at[3], [partner])
    for copy in cot_on:
        copy.wait_recv()
    inject += part_dot(cot_all, w_out, across)
    inj_re[...] = inject[:, :states]
    inj_im[...] = -inject[:, states:]

    def at_step(j):
        return pl.ds(j, GROUPS, stride=length)

    zero8 = jnp.zeros((GROUPS, states), F32)
    one8 = jnp.ones((GROUPS, states), F32)

    def leave(i, carry):
        prod_re, prod_im, sum_re, sum_im = carry
        at = at_step(length - 1 - i)
        d_re, d_im = dec_re[at, :], dec_im[at, :]
        prod_re, prod_im = conj_times(d_re, d_im, prod_re, prod_im)
        sum_re, sum_im = conj_times(d_re, d_im, inj_re[at, :] + sum_re, inj_im[at, :] + sum_im)
        return prod_re, prod_im, sum_re, sum_im

    grp = lax.fori_loop(0, length, leave, (one8, zero8, zero8, zero8), unroll=True)

    def pass_on(prod_re, prod_im, sum_re, sum_im, at_re, at_im):
        move_re, move_im = complex_times(prod_re, prod_im, at_re, at_im)
        return move_re + sum_re, move_im + sum_im

    def compose(first, then):
        prod_re, prod_im = complex_times(then[0], then[1], first[0], first[1])
        sum_re, sum_im = pass_on(*then, first[2], first[3])
        return prod_re, prod_im, sum_re, sum_im

    grp_rows = [tuple(part[g : g + 1, :] for part in grp) for g in range(GROUPS)]
    own = grp_rows[GROUPS - 1]
    for g in range(GROUPS - 2, -1, -1):
        own = compose(own, grp_rows[g])
    z_sum[s] = jnp.concatenate(own, axis=0)
    pl.semaphore_wait(known_sem.at[3], 1)

    def four(ref, at):
        return tuple(ref[at, k : k + 1, :] for k in range(4))

    def far_first(k):
        return chips // 2 + (k // 2) * (1 - 2 * (k % 2))

    def sum_start(k, carry):
        for core in range(2):
            remote(
                z_sum.at[s], z_sum.at[s], zs_send.at[SUMMARY], zs_recv.at[SUMMARY], chip(far_first(k), core)
            ).start()
        return carry

    lax.fori_loop(1, chips, sum_start, 0)
    remote(z_sum.at[s], z_sum.at[s], zs_send.at[SUMMARY], zs_recv.at[SUMMARY], partner).start()
    sum_part = z_sum.at[pl.ds(0, seqs - 1)]
    sum_all = remote(sum_part, sum_part, zs_send.at[SUMMARY], zs_recv.at[SUMMARY], partner)

    def z_start(src, dst, kind):
        def go(k, carry):
            i = far_first(k)
            remote(src(i), dst, zs_send.at[kind], zs_recv.at[kind], chip(i)).start()
            return carry

        lax.fori_loop(1, chips, go, 0)

    def z_all(buffer, kind):
        part = buffer.at[pl.ds(0, chips - 1)]
        return remote(part, part, zs_send.at[kind], zs_recv.at[kind], chip(1))

    inp_ring[0].wait_recv()
    inp_on = [forward(inp_all, 1, 0)]
    inp_ring[1].wait_recv()
    inp_on.append(forward(inp_all, 1, 1))
    inp_own.wait()
    for copy in in_copies:
        copy.wait()
    drive = part_dot(inp_all, w_in, x)

    columns = pl.ds(pl.multiple_of(c * steps, steps), steps)

    def turn(owner, at):
        there = inp_t.at[pl.ds(pl.multiple_of(owner * width, width), width), columns]
        there[...] = inp_all[owner].T
        copy = remote(there, there, pair_send.at[PAIR_INPUTS + at], pair_recv.at[PAIR_INPUTS + at], partner)
        copy.start()
        return copy

    turned = [turn(x, 0)]
    inp_ring[2].wait_recv()
    turned.append(turn(left, 1))
    drive += part_dot(inp_all, w_in, left)
    inp_ring[3].wait_recv()
    turned.append(turn(right, 2))
    drive += part_dot(inp_all, w_in, right)
    for copy in inp_on:
        copy.wait_recv()
    turned.append(turn(across, 3))

    sum_all.wait_recv()
    in_re, in_im = jnp.zeros((1, states), F32), jnp.zeros((1, states), F32)
    for j in range(seqs - 1, 0, -1):
        next_re, next_im = pass_on(*four(z_sum, j), in_re, in_im)
        in_re, in_im = jnp.where(j > s, next_re, in_re), jnp.where(j > s, next_im, in_im)
    enter = [None] * GROUPS
    for g in range(GROUPS - 1, -1, -1):
        enter[g] = (in_re, in_im)
        in_re, in_im = pass_on(*grp_rows[g], in_re, in_im)

    def back(i, carry):
        at = at_step(length - 1 - i)
        a_re, a_im = inj_re[at, :] + carry[0], inj_im[at, :] + carry[1]
        adj_re[at, :] = a_re
        adj_im[at, :] = a_im
        l_re, l_im = conj_times(dec_re[at, :], dec_im[at, :], a_re, a_im)
        left_re[at, :] = l_re
        left_im[at, :] = l_im
        return l_re, l_im

    lax.fori_loop(
        0,
        length,
        back,
        tuple(jnp.concatenate([pair[k] for pair in enter], axis=0) for k in range(2)),
        unroll=True,
    )
    bf_re, bf_im = adj_re[...].astype(BF16), adj_im[...].astype(BF16)
    adj_bf[:, :states] = bf_re
    adj_bf[:, states:] = bf_im
    first = (jnp.zeros((steps, states), jnp.int32) + c) == 0
    own_rows = pl.ds(pl.multiple_of(c * steps, steps), steps)
    adj_send[...] = jnp.where(first, adj_im[...], adj_re[...]).astype(BF16)
    adj_cat[own_rows, :] = jnp.where(first, adj_re[...], adj_im[...]).astype(BF16)
    adj_pair = remote(
        adj_send, adj_cat.at[own_rows], pair_send.at[PAIR_ADJOINT], pair_recv.at[PAIR_ADJOINT], partner
    )
    adj_pair.start()

    adj_pair.wait_recv()
    for copy in turned:
        copy.wait_recv()

    def gp_part(owner):
        return dot(inp_t[pl.ds(pl.multiple_of(owner * rows, rows), rows), :], adj_cat[...], 1, 0)

    y_copies = []
    for i in range(1, batches):
        y_send[i - 1] = gp_part((b + i) % batches).astype(BF16)
        copy = remote(y_send.at[i - 1], y_recv.at[i - 1], ys_send.at[i - 1], ys_recv.at[i - 1], row(i))
        copy.start()
        y_copies.append(copy)
    gp_own = gp_part(b)
    z_own[...] = gp_own

    def gi_part(owner):
        return dot(adj_bf[...], w_in[pl.ds(pl.multiple_of(owner * width, width), width), :], 1, 1)

    gi_copies = []
    for i in range(1, blocks):
        gi_send[i - 1] = gi_part((x + i) % blocks).astype(BF16)
        copy = remote(gi_send.at[i - 1], gi_recv.at[i - 1], gi_ssem.at[i - 1], gi_rsem.at[i - 1], block(i))
        copy.start()
        gi_copies.append(copy)

    drive += part_dot(inp_all, w_in, across)
    drv_re[...] = drive[:, :states]
    drv_im[...] = drive[:, states:]

    def run(i, carry):
        prod_re, prod_im, sum_re, sum_im = carry
        at = at_step(i)
        d_re, d_im = dec_re[at, :], dec_im[at, :]
        prod_re, prod_im = complex_times(d_re, d_im, prod_re, prod_im)
        sum_re, sum_im = pass_on(d_re, d_im, drv_re[at, :], drv_im[at, :], sum_re, sum_im)
        return prod_re, prod_im, sum_re, sum_im

    fwd = lax.fori_loop(0, length, run, (one8, zero8, zero8, zero8), unroll=True)
    fwd_rows = [tuple(part[g : g + 1, :] for part in fwd) for g in range(GROUPS)]
    for copy in saved_copies:
        copy.wait()
    spans = saved_ref.shape[1]
    begin = [None] * GROUPS
    for span in range(spans):
        slot = jnp.zeros((1, states), jnp.int32) + index_ref[0, span]
        at_re, at_im = jnp.zeros((1, states), F32), jnp.zeros((1, states), F32)
        for k in range(spans):
            at_re = jnp.where(slot == k, saved_ref[0, k, 0:1, :], at_re)
            at_im = jnp.where(slot == k, saved_ref[0, k, 1:2, :], at_im)
        for g in range(span * GROUPS // spans, (span + 1) * GROUPS // spans):
            begin[g] = (at_re, at_im)
            at_re, at_im = pass_on(*fwd_rows[g], at_re, at_im)

    def rerun(i, carry):
        at = at_step(i)
        pri_re[at, :] = carry[0]
        pri_im[at, :] = carry[1]
        return pass_on(dec_re[at, :], dec_im[at, :], drv_re[at, :], drv_im[at, :], *carry)

    lax.fori_loop(
        0,
        length,
        rerun,
        tuple(jnp.concatenate([pair[k] for pair in begin], axis=0) for k in range(2)),
        unroll=True,
    )
    wide_re, wide_im = conj_times(pri_re[...], pri_im[...], left_re[...], left_im[...])
    weight = step_col[...]
    z_dec[z] = jnp.concatenate(
        [jnp.sum(weight * part, axis=0, keepdims=True) for part in (wide_re, wide_im)], axis=0
    )
    z_start(lambda i: z_dec.at[z], z_dec.at[z], DECAY)

    for copy in y_copies:
        copy.wait_recv()
    total = z_own[...]
    for i in range(batches - 1):
        total += y_recv[i].astype(F32)
    z_own[...] = total
    z_send[...] = total.reshape(chips, piece, states).astype(BF16)
    z_recv[z] = jnp.zeros((piece, states), BF16)
    z_start(lambda i: z_send.at[(z + i) % chips], z_recv.at[z], REDUCE)

    z_all(z_dec, DECAY).wait_recv()
    part = z_dec[0]
    for j in range(1, chips):
        part += z_dec[j]
    y_dec[b] = part
    dec_copies = []
    for i in range(1, batches):
        copy = remote(y_dec.at[b], y_dec.at[b], yd_send.at[i - 1], yd_recv.at[i - 1], row(i))
        copy.start()
        dec_copies.append(copy)

    z_all(z_recv, REDUCE).wait_recv()
    total = z_own[pl.ds(pl.multiple_of(z * piece, piece), piece), :]
    for j in range(chips):
        total += z_recv[j].astype(F32)
    scale = 1.0 / math.sqrt(batches * seqs * steps)
    gp_bf[c, z] = (total * scale).astype(BF16)
    z_start(lambda i: gp_bf.at[c, z], gp_bf.at[c, z], SPREAD)

    own_gi = gi_part(x)
    for i in range(blocks - 1):
        gi_copies[i].wait_recv()
        own_gi += gi_recv[i].astype(F32)
    gi_bf[...] = own_gi.astype(BF16)
    gi_out = local(gi_bf, gi_ref.at[0], 6)

    for copy in dec_copies:
        copy.wait_recv()
    part = y_dec[0]
    for j in range(1, batches):
        part += y_dec[j]
    pair_dec[c] = part
    dec_pair = remote(pair_dec.at[c], pair_dec.at[c], pair_send.at[PAIR_DECAY], pair_recv.at[PAIR_DECAY], partner)
    dec_pair.start()
    dec_pair.wait_recv()
    gd_own[...] = (pair_dec[0] + pair_dec[1]) / (batches * seqs * steps)
    gd_out = local(gd_own, gd_ref, 13)

    z_all(gp_bf.at[c], SPREAD).wait_recv()
    gp_pair = remote(gp_bf.at[c], gp_bf.at[c], pair_send.at[PAIR_PROJ], pair_recv.at[PAIR_PROJ], partner)
    gp_pair.start()
    gp_pair.wait_recv()
    gp_out = local(gp_bf, gp_ref, 7)

    for copy in cot_ring + cot_on + inp_ring + inp_on + turned + gi_copies + y_copies + dec_copies:
        copy.wait_send()
    for copy in (sum_all, adj_pair, dec_pair, gp_pair):
        copy.wait_send()
    for buffer, kind in ((z_dec, DECAY), (z_send, REDUCE), (gp_bf.at[c], SPREAD)):
        z_all(buffer, kind).wait_send()
    for copy in (gi_out, gp_out, gd_out):
        copy.wait()


def local(sizes, inputs, cotangent, step_size, resets, log_decay, in_proj, out_proj, saved_states, saved_index):
    seqs, batches, blocks = sizes
    chips = seqs // 2
    _, steps, width = inputs.shape
    _, features, states = in_proj.shape
    rows = features // batches
    piece = rows // chips
    hbm_spec = pl.BlockSpec(memory_space=pltpu.HBM)
    per_step = pltpu.VMEM((steps, states), F32)
    dma = pltpu.SemaphoreType.DMA
    grad_inputs, grad_proj, grad_decay = pl.pallas_call(
        functools.partial(kernel, sizes),
        out_shape=(
            jax.ShapeDtypeStruct((1, steps, width), BF16),
            jax.ShapeDtypeStruct((2, chips, piece, states), BF16),
            jax.ShapeDtypeStruct((2, states), F32),
        ),
        in_specs=[hbm_spec] * 9,
        out_specs=(hbm_spec, hbm_spec, hbm_spec),
        scratch_shapes=[
            pltpu.VMEM((blocks, steps, width), BF16),
            pltpu.VMEM((blocks, steps, width), BF16),
            pltpu.VMEM((features, 2 * states), BF16),
            pltpu.VMEM((features, 2 * states), BF16),
            pltpu.VMEM((features, 2 * steps), BF16),
            *([per_step] * 13),
            pltpu.VMEM((steps, 2 * states), BF16),
            pltpu.VMEM((steps, states), BF16),
            pltpu.VMEM((2 * steps, states), BF16),
            pltpu.VMEM((seqs, 4, states), F32),
            pltpu.VMEM((blocks - 1, steps, width), BF16),
            pltpu.VMEM((blocks - 1, steps, width), BF16),
            pltpu.VMEM((steps, width), BF16),
            pltpu.VMEM((batches - 1, rows, states), BF16),
            pltpu.VMEM((batches - 1, rows, states), BF16),
            pltpu.VMEM((rows, states), F32),
            pltpu.VMEM((chips, piece, states), BF16),
            pltpu.VMEM((chips, piece, states), BF16),
            pltpu.VMEM((2, chips, piece, states), BF16),
            pltpu.VMEM((chips, 2, states), F32),
            pltpu.VMEM((batches, 2, states), F32),
            pltpu.VMEM((2, 2, states), F32),
            pltpu.VMEM(step_size.shape, F32),
            pltpu.VMEM(resets.shape, jnp.int32),
            pltpu.VMEM(log_decay.shape, F32),
            pltpu.VMEM(saved_states.shape, F32),
            pltpu.SMEM(saved_index.shape, jnp.int32),
            pltpu.VMEM((2, states), F32),
            pltpu.SemaphoreType.REGULAR((4,)),
            dma((14,)),
            dma((2, 6)),
            dma((2, 6)),
            dma((PAIR_INPUTS + blocks,)),
            dma((PAIR_INPUTS + blocks,)),
            dma((4,)),
            dma((4,)),
            dma((batches - 1,)),
            dma((batches - 1,)),
            dma((batches - 1,)),
            dma((batches - 1,)),
            dma((blocks - 1,)),
            dma((blocks - 1,)),
        ],
        compiler_params=pltpu.CompilerParams(
            collective_id=0, has_side_effects=True, vmem_limit_bytes=60 * 1024 * 1024
        ),
    )(cotangent, inputs, step_size, resets, log_decay, in_proj, out_proj, saved_states, saved_index)
    return (grad_inputs, grad_proj.reshape(2, rows, states).astype(F32), grad_decay)


def solution(mesh):
    in_specs = (
        P("batch", "seq", "state"),
        P("batch", "seq", "state"),
        P("batch", "seq"),
        P("batch", "seq"),
        P(None, "state"),
        P(None, None, "state"),
        P(None, None, "state"),
        P("batch", "seq", None, "state"),
        P("batch", "seq"),
    )
    out_specs = (P("batch", "seq", "state"), P(None, "batch", "state"), P(None, "state"))
    sizes = (mesh.shape["seq"], mesh.shape["batch"], mesh.shape["state"])
    return jax.shard_map(
        functools.partial(local, sizes), mesh=mesh, in_specs=in_specs, out_specs=out_specs, check_vma=False
    )
```

```python
import functools
import math

import jax
import jax.numpy as jnp
from jax import lax
from jax.experimental import pallas as pl
from jax.experimental.pallas import tpu as pltpu
from jax.sharding import PartitionSpec as P

MESH = pl.DeviceIdType.MESH
F32 = jnp.float32
BF16 = jnp.bfloat16
GROUPS = 8
SUMMARY, DECAY, REDUCE, NEAR, FAR, OPPOSITE = range(6)
PAIR_ADJOINT, PAIR_DECAY, PAIR_NEAR, PAIR_FAR, PAIR_INPUTS = range(5)


def complex_times(left_re, left_im, right_re, right_im):
    return (left_re * right_re - left_im * right_im, left_re * right_im + left_im * right_re)


def conj_times(left_re, left_im, right_re, right_im):
    return (left_re * right_re + left_im * right_im, left_re * right_im - left_im * right_re)


def dot(left, right, left_dim, right_dim):
    return lax.dot_general(
        left, right, (((left_dim,), (right_dim,)), ((), ())), preferred_element_type=F32
    )


def small_exp(x):
    total = jnp.full_like(x, 1.0 / 5040.0)
    for factor in (1.0 / 720.0, 1.0 / 120.0, 1.0 / 24.0, 1.0 / 6.0, 0.5):
        total = total * x + factor
    near = 1.0 + (x + x * x * total)
    return jnp.where(x > -0.4, near, jnp.exp(x))


def cos_sin(angle):
    turns = jnp.floor(angle * (2.0 / math.pi) + 0.5)
    rest = angle - turns * 1.5703125
    rest = rest - turns * 4.837512969970703125e-4
    rest = rest - turns * 7.54978995489188216e-8
    square = rest * rest
    sine = ((-1.9515295891e-4 * square + 8.3321608736e-3) * square - 1.6666654611e-1) * square
    sine = sine * rest + rest
    cosine = (2.443315711809948e-5 * square - 1.388731625493765e-3) * square + 4.166664568298827e-2
    cosine = cosine * square * square - 0.5 * square + 1.0
    half = jnp.floor(turns * 0.5)
    odd = turns - 2.0 * half
    negative = half - 2.0 * jnp.floor(half * 0.5)
    sign = 1.0 - 2.0 * negative
    swap = odd > 0.5
    return (
        sign * jnp.where(swap, -sine, cosine),
        sign * jnp.where(swap, cosine, sine),
    )


def column(row):
    steps = row.shape[1]
    return jnp.concatenate(
        [
            jnp.broadcast_to(row[:, at : at + 128], (128, 128)).T
            for at in range(0, steps, 128)
        ],
        axis=0,
    )


def kernel(
    sizes,
    cot_ref,
    inp_ref,
    step_hbm,
    resets_hbm,
    rate_hbm,
    w_in_ref,
    w_out_ref,
    saved_hbm,
    index_hbm,
    gi_ref,
    gp_ref,
    gd_ref,
    cot_all,
    inp_all,
    w_in,
    w_out,
    inp_t,
    dec_re,
    dec_im,
    step_col,
    inj_re,
    inj_im,
    drv_re,
    drv_im,
    adj_re,
    adj_im,
    left_re,
    left_im,
    pri_re,
    pri_im,
    adj_bf,
    adj_send,
    adj_cat,
    z_sum,
    gi_send,
    gi_recv,
    gi_bf,
    y_send,
    y_recv,
    z_own,
    z_send,
    z_recv,
    gp_bf,
    gp_f32,
    z_dec,
    y_dec,
    pair_dec,
    step_ref,
    resets_ref,
    rate_ref,
    saved_ref,
    index_ref,
    gd_own,
    known_sem,
    local_sem,
    ring_send,
    ring_recv,
    pair_send,
    pair_recv,
    zs_send,
    zs_recv,
    ys_send,
    ys_recv,
    yd_send,
    yd_recv,
    gi_ssem,
    gi_rsem,
):
    seqs, batches, blocks = sizes
    chips = seqs // 2
    steps, width = cot_all.shape[1], cot_all.shape[2]
    half = steps // 2
    length = steps // GROUPS
    states = dec_re.shape[1]
    rows = y_recv.shape[1]
    piece = z_recv.shape[1]
    s, b, x = lax.axis_index("seq"), lax.axis_index("batch"), lax.axis_index("state")
    z, c = s // 2, s % 2
    partner = {"seq": 2 * z + (1 - c)}
    right, left = (x + 1) % blocks, (x + blocks - 1) % blocks
    across = (x + 2) % blocks

    def chip(offset, core=c):
        return {"seq": 2 * ((z + offset) % chips) + core}

    def row(offset):
        return {"batch": (b + offset) % batches}

    def block(offset):
        return {"state": (x + offset) % blocks}

    def remote(src, dst, send, recv, device):
        return pltpu.make_async_remote_copy(
            src_ref=src, dst_ref=dst, send_sem=send, recv_sem=recv, device_id=device, device_id_type=MESH
        )

    barrier = pltpu.get_barrier_semaphore()
    peers = [partner]
    peers += [block(i) for i in range(1, blocks)]
    peers += [row(i) for i in range(1, batches)]
    peers += [chip(1), chip(chips - 1)]

    def greet(semaphore, devices):
        for device in devices:
            pl.semaphore_signal(semaphore, inc=1, device_id=device, device_id_type=MESH)

    greet(barrier, peers)

    rounds = [1 << i for i in range(chips.bit_length() - 2)]

    def round_start(at):
        if at < len(rounds):
            greet(known_sem.at[at], [chip(rounds[at]), chip(chips - rounds[at])])

    def round_end(at):
        if at < len(rounds):
            pl.semaphore_wait(known_sem.at[at], 2)

    def local(src, dst, at):
        copy = pltpu.make_async_copy(src, dst, local_sem.at[at])
        copy.start()
        return copy

    cot_own = local(cot_ref.at[0], cot_all.at[x], 0)
    out_copies = [local(w_out_ref.at[k], w_out.at[:, pl.ds(k * states, states)], 1 + k) for k in range(2)]
    inp_own = local(inp_ref.at[0], inp_all.at[x], 3)
    small = ((step_hbm, step_ref), (resets_hbm, resets_ref), (rate_hbm, rate_ref))
    small_copies = [local(*pair, 8 + k) for k, pair in enumerate(small)]
    saved_copies = [local(saved_hbm, saved_ref, 11), local(index_hbm, index_ref, 12)]
    in_copies = [local(w_in_ref.at[k], w_in.at[:, pl.ds(k * states, states)], 4 + k) for k in range(2)]

    pl.semaphore_wait(barrier, len(peers))
    round_start(0)

    low, high = pl.ds(0, half), pl.ds(half, half)

    def ring(ref, whole, at):
        def send(part, device, sem):
            copy = remote(
                ref.at[0, part], whole.at[x, part], ring_send.at[at, sem], ring_recv.at[at, sem], device
            )
            copy.start()
            return copy

        return [
            send(low, block(1), 0),
            send(high, block(blocks - 1), 1),
            send(high, block(1), 2),
            send(low, block(blocks - 1), 3),
        ]

    def forward(whole, at, way):
        owner, part, device = ((left, low, block(1)), (right, high, block(blocks - 1)))[way]
        copy = remote(
            whole.at[owner, part], whole.at[owner, part], ring_send.at[at, 4 + way], ring_recv.at[at, 4 + way], device
        )
        copy.start()
        return copy

    cot_ring = ring(cot_ref, cot_all, 0)

    for copy in small_copies:
        copy.wait()
    step = step_ref[...]
    keep = (1 - resets_ref[...]).astype(F32)
    wide = column(step)
    magnitude = column(keep) * small_exp(wide * rate_ref[0:1, :])
    cosine, sine = cos_sin(wide * rate_ref[1:2, :])
    dec_re[...] = magnitude * cosine
    dec_im[...] = magnitude * sine
    step_col[...] = wide

    def part_dot(whole, weights, owner):
        return dot(whole[owner], weights[pl.ds(pl.multiple_of(owner * width, width), width), :], 1, 0)

    cot_own.wait()
    for copy in out_copies:
        copy.wait()
    inject = part_dot(cot_all, w_out, x)
    round_end(0)
    round_start(1)
    cot_ring[0].wait_recv()
    cot_on = [forward(cot_all, 0, 0)]
    cot_ring[1].wait_recv()
    cot_on.append(forward(cot_all, 0, 1))
    inp_ring = ring(inp_ref, inp_all, 1)
    round_end(1)
    round_start(2)
    cot_ring[2].wait_recv()
    inject += part_dot(cot_all, w_out, left)
    cot_ring[3].wait_recv()
    inject += part_dot(cot_all, w_out, right)
    round_end(2)
    greet(known_sem.at[3], [partner])
    for copy in cot_on:
        copy.wait_recv()
    inject += part_dot(cot_all, w_out, across)
    inj_re[...] = inject[:, :states]
    inj_im[...] = -inject[:, states:]

    def at_step(j):
        return pl.ds(j, GROUPS, stride=length)

    zero8 = jnp.zeros((GROUPS, states), F32)
    one8 = jnp.ones((GROUPS, states), F32)

    def leave(i, carry):
        prod_re, prod_im, sum_re, sum_im = carry
        at = at_step(length - 1 - i)
        d_re, d_im = dec_re[at, :], dec_im[at, :]
        prod_re, prod_im = conj_times(d_re, d_im, prod_re, prod_im)
        sum_re, sum_im = conj_times(d_re, d_im, inj_re[at, :] + sum_re, inj_im[at, :] + sum_im)
        return prod_re, prod_im, sum_re, sum_im

    grp = lax.fori_loop(0, length, leave, (one8, zero8, zero8, zero8), unroll=True)

    def pass_on(prod_re, prod_im, sum_re, sum_im, at_re, at_im):
        move_re, move_im = complex_times(prod_re, prod_im, at_re, at_im)
        return move_re + sum_re, move_im + sum_im

    def compose(first, then):
        prod_re, prod_im = complex_times(then[0], then[1], first[0], first[1])
        sum_re, sum_im = pass_on(*then, first[2], first[3])
        return prod_re, prod_im, sum_re, sum_im

    grp_rows = [tuple(part[g : g + 1, :] for part in grp) for g in range(GROUPS)]
    own = grp_rows[GROUPS - 1]
    for g in range(GROUPS - 2, -1, -1):
        own = compose(own, grp_rows[g])
    z_sum[s] = jnp.concatenate(own, axis=0)
    pl.semaphore_wait(known_sem.at[3], 1)

    def four(ref, at):
        return tuple(ref[at, k : k + 1, :] for k in range(4))

    def far_first(k):
        return chips // 2 + (k // 2) * (1 - 2 * (k % 2))

    def sum_start(k, carry):
        for core in range(2):
            remote(
                z_sum.at[s], z_sum.at[s], zs_send.at[SUMMARY], zs_recv.at[SUMMARY], chip(far_first(k), core)
            ).start()
        return carry

    lax.fori_loop(1, chips, sum_start, 0)
    remote(z_sum.at[s], z_sum.at[s], zs_send.at[SUMMARY], zs_recv.at[SUMMARY], partner).start()
    sum_part = z_sum.at[pl.ds(0, seqs - 1)]
    sum_all = remote(sum_part, sum_part, zs_send.at[SUMMARY], zs_recv.at[SUMMARY], partner)

    def z_start(src, dst, kind):
        def go(k, carry):
            i = far_first(k)
            remote(src(i), dst, zs_send.at[kind], zs_recv.at[kind], chip(i)).start()
            return carry

        lax.fori_loop(1, chips, go, 0)

    def z_all(buffer, kind):
        part = buffer.at[pl.ds(0, chips - 1)]
        return remote(part, part, zs_send.at[kind], zs_recv.at[kind], chip(1))

    inp_ring[0].wait_recv()
    inp_on = [forward(inp_all, 1, 0)]
    inp_ring[1].wait_recv()
    inp_on.append(forward(inp_all, 1, 1))
    inp_own.wait()
    for copy in in_copies:
        copy.wait()
    drive = part_dot(inp_all, w_in, x)

    columns = pl.ds(pl.multiple_of(c * steps, steps), steps)

    def turn(owner, at):
        there = inp_t.at[pl.ds(pl.multiple_of(owner * width, width), width), columns]
        there[...] = inp_all[owner].T
        copy = remote(there, there, pair_send.at[PAIR_INPUTS + at], pair_recv.at[PAIR_INPUTS + at], partner)
        copy.start()
        return copy

    turned = [turn(x, 0)]
    inp_ring[2].wait_recv()
    turned.append(turn(left, 1))
    drive += part_dot(inp_all, w_in, left)
    inp_ring[3].wait_recv()
    turned.append(turn(right, 2))
    drive += part_dot(inp_all, w_in, right)
    sum_all.wait_recv()
    in_re, in_im = jnp.zeros((1, states), F32), jnp.zeros((1, states), F32)
    for j in range(seqs - 1, 0, -1):
        next_re, next_im = pass_on(*four(z_sum, j), in_re, in_im)
        in_re, in_im = jnp.where(j > s, next_re, in_re), jnp.where(j > s, next_im, in_im)
    enter = [None] * GROUPS
    for g in range(GROUPS - 1, -1, -1):
        enter[g] = (in_re, in_im)
        in_re, in_im = pass_on(*grp_rows[g], in_re, in_im)

    def back(i, carry):
        at = at_step(length - 1 - i)
        a_re, a_im = inj_re[at, :] + carry[0], inj_im[at, :] + carry[1]
        adj_re[at, :] = a_re
        adj_im[at, :] = a_im
        l_re, l_im = conj_times(dec_re[at, :], dec_im[at, :], a_re, a_im)
        left_re[at, :] = l_re
        left_im[at, :] = l_im
        return l_re, l_im

    lax.fori_loop(
        0,
        length,
        back,
        tuple(jnp.concatenate([pair[k] for pair in enter], axis=0) for k in range(2)),
        unroll=True,
    )
    bf_re, bf_im = adj_re[...].astype(BF16), adj_im[...].astype(BF16)
    adj_bf[:, :states] = bf_re
    adj_bf[:, states:] = bf_im
    first = (jnp.zeros((steps, states), jnp.int32) + c) == 0
    own_rows = pl.ds(pl.multiple_of(c * steps, steps), steps)
    adj_send[...] = jnp.where(first, adj_im[...], adj_re[...]).astype(BF16)
    adj_cat[own_rows, :] = jnp.where(first, adj_re[...], adj_im[...]).astype(BF16)
    adj_pair = remote(
        adj_send, adj_cat.at[own_rows], pair_send.at[PAIR_ADJOINT], pair_recv.at[PAIR_ADJOINT], partner
    )
    adj_pair.start()
    for copy in inp_on:
        copy.wait_recv()
    turned.append(turn(across, 3))

    adj_pair.wait_recv()
    y_copies = [
        remote(y_send.at[i], y_recv.at[i], ys_send.at[i], ys_recv.at[i], row(i + 1)) for i in range(batches - 1)
    ]
    for at, owner in enumerate((x, left, right, across)):
        turned[at].wait_recv()
        here = pl.ds(pl.multiple_of(owner * width, width), width)
        part = dot(inp_t[here, :], adj_cat[...], 1, 0)
        offset = (owner + batches - b) % batches

        @pl.when(offset == 0)
        def _():
            z_own[...] = part

        @pl.when(offset != 0)
        def _():
            to = jnp.maximum(offset - 1, 0)
            y_send[to] = part.astype(BF16)
            remote(
                y_send.at[to], y_recv.at[to], ys_send.at[to], ys_recv.at[to], row(offset)
            ).start()

    def gi_part(owner):
        return dot(adj_bf[...], w_in[pl.ds(pl.multiple_of(owner * width, width), width), :], 1, 1)

    gi_copies = []
    for i in range(1, blocks):
        gi_send[i - 1] = gi_part((x + i) % blocks).astype(BF16)
        copy = remote(gi_send.at[i - 1], gi_recv.at[i - 1], gi_ssem.at[i - 1], gi_rsem.at[i - 1], block(i))
        copy.start()
        gi_copies.append(copy)

    drive += part_dot(inp_all, w_in, across)
    drv_re[...] = drive[:, :states]
    drv_im[...] = drive[:, states:]

    def run(i, carry):
        prod_re, prod_im, sum_re, sum_im = carry
        at = at_step(i)
        d_re, d_im = dec_re[at, :], dec_im[at, :]
        prod_re, prod_im = complex_times(d_re, d_im, prod_re, prod_im)
        sum_re, sum_im = pass_on(d_re, d_im, drv_re[at, :], drv_im[at, :], sum_re, sum_im)
        return prod_re, prod_im, sum_re, sum_im

    fwd = lax.fori_loop(0, length, run, (one8, zero8, zero8, zero8), unroll=True)
    fwd_rows = [tuple(part[g : g + 1, :] for part in fwd) for g in range(GROUPS)]
    for copy in saved_copies:
        copy.wait()
    spans = saved_ref.shape[1]
    begin = [None] * GROUPS
    for span in range(spans):
        slot = jnp.zeros((1, states), jnp.int32) + index_ref[0, span]
        at_re, at_im = jnp.zeros((1, states), F32), jnp.zeros((1, states), F32)
        for k in range(spans):
            at_re = jnp.where(slot == k, saved_ref[0, k, 0:1, :], at_re)
            at_im = jnp.where(slot == k, saved_ref[0, k, 1:2, :], at_im)
        for g in range(span * GROUPS // spans, (span + 1) * GROUPS // spans):
            begin[g] = (at_re, at_im)
            at_re, at_im = pass_on(*fwd_rows[g], at_re, at_im)

    def rerun(i, carry):
        at = at_step(i)
        pri_re[at, :] = carry[0]
        pri_im[at, :] = carry[1]
        return pass_on(dec_re[at, :], dec_im[at, :], drv_re[at, :], drv_im[at, :], *carry)

    lax.fori_loop(
        0,
        length,
        rerun,
        tuple(jnp.concatenate([pair[k] for pair in begin], axis=0) for k in range(2)),
        unroll=True,
    )
    wide_re, wide_im = conj_times(pri_re[...], pri_im[...], left_re[...], left_im[...])
    weight = step_col[...]
    z_dec[z] = jnp.concatenate(
        [jnp.sum(weight * part, axis=0, keepdims=True) for part in (wide_re, wide_im)], axis=0
    )
    z_start(lambda i: z_dec.at[z], z_dec.at[z], DECAY)

    for copy in y_copies:
        copy.wait_recv()
    total = z_own[...]
    for i in range(batches - 1):
        total += y_recv[i].astype(F32)
    z_own[...] = total
    z_send[...] = total.reshape(chips, piece, states).astype(BF16)
    z_recv[z] = jnp.zeros((piece, states), BF16)
    z_start(lambda i: z_send.at[(z + i) % chips], z_recv.at[z], REDUCE)

    z_all(z_dec, DECAY).wait_recv()
    part = z_dec[0]
    for j in range(1, chips):
        part += z_dec[j]
    y_dec[b] = part
    dec_copies = []
    for i in range(1, batches):
        copy = remote(y_dec.at[b], y_dec.at[b], yd_send.at[i - 1], yd_recv.at[i - 1], row(i))
        copy.start()
        dec_copies.append(copy)

    z_all(z_recv, REDUCE).wait_recv()
    total = z_own[pl.ds(pl.multiple_of(z * piece, piece), piece), :]
    for j in range(chips):
        total += z_recv[j].astype(F32)
    scale = 1.0 / math.sqrt(batches * seqs * steps)
    gp_bf[c, z] = (total * scale).astype(BF16)

    mine = gp_bf.at[c, z]

    def spread(offset, kind, core=c):
        remote(mine, mine, zs_send.at[kind], zs_recv.at[kind], chip(offset, core)).start()

    def hand(offset, kind):
        there = gp_bf.at[c, (z + offset) % chips]
        remote(there, there, pair_send.at[kind], pair_recv.at[kind], partner).start()

    reach = chips // 2
    near = [sign * d for d in range(min(4, reach - 1), 0, -1) for sign in (1, -1)]
    far = [sign * d for d in range(reach - 1, 4, -1) for sign in (1, -1)]

    def groups(kind, pair_kind, count, extra):
        if count == 0 and extra == 0:
            return (None, None)
        part = gp_bf.at[c, pl.ds(0, max(count, 1))]
        more = gp_bf.at[c, pl.ds(0, count + extra)]
        return (
            remote(part, part, zs_send.at[kind], zs_recv.at[kind], partner) if count else None,
            remote(more, more, pair_send.at[pair_kind], pair_recv.at[pair_kind], partner),
        )

    spread(reach, OPPOSITE, 0)
    spread(reach, OPPOSITE, 1)
    for offset in far:
        spread(offset + chips, FAR)
    for offset in near:
        spread(offset + chips, NEAR)
    hand(0, PAIR_NEAR)
    near_all, near_hand = groups(NEAR, PAIR_NEAR, len(near), 1)
    far_all, far_hand = groups(FAR, PAIR_FAR, len(far), 0)
    two = gp_bf.at[c, pl.ds(0, 2)]
    opposite_all = remote(two, two, zs_send.at[OPPOSITE], zs_recv.at[OPPOSITE], partner)

    own_gi = gi_part(x)
    for i in range(blocks - 1):
        gi_copies[i].wait_recv()
        own_gi += gi_recv[i].astype(F32)
    gi_bf[...] = own_gi.astype(BF16)
    gi_out = local(gi_bf, gi_ref.at[0], 6)

    if near:
        near_all.wait_recv()
        for offset in near:
            hand(offset + chips, PAIR_NEAR)
    for copy in dec_copies:
        copy.wait_recv()
    part = y_dec[0]
    for j in range(1, batches):
        part += y_dec[j]
    pair_dec[c] = part
    dec_pair = remote(pair_dec.at[c], pair_dec.at[c], pair_send.at[PAIR_DECAY], pair_recv.at[PAIR_DECAY], partner)
    dec_pair.start()
    dec_pair.wait_recv()
    gd_own[...] = (pair_dec[0] + pair_dec[1]) / (batches * seqs * steps)
    gd_out = local(gd_own, gd_ref, 13)

    if far:
        far_all.wait_recv()
        for offset in far:
            hand(offset + chips, PAIR_FAR)
    opposite_all.wait_recv()
    gp_f32[c] = gp_bf[c].astype(F32)
    gp_outs = [local(gp_f32.at[c], gp_ref.at[c], 7)]
    near_hand.wait_recv()
    if far:
        far_hand.wait_recv()
    gp_f32[1 - c] = gp_bf[1 - c].astype(F32)
    gp_outs.append(local(gp_f32.at[1 - c], gp_ref.at[1 - c], 14))

    for copy in cot_ring + cot_on + inp_ring + inp_on + turned + gi_copies + y_copies + dec_copies:
        copy.wait_send()
    for copy in (sum_all, adj_pair, dec_pair, near_all, near_hand, far_all, far_hand, opposite_all):
        if copy is not None:
            copy.wait_send()
    for buffer, kind in ((z_dec, DECAY), (z_send, REDUCE)):
        z_all(buffer, kind).wait_send()
    for copy in (gi_out, gd_out, *gp_outs):
        copy.wait()


def hand_out(gi_in, gp_in, gd_in, gi_out, gp_out, gd_out, sems):
    pairs = ((gp_in, gp_out), (gi_in, gi_out), (gd_in, gd_out))
    copies = [pltpu.make_async_copy(src, dst, sems.at[i]) for i, (src, dst) in enumerate(pairs)]
    for copy in copies:
        copy.start()
    for copy in copies:
        copy.wait()


def local(sizes, inputs, cotangent, step_size, resets, log_decay, in_proj, out_proj, saved_states, saved_index):
    seqs, batches, blocks = sizes
    chips = seqs // 2
    _, steps, width = inputs.shape
    _, features, states = in_proj.shape
    rows = features // batches
    piece = rows // chips
    hbm_spec = pl.BlockSpec(memory_space=pltpu.HBM)
    per_step = pltpu.VMEM((steps, states), F32)
    dma = pltpu.SemaphoreType.DMA
    grad_inputs, grad_proj, grad_decay = pl.pallas_call(
        functools.partial(kernel, sizes),
        out_shape=(
            jax.ShapeDtypeStruct((1, steps, width), BF16),
            jax.ShapeDtypeStruct((2, chips, piece, states), F32),
            jax.ShapeDtypeStruct((2, states), F32),
        ),
        in_specs=[hbm_spec] * 9,
        out_specs=(hbm_spec, hbm_spec, hbm_spec),
        scratch_shapes=[
            pltpu.VMEM((blocks, steps, width), BF16),
            pltpu.VMEM((blocks, steps, width), BF16),
            pltpu.VMEM((features, 2 * states), BF16),
            pltpu.VMEM((features, 2 * states), BF16),
            pltpu.VMEM((features, 2 * steps), BF16),
            *([per_step] * 13),
            pltpu.VMEM((steps, 2 * states), BF16),
            pltpu.VMEM((steps, states), BF16),
            pltpu.VMEM((2 * steps, states), BF16),
            pltpu.VMEM((seqs, 4, states), F32),
            pltpu.VMEM((blocks - 1, steps, width), BF16),
            pltpu.VMEM((blocks - 1, steps, width), BF16),
            pltpu.VMEM((steps, width), BF16),
            pltpu.VMEM((batches - 1, rows, states), BF16),
            pltpu.VMEM((batches - 1, rows, states), BF16),
            pltpu.VMEM((rows, states), F32),
            pltpu.VMEM((chips, piece, states), BF16),
            pltpu.VMEM((chips, piece, states), BF16),
            pltpu.VMEM((2, chips, piece, states), BF16),
            pltpu.VMEM((2, chips, piece, states), F32),
            pltpu.VMEM((chips, 2, states), F32),
            pltpu.VMEM((batches, 2, states), F32),
            pltpu.VMEM((2, 2, states), F32),
            pltpu.VMEM(step_size.shape, F32),
            pltpu.VMEM(resets.shape, jnp.int32),
            pltpu.VMEM(log_decay.shape, F32),
            pltpu.VMEM(saved_states.shape, F32),
            pltpu.SMEM(saved_index.shape, jnp.int32),
            pltpu.VMEM((2, states), F32),
            pltpu.SemaphoreType.REGULAR((4,)),
            dma((15,)),
            dma((2, 6)),
            dma((2, 6)),
            dma((PAIR_INPUTS + blocks,)),
            dma((PAIR_INPUTS + blocks,)),
            dma((6,)),
            dma((6,)),
            dma((batches - 1,)),
            dma((batches - 1,)),
            dma((batches - 1,)),
            dma((batches - 1,)),
            dma((blocks - 1,)),
            dma((blocks - 1,)),
        ],
        compiler_params=pltpu.CompilerParams(
            collective_id=0, has_side_effects=True, vmem_limit_bytes=60 * 1024 * 1024
        ),
    )(cotangent, inputs, step_size, resets, log_decay, in_proj, out_proj, saved_states, saved_index)
    results = (grad_inputs, grad_proj.reshape(2, rows, states), grad_decay)
    return pl.pallas_call(
        hand_out,
        out_shape=[jax.ShapeDtypeStruct(part.shape, part.dtype) for part in results],
        in_specs=[hbm_spec] * 3,
        out_specs=[hbm_spec] * 3,
        scratch_shapes=[dma((3,))],
        compiler_params=pltpu.CompilerParams(vmem_limit_bytes=60 * 1024 * 1024),
    )(*results)


def solution(mesh):
    in_specs = (
        P("batch", "seq", "state"),
        P("batch", "seq", "state"),
        P("batch", "seq"),
        P("batch", "seq"),
        P(None, "state"),
        P(None, None, "state"),
        P(None, None, "state"),
        P("batch", "seq", None, "state"),
        P("batch", "seq"),
    )
    out_specs = (P("batch", "seq", "state"), P(None, "batch", "state"), P(None, "state"))
    sizes = (mesh.shape["seq"], mesh.shape["batch"], mesh.shape["state"])
    return jax.shard_map(
        functools.partial(local, sizes), mesh=mesh, in_specs=in_specs, out_specs=out_specs, check_vma=False
    )
```

```python
import functools
import math

import jax
import jax.numpy as jnp
from jax import lax
from jax.experimental import pallas as pl
from jax.experimental.pallas import tpu as pltpu
from jax.sharding import PartitionSpec as P

MESH = pl.DeviceIdType.MESH
F32 = jnp.float32
BF16 = jnp.bfloat16
GROUPS = 8
SUMMARY, DECAY, REDUCE, NEAR, FAR, OPPOSITE = range(6)
PAIR_ADJOINT, PAIR_DECAY, PAIR_NEAR, PAIR_FAR, PAIR_INPUTS = range(5)


def complex_times(left_re, left_im, right_re, right_im):
    return (left_re * right_re - left_im * right_im, left_re * right_im + left_im * right_re)


def conj_times(left_re, left_im, right_re, right_im):
    return (left_re * right_re + left_im * right_im, left_re * right_im - left_im * right_re)


def dot(left, right, left_dim, right_dim):
    return lax.dot_general(
        left, right, (((left_dim,), (right_dim,)), ((), ())), preferred_element_type=F32
    )


def small_exp(x):
    total = jnp.full_like(x, 1.0 / 5040.0)
    for factor in (1.0 / 720.0, 1.0 / 120.0, 1.0 / 24.0, 1.0 / 6.0, 0.5):
        total = total * x + factor
    near = 1.0 + (x + x * x * total)
    return jnp.where(x > -0.4, near, jnp.exp(x))


def cos_sin(angle):
    turns = jnp.floor(angle * (2.0 / math.pi) + 0.5)
    rest = angle - turns * 1.5703125
    rest = rest - turns * 4.837512969970703125e-4
    rest = rest - turns * 7.54978995489188216e-8
    square = rest * rest
    sine = ((-1.9515295891e-4 * square + 8.3321608736e-3) * square - 1.6666654611e-1) * square
    sine = sine * rest + rest
    cosine = (2.443315711809948e-5 * square - 1.388731625493765e-3) * square + 4.166664568298827e-2
    cosine = cosine * square * square - 0.5 * square + 1.0
    half = jnp.floor(turns * 0.5)
    odd = turns - 2.0 * half
    negative = half - 2.0 * jnp.floor(half * 0.5)
    sign = 1.0 - 2.0 * negative
    swap = odd > 0.5
    return (
        sign * jnp.where(swap, -sine, cosine),
        sign * jnp.where(swap, cosine, sine),
    )


def column(row):
    steps = row.shape[1]
    return jnp.concatenate(
        [
            jnp.broadcast_to(row[:, at : at + 128], (128, 128)).T
            for at in range(0, steps, 128)
        ],
        axis=0,
    )


def kernel(
    sizes,
    cot_ref,
    inp_ref,
    step_hbm,
    resets_hbm,
    rate_hbm,
    w_in_ref,
    w_out_ref,
    saved_hbm,
    index_hbm,
    gi_ref,
    gp_ref,
    gd_ref,
    cot_all,
    inp_all,
    w_in,
    w_out,
    inp_t,
    dec_re,
    dec_im,
    step_col,
    inj_re,
    inj_im,
    drv_re,
    drv_im,
    adj_re,
    adj_im,
    left_re,
    left_im,
    pri_re,
    pri_im,
    adj_bf,
    adj_send,
    adj_cat,
    z_sum,
    gi_send,
    gi_recv,
    gi_bf,
    y_send,
    y_recv,
    z_own,
    z_send,
    z_recv,
    gp_bf,
    gp_f32,
    z_dec,
    y_dec,
    pair_dec,
    step_ref,
    resets_ref,
    rate_ref,
    saved_ref,
    index_ref,
    gd_own,
    known_sem,
    local_sem,
    ring_send,
    ring_recv,
    pair_send,
    pair_recv,
    zs_send,
    zs_recv,
    ys_send,
    ys_recv,
    yd_send,
    yd_recv,
    gi_ssem,
    gi_rsem,
):
    seqs, batches, blocks = sizes
    chips = seqs // 2
    steps, width = cot_all.shape[1], cot_all.shape[2]
    half = steps // 2
    length = steps // GROUPS
    states = dec_re.shape[1]
    rows = y_recv.shape[1]
    piece = z_recv.shape[1]
    s, b, x = lax.axis_index("seq"), lax.axis_index("batch"), lax.axis_index("state")
    z, c = s // 2, s % 2
    partner = {"seq": 2 * z + (1 - c)}
    right, left = (x + 1) % blocks, (x + blocks - 1) % blocks
    across = (x + 2) % blocks

    def chip(offset, core=c):
        return {"seq": 2 * ((z + offset) % chips) + core}

    def row(offset):
        return {"batch": (b + offset) % batches}

    def block(offset):
        return {"state": (x + offset) % blocks}

    def remote(src, dst, send, recv, device):
        return pltpu.make_async_remote_copy(
            src_ref=src, dst_ref=dst, send_sem=send, recv_sem=recv, device_id=device, device_id_type=MESH
        )

    barrier = pltpu.get_barrier_semaphore()
    peers = [partner]
    peers += [block(i) for i in range(1, blocks)]
    peers += [row(i) for i in range(1, batches)]
    peers += [chip(1), chip(chips - 1)]

    def greet(semaphore, devices):
        for device in devices:
            pl.semaphore_signal(semaphore, inc=1, device_id=device, device_id_type=MESH)

    greet(barrier, peers)

    rounds = [1 << i for i in range(chips.bit_length() - 2)]

    def round_start(at):
        if at < len(rounds):
            greet(known_sem.at[at], [chip(rounds[at]), chip(chips - rounds[at])])

    def round_end(at):
        if at < len(rounds):
            pl.semaphore_wait(known_sem.at[at], 2)

    def local(src, dst, at):
        copy = pltpu.make_async_copy(src, dst, local_sem.at[at])
        copy.start()
        return copy

    cot_own = local(cot_ref.at[0], cot_all.at[x], 0)
    out_copies = [local(w_out_ref.at[k], w_out.at[:, pl.ds(k * states, states)], 1 + k) for k in range(2)]
    inp_own = local(inp_ref.at[0], inp_all.at[x], 3)
    small = ((step_hbm, step_ref), (resets_hbm, resets_ref), (rate_hbm, rate_ref))
    small_copies = [local(*pair, 8 + k) for k, pair in enumerate(small)]
    saved_copies = [local(saved_hbm, saved_ref, 11), local(index_hbm, index_ref, 12)]
    in_copies = [local(w_in_ref.at[k], w_in.at[:, pl.ds(k * states, states)], 4 + k) for k in range(2)]

    pl.semaphore_wait(barrier, len(peers))
    round_start(0)

    low, high = pl.ds(0, half), pl.ds(half, half)

    def ring(ref, whole, at):
        def send(part, device, sem):
            copy = remote(
                ref.at[0, part], whole.at[x, part], ring_send.at[at, sem], ring_recv.at[at, sem], device
            )
            copy.start()
            return copy

        return [
            send(low, block(1), 0),
            send(high, block(blocks - 1), 1),
            send(high, block(1), 2),
            send(low, block(blocks - 1), 3),
        ]

    def forward(whole, at, way):
        owner, part, device = ((left, low, block(1)), (right, high, block(blocks - 1)))[way]
        copy = remote(
            whole.at[owner, part], whole.at[owner, part], ring_send.at[at, 4 + way], ring_recv.at[at, 4 + way], device
        )
        copy.start()
        return copy

    cot_ring = ring(cot_ref, cot_all, 0)

    for copy in small_copies:
        copy.wait()
    step = step_ref[...]
    keep = (1 - resets_ref[...]).astype(F32)
    wide = column(step)
    magnitude = column(keep) * small_exp(wide * rate_ref[0:1, :])
    cosine, sine = cos_sin(wide * rate_ref[1:2, :])
    dec_re[...] = magnitude * cosine
    dec_im[...] = magnitude * sine
    step_col[...] = wide

    def part_dot(whole, weights, owner):
        return dot(whole[owner], weights[pl.ds(pl.multiple_of(owner * width, width), width), :], 1, 0)

    cot_own.wait()
    for copy in out_copies:
        copy.wait()
    inject = part_dot(cot_all, w_out, x)
    round_end(0)
    round_start(1)
    cot_ring[0].wait_recv()
    cot_on = [forward(cot_all, 0, 0)]
    cot_ring[1].wait_recv()
    cot_on.append(forward(cot_all, 0, 1))
    inp_ring = ring(inp_ref, inp_all, 1)
    round_end(1)
    round_start(2)
    cot_ring[2].wait_recv()
    inject += part_dot(cot_all, w_out, left)
    cot_ring[3].wait_recv()
    inject += part_dot(cot_all, w_out, right)
    round_end(2)
    greet(known_sem.at[3], [partner])
    for copy in cot_on:
        copy.wait_recv()
    inject += part_dot(cot_all, w_out, across)
    inj_re[...] = inject[:, :states]
    inj_im[...] = -inject[:, states:]

    def at_step(j):
        return pl.ds(j, GROUPS, stride=length)

    zero8 = jnp.zeros((GROUPS, states), F32)
    one8 = jnp.ones((GROUPS, states), F32)

    def leave(i, carry):
        prod_re, prod_im, sum_re, sum_im = carry
        at = at_step(length - 1 - i)
        d_re, d_im = dec_re[at, :], dec_im[at, :]
        prod_re, prod_im = conj_times(d_re, d_im, prod_re, prod_im)
        sum_re, sum_im = conj_times(d_re, d_im, inj_re[at, :] + sum_re, inj_im[at, :] + sum_im)
        return prod_re, prod_im, sum_re, sum_im

    grp = lax.fori_loop(0, length, leave, (one8, zero8, zero8, zero8), unroll=True)

    def pass_on(prod_re, prod_im, sum_re, sum_im, at_re, at_im):
        move_re, move_im = complex_times(prod_re, prod_im, at_re, at_im)
        return move_re + sum_re, move_im + sum_im

    def compose(first, then):
        prod_re, prod_im = complex_times(then[0], then[1], first[0], first[1])
        sum_re, sum_im = pass_on(*then, first[2], first[3])
        return prod_re, prod_im, sum_re, sum_im

    grp_rows = [tuple(part[g : g + 1, :] for part in grp) for g in range(GROUPS)]
    own = grp_rows[GROUPS - 1]
    for g in range(GROUPS - 2, -1, -1):
        own = compose(own, grp_rows[g])
    z_sum[s] = jnp.concatenate(own, axis=0)
    pl.semaphore_wait(known_sem.at[3], 1)

    def four(ref, at):
        return tuple(ref[at, k : k + 1, :] for k in range(4))

    def far_first(k):
        return chips // 2 + (k // 2) * (1 - 2 * (k % 2))

    def sum_start(k, carry):
        for core in range(2):
            remote(
                z_sum.at[s], z_sum.at[s], zs_send.at[SUMMARY], zs_recv.at[SUMMARY], chip(far_first(k), core)
            ).start()
        return carry

    lax.fori_loop(1, chips, sum_start, 0)
    remote(z_sum.at[s], z_sum.at[s], zs_send.at[SUMMARY], zs_recv.at[SUMMARY], partner).start()
    sum_part = z_sum.at[pl.ds(0, seqs - 1)]
    sum_all = remote(sum_part, sum_part, zs_send.at[SUMMARY], zs_recv.at[SUMMARY], partner)

    def z_start(src, dst, kind):
        def go(k, carry):
            i = far_first(k)
            remote(src(i), dst, zs_send.at[kind], zs_recv.at[kind], chip(i)).start()
            return carry

        lax.fori_loop(1, chips, go, 0)

    def z_all(buffer, kind):
        part = buffer.at[pl.ds(0, chips - 1)]
        return remote(part, part, zs_send.at[kind], zs_recv.at[kind], chip(1))

    inp_ring[0].wait_recv()
    inp_on = [forward(inp_all, 1, 0)]
    inp_ring[1].wait_recv()
    inp_on.append(forward(inp_all, 1, 1))
    inp_own.wait()
    for copy in in_copies:
        copy.wait()
    drive = part_dot(inp_all, w_in, x)

    columns = pl.ds(pl.multiple_of(c * steps, steps), steps)

    def turn(owner, at):
        there = inp_t.at[pl.ds(pl.multiple_of(owner * width, width), width), columns]
        there[...] = inp_all[owner].T
        copy = remote(there, there, pair_send.at[PAIR_INPUTS + at], pair_recv.at[PAIR_INPUTS + at], partner)
        copy.start()
        return copy

    turned = [turn(x, 0)]
    inp_ring[2].wait_recv()
    turned.append(turn(left, 1))
    drive += part_dot(inp_all, w_in, left)
    inp_ring[3].wait_recv()
    turned.append(turn(right, 2))
    drive += part_dot(inp_all, w_in, right)
    sum_all.wait_recv()
    in_re, in_im = jnp.zeros((1, states), F32), jnp.zeros((1, states), F32)
    for j in range(seqs - 1, 0, -1):
        next_re, next_im = pass_on(*four(z_sum, j), in_re, in_im)
        in_re, in_im = jnp.where(j > s, next_re, in_re), jnp.where(j > s, next_im, in_im)
    enter = [None] * GROUPS
    for g in range(GROUPS - 1, -1, -1):
        enter[g] = (in_re, in_im)
        in_re, in_im = pass_on(*grp_rows[g], in_re, in_im)

    def back(i, carry):
        at = at_step(length - 1 - i)
        a_re, a_im = inj_re[at, :] + carry[0], inj_im[at, :] + carry[1]
        adj_re[at, :] = a_re
        adj_im[at, :] = a_im
        l_re, l_im = conj_times(dec_re[at, :], dec_im[at, :], a_re, a_im)
        left_re[at, :] = l_re
        left_im[at, :] = l_im
        return l_re, l_im

    lax.fori_loop(
        0,
        length,
        back,
        tuple(jnp.concatenate([pair[k] for pair in enter], axis=0) for k in range(2)),
        unroll=True,
    )
    bf_re, bf_im = adj_re[...].astype(BF16), adj_im[...].astype(BF16)
    adj_bf[:, :states] = bf_re
    adj_bf[:, states:] = bf_im
    first = (jnp.zeros((steps, states), jnp.int32) + c) == 0
    own_rows = pl.ds(pl.multiple_of(c * steps, steps), steps)
    adj_send[...] = jnp.where(first, adj_im[...], adj_re[...]).astype(BF16)
    adj_cat[own_rows, :] = jnp.where(first, adj_re[...], adj_im[...]).astype(BF16)
    adj_pair = remote(
        adj_send, adj_cat.at[own_rows], pair_send.at[PAIR_ADJOINT], pair_recv.at[PAIR_ADJOINT], partner
    )
    adj_pair.start()
    for copy in inp_on:
        copy.wait_recv()
    turned.append(turn(across, 3))

    adj_pair.wait_recv()
    y_copies = [
        remote(y_send.at[i], y_recv.at[i], ys_send.at[i], ys_recv.at[i], row(i + 1)) for i in range(batches - 1)
    ]
    for at, owner in enumerate((x, left, right, across)):
        turned[at].wait_recv()
        here = pl.ds(pl.multiple_of(owner * width, width), width)
        part = dot(inp_t[here, :], adj_cat[...], 1, 0)
        offset = (owner + batches - b) % batches

        @pl.when(offset == 0)
        def _():
            z_own[...] = part

        @pl.when(offset != 0)
        def _():
            to = jnp.maximum(offset - 1, 0)
            y_send[to] = part.astype(BF16)
            remote(
                y_send.at[to], y_recv.at[to], ys_send.at[to], ys_recv.at[to], row(offset)
            ).start()

    def gi_part(owner):
        return dot(adj_bf[...], w_in[pl.ds(pl.multiple_of(owner * width, width), width), :], 1, 1)

    gi_copies = []
    for i in range(1, blocks):
        gi_send[i - 1] = gi_part((x + i) % blocks).astype(BF16)
        copy = remote(gi_send.at[i - 1], gi_recv.at[i - 1], gi_ssem.at[i - 1], gi_rsem.at[i - 1], block(i))
        copy.start()
        gi_copies.append(copy)

    drive += part_dot(inp_all, w_in, across)
    drv_re[...] = drive[:, :states]
    drv_im[...] = drive[:, states:]

    def run(i, carry):
        prod_re, prod_im, sum_re, sum_im = carry
        at = at_step(i)
        d_re, d_im = dec_re[at, :], dec_im[at, :]
        prod_re, prod_im = complex_times(d_re, d_im, prod_re, prod_im)
        sum_re, sum_im = pass_on(d_re, d_im, drv_re[at, :], drv_im[at, :], sum_re, sum_im)
        return prod_re, prod_im, sum_re, sum_im

    fwd = lax.fori_loop(0, length, run, (one8, zero8, zero8, zero8), unroll=True)
    fwd_rows = [tuple(part[g : g + 1, :] for part in fwd) for g in range(GROUPS)]
    for copy in saved_copies:
        copy.wait()
    spans = saved_ref.shape[1]
    begin = [None] * GROUPS
    for span in range(spans):
        slot = jnp.zeros((1, states), jnp.int32) + index_ref[0, span]
        at_re, at_im = jnp.zeros((1, states), F32), jnp.zeros((1, states), F32)
        for k in range(spans):
            at_re = jnp.where(slot == k, saved_ref[0, k, 0:1, :], at_re)
            at_im = jnp.where(slot == k, saved_ref[0, k, 1:2, :], at_im)
        for g in range(span * GROUPS // spans, (span + 1) * GROUPS // spans):
            begin[g] = (at_re, at_im)
            at_re, at_im = pass_on(*fwd_rows[g], at_re, at_im)

    def rerun(i, carry):
        at = at_step(i)
        pri_re[at, :] = carry[0]
        pri_im[at, :] = carry[1]
        return pass_on(dec_re[at, :], dec_im[at, :], drv_re[at, :], drv_im[at, :], *carry)

    lax.fori_loop(
        0,
        length,
        rerun,
        tuple(jnp.concatenate([pair[k] for pair in begin], axis=0) for k in range(2)),
        unroll=True,
    )
    wide_re, wide_im = conj_times(pri_re[...], pri_im[...], left_re[...], left_im[...])
    weight = step_col[...]
    z_dec[z] = jnp.concatenate(
        [jnp.sum(weight * part, axis=0, keepdims=True) for part in (wide_re, wide_im)], axis=0
    )
    z_start(lambda i: z_dec.at[z], z_dec.at[z], DECAY)

    for copy in y_copies:
        copy.wait_recv()
    total = z_own[...]
    for i in range(batches - 1):
        total += y_recv[i].astype(F32)
    z_own[...] = total
    z_send[...] = total.reshape(chips, piece, states).astype(BF16)
    z_recv[z] = jnp.zeros((piece, states), BF16)
    z_start(lambda i: z_send.at[(z + i) % chips], z_recv.at[z], REDUCE)

    z_all(z_dec, DECAY).wait_recv()
    part = z_dec[0]
    for j in range(1, chips):
        part += z_dec[j]
    y_dec[b] = part
    dec_copies = []
    for i in range(1, batches):
        copy = remote(y_dec.at[b], y_dec.at[b], yd_send.at[i - 1], yd_recv.at[i - 1], row(i))
        copy.start()
        dec_copies.append(copy)

    z_all(z_recv, REDUCE).wait_recv()
    total = z_own[pl.ds(pl.multiple_of(z * piece, piece), piece), :]
    for j in range(chips):
        total += z_recv[j].astype(F32)
    scale = 1.0 / math.sqrt(batches * seqs * steps)
    gp_bf[c, z] = (total * scale).astype(BF16)

    mine = gp_bf.at[c, z]

    def spread(offset, kind, core=c):
        remote(mine, mine, zs_send.at[kind], zs_recv.at[kind], chip(offset, core)).start()

    def hand(offset, kind):
        there = gp_bf.at[c, (z + offset) % chips]
        remote(there, there, pair_send.at[kind], pair_recv.at[kind], partner).start()

    reach = chips // 2
    near = [sign * d for d in range(min(4, reach - 1), 0, -1) for sign in (1, -1)]
    far = [sign * d for d in range(reach - 1, 4, -1) for sign in (1, -1)]

    def groups(kind, pair_kind, count, extra):
        if count == 0 and extra == 0:
            return (None, None)
        part = gp_bf.at[c, pl.ds(0, max(count, 1))]
        more = gp_bf.at[c, pl.ds(0, count + extra)]
        return (
            remote(part, part, zs_send.at[kind], zs_recv.at[kind], partner) if count else None,
            remote(more, more, pair_send.at[pair_kind], pair_recv.at[pair_kind], partner),
        )

    spread(reach, OPPOSITE, 0)
    spread(reach, OPPOSITE, 1)
    for offset in far:
        spread(offset + chips, FAR)
    for offset in near:
        spread(offset + chips, NEAR)
    hand(0, PAIR_NEAR)
    near_all, near_hand = groups(NEAR, PAIR_NEAR, len(near), 1)
    far_all, far_hand = groups(FAR, PAIR_FAR, len(far), 0)
    two = gp_bf.at[c, pl.ds(0, 2)]
    opposite_all = remote(two, two, zs_send.at[OPPOSITE], zs_recv.at[OPPOSITE], partner)

    own_gi = gi_part(x)
    for i in range(blocks - 1):
        gi_copies[i].wait_recv()
        own_gi += gi_recv[i].astype(F32)
    gi_bf[...] = own_gi.astype(BF16)
    gi_out = local(gi_bf, gi_ref.at[0], 6)

    if near:
        near_all.wait_recv()
        for offset in near:
            hand(offset + chips, PAIR_NEAR)
    for copy in dec_copies:
        copy.wait_recv()
    part = y_dec[0]
    for j in range(1, batches):
        part += y_dec[j]
    pair_dec[c] = part
    dec_pair = remote(pair_dec.at[c], pair_dec.at[c], pair_send.at[PAIR_DECAY], pair_recv.at[PAIR_DECAY], partner)
    dec_pair.start()
    dec_pair.wait_recv()
    gd_own[...] = (pair_dec[0] + pair_dec[1]) / (batches * seqs * steps)
    gd_out = local(gd_own, gd_ref, 13)

    if far:
        far_all.wait_recv()
        for offset in far:
            hand(offset + chips, PAIR_FAR)
    opposite_all.wait_recv()
    gp_f32[c] = gp_bf[c].astype(F32)
    gp_outs = [local(gp_f32.at[c], gp_ref.at[c], 7)]
    near_hand.wait_recv()
    if far:
        far_hand.wait_recv()
    gp_f32[1 - c] = gp_bf[1 - c].astype(F32)
    gp_outs.append(local(gp_f32.at[1 - c], gp_ref.at[1 - c], 14))

    for copy in cot_ring + cot_on + inp_ring + inp_on + turned + gi_copies + y_copies + dec_copies:
        copy.wait_send()
    for copy in (sum_all, adj_pair, dec_pair, near_all, near_hand, far_all, far_hand, opposite_all):
        if copy is not None:
            copy.wait_send()
    for buffer, kind in ((z_dec, DECAY), (z_send, REDUCE)):
        z_all(buffer, kind).wait_send()
    for copy in (gi_out, gd_out, *gp_outs):
        copy.wait()


def hand_out(gi_in, gp_in, gd_in, gi_out, gp_out, gd_out, gi, gp, gd, sems):
    parts = ((gp_in, gp, gp_out), (gi_in, gi, gi_out), (gd_in, gd, gd_out))
    come = [pltpu.make_async_copy(src, here, sems.at[0, i]) for i, (src, here, _) in enumerate(parts)]
    go = [pltpu.make_async_copy(here, dst, sems.at[1, i]) for i, (_, here, dst) in enumerate(parts)]
    for copy in come:
        copy.start()
    for first, then in zip(come, go):
        first.wait()
        then.start()
    for copy in go:
        copy.wait()


def local(sizes, inputs, cotangent, step_size, resets, log_decay, in_proj, out_proj, saved_states, saved_index):
    seqs, batches, blocks = sizes
    chips = seqs // 2
    _, steps, width = inputs.shape
    _, features, states = in_proj.shape
    rows = features // batches
    piece = rows // chips
    hbm_spec = pl.BlockSpec(memory_space=pltpu.HBM)
    per_step = pltpu.VMEM((steps, states), F32)
    dma = pltpu.SemaphoreType.DMA
    grad_inputs, grad_proj, grad_decay = pl.pallas_call(
        functools.partial(kernel, sizes),
        out_shape=(
            jax.ShapeDtypeStruct((1, steps, width), BF16),
            jax.ShapeDtypeStruct((2, chips, piece, states), F32),
            jax.ShapeDtypeStruct((2, states), F32),
        ),
        in_specs=[hbm_spec] * 9,
        out_specs=(hbm_spec, hbm_spec, hbm_spec),
        scratch_shapes=[
            pltpu.VMEM((blocks, steps, width), BF16),
            pltpu.VMEM((blocks, steps, width), BF16),
            pltpu.VMEM((features, 2 * states), BF16),
            pltpu.VMEM((features, 2 * states), BF16),
            pltpu.VMEM((features, 2 * steps), BF16),
            *([per_step] * 13),
            pltpu.VMEM((steps, 2 * states), BF16),
            pltpu.VMEM((steps, states), BF16),
            pltpu.VMEM((2 * steps, states), BF16),
            pltpu.VMEM((seqs, 4, states), F32),
            pltpu.VMEM((blocks - 1, steps, width), BF16),
            pltpu.VMEM((blocks - 1, steps, width), BF16),
            pltpu.VMEM((steps, width), BF16),
            pltpu.VMEM((batches - 1, rows, states), BF16),
            pltpu.VMEM((batches - 1, rows, states), BF16),
            pltpu.VMEM((rows, states), F32),
            pltpu.VMEM((chips, piece, states), BF16),
            pltpu.VMEM((chips, piece, states), BF16),
            pltpu.VMEM((2, chips, piece, states), BF16),
            pltpu.VMEM((2, chips, piece, states), F32),
            pltpu.VMEM((chips, 2, states), F32),
            pltpu.VMEM((batches, 2, states), F32),
            pltpu.VMEM((2, 2, states), F32),
            pltpu.VMEM(step_size.shape, F32),
            pltpu.VMEM(resets.shape, jnp.int32),
            pltpu.VMEM(log_decay.shape, F32),
            pltpu.VMEM(saved_states.shape, F32),
            pltpu.SMEM(saved_index.shape, jnp.int32),
            pltpu.VMEM((2, states), F32),
            pltpu.SemaphoreType.REGULAR((4,)),
            dma((15,)),
            dma((2, 6)),
            dma((2, 6)),
            dma((PAIR_INPUTS + blocks,)),
            dma((PAIR_INPUTS + blocks,)),
            dma((6,)),
            dma((6,)),
            dma((batches - 1,)),
            dma((batches - 1,)),
            dma((batches - 1,)),
            dma((batches - 1,)),
            dma((blocks - 1,)),
            dma((blocks - 1,)),
        ],
        compiler_params=pltpu.CompilerParams(
            collective_id=0, has_side_effects=True, vmem_limit_bytes=60 * 1024 * 1024
        ),
    )(cotangent, inputs, step_size, resets, log_decay, in_proj, out_proj, saved_states, saved_index)
    results = (grad_inputs, grad_proj.reshape(2, rows, states), grad_decay)
    return pl.pallas_call(
        hand_out,
        out_shape=[jax.ShapeDtypeStruct(part.shape, part.dtype) for part in results],
        in_specs=[hbm_spec] * 3,
        out_specs=[hbm_spec] * 3,
        scratch_shapes=[*(pltpu.VMEM(part.shape, part.dtype) for part in results), dma((2, 3))],
        compiler_params=pltpu.CompilerParams(vmem_limit_bytes=60 * 1024 * 1024),
    )(*results)


def solution(mesh):
    in_specs = (
        P("batch", "seq", "state"),
        P("batch", "seq", "state"),
        P("batch", "seq"),
        P("batch", "seq"),
        P(None, "state"),
        P(None, None, "state"),
        P(None, None, "state"),
        P("batch", "seq", None, "state"),
        P("batch", "seq"),
    )
    out_specs = (P("batch", "seq", "state"), P(None, "batch", "state"), P(None, "state"))
    sizes = (mesh.shape["seq"], mesh.shape["batch"], mesh.shape["state"])
    return jax.shard_map(
        functools.partial(local, sizes), mesh=mesh, in_specs=in_specs, out_specs=out_specs, check_vma=False
    )
```

```python
import functools
import math

import jax
import jax.numpy as jnp
from jax import lax
from jax.experimental import pallas as pl
from jax.experimental.pallas import tpu as pltpu
from jax.sharding import PartitionSpec as P

MESH = pl.DeviceIdType.MESH
F32 = jnp.float32
BF16 = jnp.bfloat16
GROUPS = 8
CLASSES = 4
SUMMARY, DECAY = range(2)
PAIR_ADJOINT, PAIR_DECAY, PAIR_PROJ = range(3)
PAIR_INPUTS = PAIR_PROJ + 3


def complex_times(left_re, left_im, right_re, right_im):
    return (left_re * right_re - left_im * right_im, left_re * right_im + left_im * right_re)


def conj_times(left_re, left_im, right_re, right_im):
    return (left_re * right_re + left_im * right_im, left_re * right_im - left_im * right_re)


def dot(left, right, left_dim, right_dim):
    return lax.dot_general(
        left, right, (((left_dim,), (right_dim,)), ((), ())), preferred_element_type=F32
    )


def small_exp(x):
    total = jnp.full_like(x, 1.0 / 5040.0)
    for factor in (1.0 / 720.0, 1.0 / 120.0, 1.0 / 24.0, 1.0 / 6.0, 0.5):
        total = total * x + factor
    near = 1.0 + (x + x * x * total)
    return jnp.where(x > -0.4, near, jnp.exp(x))


def cos_sin(angle):
    turns = jnp.floor(angle * (2.0 / math.pi) + 0.5)
    rest = angle - turns * 1.5703125
    rest = rest - turns * 4.837512969970703125e-4
    rest = rest - turns * 7.54978995489188216e-8
    square = rest * rest
    sine = ((-1.9515295891e-4 * square + 8.3321608736e-3) * square - 1.6666654611e-1) * square
    sine = sine * rest + rest
    cosine = (2.443315711809948e-5 * square - 1.388731625493765e-3) * square + 4.166664568298827e-2
    cosine = cosine * square * square - 0.5 * square + 1.0
    half = jnp.floor(turns * 0.5)
    odd = turns - 2.0 * half
    negative = half - 2.0 * jnp.floor(half * 0.5)
    sign = 1.0 - 2.0 * negative
    swap = odd > 0.5
    return (
        sign * jnp.where(swap, -sine, cosine),
        sign * jnp.where(swap, cosine, sine),
    )


def column(row):
    steps = row.shape[1]
    return jnp.concatenate(
        [
            jnp.broadcast_to(row[:, at : at + 128], (128, 128)).T
            for at in range(0, steps, 128)
        ],
        axis=0,
    )


def kernel(
    sizes,
    cot_ref,
    inp_ref,
    step_hbm,
    resets_hbm,
    rate_hbm,
    w_in_ref,
    w_out_ref,
    saved_hbm,
    index_hbm,
    gi_ref,
    gp_ref,
    gd_ref,
    cot_all,
    inp_all,
    w_in,
    w_out,
    inp_t,
    dec_re,
    dec_im,
    step_col,
    inj_re,
    inj_im,
    drv_re,
    drv_im,
    adj_re,
    adj_im,
    left_re,
    left_im,
    pri_re,
    pri_im,
    adj_bf,
    adj_send,
    adj_cat,
    z_sum,
    gi_send,
    gi_recv,
    gi_bf,
    g_send,
    g_full,
    g_half,
    z_own,
    z_mem,
    gp_bf,
    gp_f32,
    z_dec,
    y_dec,
    pair_dec,
    step_ref,
    resets_ref,
    rate_ref,
    saved_ref,
    index_ref,
    gd_own,
    known_sem,
    local_sem,
    ring_send,
    ring_recv,
    pair_send,
    pair_recv,
    zs_send,
    zs_recv,
    gs_send,
    gs_recv,
    zm_send,
    zm_recv,
    sp_send,
    sp_recv,
    yd_send,
    yd_recv,
    gi_ssem,
    gi_rsem,
):
    seqs, batches, blocks = sizes
    chips = seqs // 2
    steps, width = cot_all.shape[1], cot_all.shape[2]
    half = steps // 2
    length = steps // GROUPS
    states = dec_re.shape[1]
    piece = z_mem.shape[1]
    s, b, x = lax.axis_index("seq"), lax.axis_index("batch"), lax.axis_index("state")
    z, c = s // 2, s % 2
    partner = {"seq": 2 * z + (1 - c)}
    right, left = (x + 1) % blocks, (x + blocks - 1) % blocks
    across = (x + 2) % blocks

    def chip(offset, core=c):
        return {"seq": 2 * ((z + offset) % chips) + core}

    def row(offset):
        return {"batch": (b + offset) % batches}

    def block(offset):
        return {"state": (x + offset) % blocks}

    def remote(src, dst, send, recv, device):
        return pltpu.make_async_remote_copy(
            src_ref=src, dst_ref=dst, send_sem=send, recv_sem=recv, device_id=device, device_id_type=MESH
        )

    barrier = pltpu.get_barrier_semaphore()
    peers = [partner]
    peers += [block(i) for i in range(1, blocks)]
    peers += [row(i) for i in range(1, batches)]
    peers += [chip(1), chip(chips - 1)]

    def greet(semaphore, devices):
        for device in devices:
            pl.semaphore_signal(semaphore, inc=1, device_id=device, device_id_type=MESH)

    greet(barrier, peers)

    rounds = [1 << i for i in range(chips.bit_length() - 2)]

    def round_start(at):
        if at < len(rounds):
            greet(known_sem.at[at], [chip(rounds[at]), chip(chips - rounds[at])])

    def round_end(at):
        if at < len(rounds):
            pl.semaphore_wait(known_sem.at[at], 2)

    def local(src, dst, at):
        copy = pltpu.make_async_copy(src, dst, local_sem.at[at])
        copy.start()
        return copy

    cot_own = local(cot_ref.at[0], cot_all.at[x], 0)
    out_copies = [local(w_out_ref.at[k], w_out.at[:, pl.ds(k * states, states)], 1 + k) for k in range(2)]
    inp_own = local(inp_ref.at[0], inp_all.at[x], 3)
    small = ((step_hbm, step_ref), (resets_hbm, resets_ref), (rate_hbm, rate_ref))
    small_copies = [local(*pair, 8 + k) for k, pair in enumerate(small)]
    saved_copies = [local(saved_hbm, saved_ref, 11), local(index_hbm, index_ref, 12)]
    in_copies = [local(w_in_ref.at[k], w_in.at[:, pl.ds(k * states, states)], 4 + k) for k in range(2)]

    pl.semaphore_wait(barrier, len(peers))
    round_start(0)

    low, high = pl.ds(0, half), pl.ds(half, half)

    def ring(ref, whole, at):
        def send(part, device, sem):
            copy = remote(
                ref.at[0, part], whole.at[x, part], ring_send.at[at, sem], ring_recv.at[at, sem], device
            )
            copy.start()
            return copy

        return [
            send(low, block(1), 0),
            send(high, block(blocks - 1), 1),
            send(high, block(1), 2),
            send(low, block(blocks - 1), 3),
        ]

    def forward(whole, at, way):
        owner, part, device = ((left, low, block(1)), (right, high, block(blocks - 1)))[way]
        copy = remote(
            whole.at[owner, part], whole.at[owner, part], ring_send.at[at, 4 + way], ring_recv.at[at, 4 + way], device
        )
        copy.start()
        return copy

    cot_ring = ring(cot_ref, cot_all, 0)

    for copy in small_copies:
        copy.wait()
    step = step_ref[...]
    keep = (1 - resets_ref[...]).astype(F32)
    wide = column(step)
    magnitude = column(keep) * small_exp(wide * rate_ref[0:1, :])
    cosine, sine = cos_sin(wide * rate_ref[1:2, :])
    dec_re[...] = magnitude * cosine
    dec_im[...] = magnitude * sine
    step_col[...] = wide

    def part_dot(whole, weights, owner):
        return dot(whole[owner], weights[pl.ds(pl.multiple_of(owner * width, width), width), :], 1, 0)

    cot_own.wait()
    for copy in out_copies:
        copy.wait()
    inject = part_dot(cot_all, w_out, x)
    round_end(0)
    round_start(1)
    cot_ring[0].wait_recv()
    cot_on = [forward(cot_all, 0, 0)]
    cot_ring[1].wait_recv()
    cot_on.append(forward(cot_all, 0, 1))
    inp_ring = ring(inp_ref, inp_all, 1)
    round_end(1)
    round_start(2)
    cot_ring[2].wait_recv()
    inject += part_dot(cot_all, w_out, left)
    cot_ring[3].wait_recv()
    inject += part_dot(cot_all, w_out, right)
    round_end(2)
    greet(known_sem.at[3], [partner])
    greet(known_sem.at[4], [row(i) for i in range(1, batches)])
    for copy in cot_on:
        copy.wait_recv()
    inject += part_dot(cot_all, w_out, across)
    inj_re[...] = inject[:, :states]
    inj_im[...] = -inject[:, states:]

    def at_step(j):
        return pl.ds(j, GROUPS, stride=length)

    zero8 = jnp.zeros((GROUPS, states), F32)
    one8 = jnp.ones((GROUPS, states), F32)

    def leave(i, carry):
        prod_re, prod_im, sum_re, sum_im = carry
        at = at_step(length - 1 - i)
        d_re, d_im = dec_re[at, :], dec_im[at, :]
        prod_re, prod_im = conj_times(d_re, d_im, prod_re, prod_im)
        sum_re, sum_im = conj_times(d_re, d_im, inj_re[at, :] + sum_re, inj_im[at, :] + sum_im)
        return prod_re, prod_im, sum_re, sum_im

    grp = lax.fori_loop(0, length, leave, (one8, zero8, zero8, zero8), unroll=True)

    def pass_on(prod_re, prod_im, sum_re, sum_im, at_re, at_im):
        move_re, move_im = complex_times(prod_re, prod_im, at_re, at_im)
        return move_re + sum_re, move_im + sum_im

    def compose(first, then):
        prod_re, prod_im = complex_times(then[0], then[1], first[0], first[1])
        sum_re, sum_im = pass_on(*then, first[2], first[3])
        return prod_re, prod_im, sum_re, sum_im

    grp_rows = [tuple(part[g : g + 1, :] for part in grp) for g in range(GROUPS)]
    own = grp_rows[GROUPS - 1]
    for g in range(GROUPS - 2, -1, -1):
        own = compose(own, grp_rows[g])
    z_sum[s] = jnp.concatenate(own, axis=0)
    pl.semaphore_wait(known_sem.at[3], 1)

    def four(ref, at):
        return tuple(ref[at, k : k + 1, :] for k in range(4))

    def far_first(k):
        return chips // 2 + (k // 2) * (1 - 2 * (k % 2))

    def sum_start(k, carry):
        for core in range(2):
            remote(
                z_sum.at[s], z_sum.at[s], zs_send.at[SUMMARY], zs_recv.at[SUMMARY], chip(far_first(k), core)
            ).start()
        return carry

    lax.fori_loop(1, chips, sum_start, 0)
    remote(z_sum.at[s], z_sum.at[s], zs_send.at[SUMMARY], zs_recv.at[SUMMARY], partner).start()
    sum_part = z_sum.at[pl.ds(0, seqs - 1)]
    sum_all = remote(sum_part, sum_part, zs_send.at[SUMMARY], zs_recv.at[SUMMARY], partner)

    def z_start(src, dst, kind):
        def go(k, carry):
            i = far_first(k)
            remote(src(i), dst, zs_send.at[kind], zs_recv.at[kind], chip(i)).start()
            return carry

        lax.fori_loop(1, chips, go, 0)

    def z_all(buffer, kind):
        part = buffer.at[pl.ds(0, chips - 1)]
        return remote(part, part, zs_send.at[kind], zs_recv.at[kind], chip(1))

    inp_ring[0].wait_recv()
    inp_on = [forward(inp_all, 1, 0)]
    inp_ring[1].wait_recv()
    inp_on.append(forward(inp_all, 1, 1))
    inp_own.wait()
    for copy in in_copies:
        copy.wait()
    drive = part_dot(inp_all, w_in, x)

    columns = pl.ds(pl.multiple_of(c * steps, steps), steps)

    def turn(owner, at):
        there = inp_t.at[pl.ds(pl.multiple_of(owner * width, width), width), columns]
        there[...] = inp_all[owner].T
        copy = remote(there, there, pair_send.at[PAIR_INPUTS + at], pair_recv.at[PAIR_INPUTS + at], partner)
        copy.start()
        return copy

    turned = [turn(x, 0)]
    inp_ring[2].wait_recv()
    turned.append(turn(left, 1))
    drive += part_dot(inp_all, w_in, left)
    inp_ring[3].wait_recv()
    turned.append(turn(right, 2))
    drive += part_dot(inp_all, w_in, right)
    sum_all.wait_recv()
    in_re, in_im = jnp.zeros((1, states), F32), jnp.zeros((1, states), F32)
    for j in range(seqs - 1, 0, -1):
        next_re, next_im = pass_on(*four(z_sum, j), in_re, in_im)
        in_re, in_im = jnp.where(j > s, next_re, in_re), jnp.where(j > s, next_im, in_im)
    enter = [None] * GROUPS
    for g in range(GROUPS - 1, -1, -1):
        enter[g] = (in_re, in_im)
        in_re, in_im = pass_on(*grp_rows[g], in_re, in_im)

    def back(i, carry):
        at = at_step(length - 1 - i)
        a_re, a_im = inj_re[at, :] + carry[0], inj_im[at, :] + carry[1]
        adj_re[at, :] = a_re
        adj_im[at, :] = a_im
        l_re, l_im = conj_times(dec_re[at, :], dec_im[at, :], a_re, a_im)
        left_re[at, :] = l_re
        left_im[at, :] = l_im
        return l_re, l_im

    lax.fori_loop(
        0,
        length,
        back,
        tuple(jnp.concatenate([pair[k] for pair in enter], axis=0) for k in range(2)),
        unroll=True,
    )
    bf_re, bf_im = adj_re[...].astype(BF16), adj_im[...].astype(BF16)
    adj_bf[:, :states] = bf_re
    adj_bf[:, states:] = bf_im
    first = (jnp.zeros((steps, states), jnp.int32) + c) == 0
    own_rows = pl.ds(pl.multiple_of(c * steps, steps), steps)
    adj_send[...] = jnp.where(first, adj_im[...], adj_re[...]).astype(BF16)
    adj_cat[own_rows, :] = jnp.where(first, adj_re[...], adj_im[...]).astype(BF16)
    adj_pair = remote(
        adj_send, adj_cat.at[own_rows], pair_send.at[PAIR_ADJOINT], pair_recv.at[PAIR_ADJOINT], partner
    )
    adj_pair.start()
    for copy in inp_on:
        copy.wait_recv()
    turned.append(turn(across, 3))

    adj_pair.wait_recv()
    pl.semaphore_wait(known_sem.at[4], batches - 1)
    kind = z % CLASSES
    around = (2, -2, 1, -1, 0)

    def class_rows(of, at):
        start = of * piece + (piece // 2 if at == -2 else 0)
        size = piece // 2 if abs(at) == 2 else piece
        return pl.ds(pl.multiple_of(start, size), size)

    def near_copy(offset, at):
        src = g_send.at[offset, class_rows((z + at + chips) % CLASSES, at)]
        place = around.index(at)
        dst = g_half.at[offset, place] if abs(at) == 2 else g_full.at[offset, place - 2]
        device = {"seq": 2 * ((z + at + chips) % chips) + c, "batch": (b + offset) % batches}
        return remote(src, dst, gs_send.at[offset, place], gs_recv.at[offset, place], device)

    for at, owner in enumerate((x, left, right, across)):
        turned[at].wait_recv()
        here = pl.ds(pl.multiple_of(owner * width, width), width)
        part = dot(inp_t[here, :], adj_cat[...], 1, 0)
        offset = (owner + batches - b) % batches
        g_send[offset] = part.astype(BF16)
        for distance in around[:-1]:
            near_copy(offset, distance).start()

        @pl.when(offset == 0)
        def _():
            z_own[...] = part

        @pl.when(offset != 0)
        def _():
            near_copy(offset, 0).start()

    g_copies = {
        (offset, distance): near_copy(offset, distance)
        for offset in range(batches)
        for distance in around
        if offset or distance
    }

    def gi_part(owner):
        return dot(adj_bf[...], w_in[pl.ds(pl.multiple_of(owner * width, width), width), :], 1, 1)

    gi_copies = []
    for i in range(1, blocks):
        gi_send[i - 1] = gi_part((x + i) % blocks).astype(BF16)
        copy = remote(gi_send.at[i - 1], gi_recv.at[i - 1], gi_ssem.at[i - 1], gi_rsem.at[i - 1], block(i))
        copy.start()
        gi_copies.append(copy)

    drive += part_dot(inp_all, w_in, across)
    drv_re[...] = drive[:, :states]
    drv_im[...] = drive[:, states:]

    def run(i, carry):
        prod_re, prod_im, sum_re, sum_im = carry
        at = at_step(i)
        d_re, d_im = dec_re[at, :], dec_im[at, :]
        prod_re, prod_im = complex_times(d_re, d_im, prod_re, prod_im)
        sum_re, sum_im = pass_on(d_re, d_im, drv_re[at, :], drv_im[at, :], sum_re, sum_im)
        return prod_re, prod_im, sum_re, sum_im

    fwd = lax.fori_loop(0, length, run, (one8, zero8, zero8, zero8), unroll=True)
    fwd_rows = [tuple(part[g : g + 1, :] for part in fwd) for g in range(GROUPS)]
    for copy in saved_copies:
        copy.wait()
    spans = saved_ref.shape[1]
    begin = [None] * GROUPS
    for span in range(spans):
        slot = jnp.zeros((1, states), jnp.int32) + index_ref[0, span]
        at_re, at_im = jnp.zeros((1, states), F32), jnp.zeros((1, states), F32)
        for k in range(spans):
            at_re = jnp.where(slot == k, saved_ref[0, k, 0:1, :], at_re)
            at_im = jnp.where(slot == k, saved_ref[0, k, 1:2, :], at_im)
        for g in range(span * GROUPS // spans, (span + 1) * GROUPS // spans):
            begin[g] = (at_re, at_im)
            at_re, at_im = pass_on(*fwd_rows[g], at_re, at_im)

    def rerun(i, carry):
        at = at_step(i)
        pri_re[at, :] = carry[0]
        pri_im[at, :] = carry[1]
        return pass_on(dec_re[at, :], dec_im[at, :], drv_re[at, :], drv_im[at, :], *carry)

    lax.fori_loop(
        0,
        length,
        rerun,
        tuple(jnp.concatenate([pair[k] for pair in begin], axis=0) for k in range(2)),
        unroll=True,
    )
    wide_re, wide_im = conj_times(pri_re[...], pri_im[...], left_re[...], left_im[...])
    weight = step_col[...]
    z_dec[z] = jnp.concatenate(
        [jnp.sum(weight * part, axis=0, keepdims=True) for part in (wide_re, wide_im)], axis=0
    )
    z_start(lambda i: z_dec.at[z], z_dec.at[z], DECAY)

    for copy in g_copies.values():
        copy.wait_recv()
    total = z_own[class_rows(kind, 0), :]
    for offset in range(batches):
        if offset:
            total += g_full[offset, 2].astype(F32)
        total += g_full[offset, 0].astype(F32) + g_full[offset, 1].astype(F32)
        total += jnp.concatenate([g_half[offset, 0], g_half[offset, 1]], axis=0).astype(F32)
    z_mem[z // CLASSES] = total.astype(BF16)
    member = z_mem.at[z // CLASSES]
    members = []
    for i in range(chips // CLASSES - 1):
        copy = remote(member, member, zm_send.at[i], zm_recv.at[i], chip(CLASSES * (i + 1)))
        copy.start()
        members.append(copy)

    z_all(z_dec, DECAY).wait_recv()
    part = z_dec[0]
    for j in range(1, chips):
        part += z_dec[j]
    y_dec[b] = part
    dec_copies = []
    for i in range(1, batches):
        copy = remote(y_dec.at[b], y_dec.at[b], yd_send.at[i - 1], yd_recv.at[i - 1], row(i))
        copy.start()
        dec_copies.append(copy)

    for copy in members:
        copy.wait_recv()
    total = z_mem[0].astype(F32)
    for i in range(1, chips // CLASSES):
        total += z_mem[i].astype(F32)
    scale = 1.0 / math.sqrt(batches * seqs * steps)
    gp_bf[c, kind] = (total * scale).astype(BF16)

    def spread(at, core, place):
        rows_of = pl.ds(piece // 2 if at == -2 else 0, piece // 2 if abs(at) == 2 else piece)
        mine = gp_bf.at[c, kind, rows_of]
        copy = remote(mine, mine, sp_send.at[place], sp_recv.at[place], chip(at + chips, core))
        copy.start()
        return copy

    def hand(of, place):
        there = gp_bf.at[c, of]
        copy = remote(there, there, pair_send.at[place], pair_recv.at[place], partner)
        copy.start()
        return copy

    halves = [spread(at, core, place) for place, (at, core) in enumerate(((2, c), (-2, c), (2, 1 - c), (-2, 1 - c)))]
    wholes = [spread(1, c, 4), spread(-1, c, 5)]
    hands = [hand(kind, PAIR_PROJ)]

    own_gi = gi_part(x)
    for i in range(blocks - 1):
        gi_copies[i].wait_recv()
        own_gi += gi_recv[i].astype(F32)
    gi_bf[...] = own_gi.astype(BF16)
    gi_out = local(gi_bf, gi_ref.at[0], 6)

    wholes[0].wait_recv()
    hands.append(hand((kind + CLASSES - 1) % CLASSES, PAIR_PROJ + 1))
    wholes[1].wait_recv()
    hands.append(hand((kind + 1) % CLASSES, PAIR_PROJ + 2))
    for copy in dec_copies:
        copy.wait_recv()
    part = y_dec[0]
    for j in range(1, batches):
        part += y_dec[j]
    pair_dec[c] = part
    dec_pair = remote(pair_dec.at[c], pair_dec.at[c], pair_send.at[PAIR_DECAY], pair_recv.at[PAIR_DECAY], partner)
    dec_pair.start()
    dec_pair.wait_recv()
    gd_own[...] = (pair_dec[0] + pair_dec[1]) / (batches * seqs * steps)
    gd_out = local(gd_own, gd_ref, 13)

    for copy in halves[:2]:
        copy.wait_recv()
    gp_f32[c] = gp_bf[c].astype(F32)
    gp_outs = [local(gp_f32.at[c], gp_ref.at[c], 7)]
    for copy in halves[2:] + hands:
        copy.wait_recv()
    gp_f32[1 - c] = gp_bf[1 - c].astype(F32)
    gp_outs.append(local(gp_f32.at[1 - c], gp_ref.at[1 - c], 14))

    for copy in cot_ring + cot_on + inp_ring + inp_on + turned + gi_copies + dec_copies:
        copy.wait_send()
    for copy in (sum_all, adj_pair, dec_pair, *g_copies.values(), *members, *halves, *wholes, *hands):
        copy.wait_send()
    z_all(z_dec, DECAY).wait_send()
    for copy in (gi_out, gd_out, *gp_outs):
        copy.wait()


def hand_out(gi_in, gp_in, gd_in, gi_out, gp_out, gd_out, gi, gp, gd, sems):
    parts = ((gp_in, gp, gp_out), (gi_in, gi, gi_out), (gd_in, gd, gd_out))
    come = [pltpu.make_async_copy(src, here, sems.at[0, i]) for i, (src, here, _) in enumerate(parts)]
    go = [pltpu.make_async_copy(here, dst, sems.at[1, i]) for i, (_, here, dst) in enumerate(parts)]
    for copy in come:
        copy.start()
    for first, then in zip(come, go):
        first.wait()
        then.start()
    for copy in go:
        copy.wait()


def local(sizes, inputs, cotangent, step_size, resets, log_decay, in_proj, out_proj, saved_states, saved_index):
    seqs, batches, blocks = sizes
    chips = seqs // 2
    _, steps, width = inputs.shape
    _, features, states = in_proj.shape
    rows = features // batches
    piece = rows // CLASSES
    hbm_spec = pl.BlockSpec(memory_space=pltpu.HBM)
    per_step = pltpu.VMEM((steps, states), F32)
    dma = pltpu.SemaphoreType.DMA
    grad_inputs, grad_proj, grad_decay = pl.pallas_call(
        functools.partial(kernel, sizes),
        out_shape=(
            jax.ShapeDtypeStruct((1, steps, width), BF16),
            jax.ShapeDtypeStruct((2, CLASSES, piece, states), F32),
            jax.ShapeDtypeStruct((2, states), F32),
        ),
        in_specs=[hbm_spec] * 9,
        out_specs=(hbm_spec, hbm_spec, hbm_spec),
        scratch_shapes=[
            pltpu.VMEM((blocks, steps, width), BF16),
            pltpu.VMEM((blocks, steps, width), BF16),
            pltpu.VMEM((features, 2 * states), BF16),
            pltpu.VMEM((features, 2 * states), BF16),
            pltpu.VMEM((features, 2 * steps), BF16),
            *([per_step] * 13),
            pltpu.VMEM((steps, 2 * states), BF16),
            pltpu.VMEM((steps, states), BF16),
            pltpu.VMEM((2 * steps, states), BF16),
            pltpu.VMEM((seqs, 4, states), F32),
            pltpu.VMEM((blocks - 1, steps, width), BF16),
            pltpu.VMEM((blocks - 1, steps, width), BF16),
            pltpu.VMEM((steps, width), BF16),
            pltpu.VMEM((batches, rows, states), BF16),
            pltpu.VMEM((batches, 3, piece, states), BF16),
            pltpu.VMEM((batches, 2, piece // 2, states), BF16),
            pltpu.VMEM((rows, states), F32),
            pltpu.VMEM((chips // CLASSES, piece, states), BF16),
            pltpu.VMEM((2, CLASSES, piece, states), BF16),
            pltpu.VMEM((2, CLASSES, piece, states), F32),
            pltpu.VMEM((chips, 2, states), F32),
            pltpu.VMEM((batches, 2, states), F32),
            pltpu.VMEM((2, 2, states), F32),
            pltpu.VMEM(step_size.shape, F32),
            pltpu.VMEM(resets.shape, jnp.int32),
            pltpu.VMEM(log_decay.shape, F32),
            pltpu.VMEM(saved_states.shape, F32),
            pltpu.SMEM(saved_index.shape, jnp.int32),
            pltpu.VMEM((2, states), F32),
            pltpu.SemaphoreType.REGULAR((5,)),
            dma((15,)),
            dma((2, 6)),
            dma((2, 6)),
            dma((PAIR_INPUTS + blocks,)),
            dma((PAIR_INPUTS + blocks,)),
            dma((2,)),
            dma((2,)),
            dma((batches, 5)),
            dma((batches, 5)),
            dma((chips // CLASSES,)),
            dma((chips // CLASSES,)),
            dma((6,)),
            dma((6,)),
            dma((batches - 1,)),
            dma((batches - 1,)),
            dma((blocks - 1,)),
            dma((blocks - 1,)),
        ],
        compiler_params=pltpu.CompilerParams(
            collective_id=0, has_side_effects=True, vmem_limit_bytes=60 * 1024 * 1024
        ),
    )(cotangent, inputs, step_size, resets, log_decay, in_proj, out_proj, saved_states, saved_index)
    results = (grad_inputs, grad_proj.reshape(2, rows, states), grad_decay)
    return pl.pallas_call(
        hand_out,
        out_shape=[jax.ShapeDtypeStruct(part.shape, part.dtype) for part in results],
        in_specs=[hbm_spec] * 3,
        out_specs=[hbm_spec] * 3,
        scratch_shapes=[*(pltpu.VMEM(part.shape, part.dtype) for part in results), dma((2, 3))],
        compiler_params=pltpu.CompilerParams(vmem_limit_bytes=60 * 1024 * 1024),
    )(*results)


def solution(mesh):
    in_specs = (
        P("batch", "seq", "state"),
        P("batch", "seq", "state"),
        P("batch", "seq"),
        P("batch", "seq"),
        P(None, "state"),
        P(None, None, "state"),
        P(None, None, "state"),
        P("batch", "seq", None, "state"),
        P("batch", "seq"),
    )
    out_specs = (P("batch", "seq", "state"), P(None, "batch", "state"), P(None, "state"))
    sizes = (mesh.shape["seq"], mesh.shape["batch"], mesh.shape["state"])
    return jax.shard_map(
        functools.partial(local, sizes), mesh=mesh, in_specs=in_specs, out_specs=out_specs, check_vma=False
    )
```

```python
import functools
import math

import jax
import jax.numpy as jnp
from jax import lax
from jax.experimental import pallas as pl
from jax.experimental.pallas import tpu as pltpu
from jax.sharding import PartitionSpec as P

MESH = pl.DeviceIdType.MESH
F32 = jnp.float32
BF16 = jnp.bfloat16
GROUPS = 8
CLASSES = 4
SUMMARY, DECAY = range(2)
PAIR_ADJOINT, PAIR_DECAY, PAIR_PROJ = range(3)
PAIR_INPUTS = PAIR_PROJ + 3


def complex_times(left_re, left_im, right_re, right_im):
    return (left_re * right_re - left_im * right_im, left_re * right_im + left_im * right_re)


def conj_times(left_re, left_im, right_re, right_im):
    return (left_re * right_re + left_im * right_im, left_re * right_im - left_im * right_re)


def dot(left, right, left_dim, right_dim):
    return lax.dot_general(
        left, right, (((left_dim,), (right_dim,)), ((), ())), preferred_element_type=F32
    )


def small_exp(x):
    total = jnp.full_like(x, 1.0 / 5040.0)
    for factor in (1.0 / 720.0, 1.0 / 120.0, 1.0 / 24.0, 1.0 / 6.0, 0.5):
        total = total * x + factor
    near = 1.0 + (x + x * x * total)
    return jnp.where(x > -0.4, near, jnp.exp(x))


def cos_sin(angle):
    turns = jnp.floor(angle * (2.0 / math.pi) + 0.5)
    rest = angle - turns * 1.5703125
    rest = rest - turns * 4.837512969970703125e-4
    rest = rest - turns * 7.54978995489188216e-8
    square = rest * rest
    sine = ((-1.9515295891e-4 * square + 8.3321608736e-3) * square - 1.6666654611e-1) * square
    sine = sine * rest + rest
    cosine = (2.443315711809948e-5 * square - 1.388731625493765e-3) * square + 4.166664568298827e-2
    cosine = cosine * square * square - 0.5 * square + 1.0
    half = jnp.floor(turns * 0.5)
    odd = turns - 2.0 * half
    negative = half - 2.0 * jnp.floor(half * 0.5)
    sign = 1.0 - 2.0 * negative
    swap = odd > 0.5
    return (
        sign * jnp.where(swap, -sine, cosine),
        sign * jnp.where(swap, cosine, sine),
    )


def column(row):
    steps = row.shape[1]
    return jnp.concatenate(
        [
            jnp.broadcast_to(row[:, at : at + 128], (128, 128)).T
            for at in range(0, steps, 128)
        ],
        axis=0,
    )


def kernel(
    sizes,
    cot_ref,
    inp_ref,
    step_hbm,
    resets_hbm,
    rate_hbm,
    w_in_ref,
    w_out_ref,
    saved_hbm,
    index_hbm,
    gi_ref,
    gp_ref,
    gd_ref,
    cot_all,
    inp_all,
    w_in,
    w_out,
    inp_t,
    dec_re,
    dec_im,
    step_col,
    inj_re,
    inj_im,
    drv_re,
    drv_im,
    adj_re,
    adj_im,
    left_re,
    left_im,
    pri_re,
    pri_im,
    adj_bf,
    adj_send,
    adj_cat,
    z_sum,
    gi_send,
    gi_recv,
    gi_bf,
    g_send,
    g_full,
    g_half,
    z_own,
    z_mem,
    gp_bf,
    z_dec,
    y_dec,
    pair_dec,
    step_ref,
    resets_ref,
    rate_ref,
    saved_ref,
    index_ref,
    gd_own,
    known_sem,
    local_sem,
    ring_send,
    ring_recv,
    pair_send,
    pair_recv,
    zs_send,
    zs_recv,
    gs_send,
    gs_recv,
    zm_send,
    zm_recv,
    sp_send,
    sp_recv,
    yd_send,
    yd_recv,
    gi_ssem,
    gi_rsem,
):
    seqs, batches, blocks = sizes
    chips = seqs // 2
    steps, width = cot_all.shape[1], cot_all.shape[2]
    half = steps // 2
    length = steps // GROUPS
    states = dec_re.shape[1]
    piece = z_mem.shape[1]
    s, b, x = lax.axis_index("seq"), lax.axis_index("batch"), lax.axis_index("state")
    z, c = s // 2, s % 2
    partner = {"seq": 2 * z + (1 - c)}
    right, left = (x + 1) % blocks, (x + blocks - 1) % blocks
    across = (x + 2) % blocks

    def chip(offset, core=c):
        return {"seq": 2 * ((z + offset) % chips) + core}

    def row(offset):
        return {"batch": (b + offset) % batches}

    def block(offset):
        return {"state": (x + offset) % blocks}

    def remote(src, dst, send, recv, device):
        return pltpu.make_async_remote_copy(
            src_ref=src, dst_ref=dst, send_sem=send, recv_sem=recv, device_id=device, device_id_type=MESH
        )

    barrier = pltpu.get_barrier_semaphore()
    peers = [partner]
    peers += [block(i) for i in range(1, blocks)]
    peers += [row(i) for i in range(1, batches)]
    peers += [chip(offset, core) for offset in (1, chips - 1) for core in (c, 1 - c)]

    def greet(semaphore, devices):
        for device in devices:
            pl.semaphore_signal(semaphore, inc=1, device_id=device, device_id_type=MESH)

    greet(barrier, peers)

    rounds = [1 << i for i in range(chips.bit_length() - 2)]

    def round_start(at):
        if at < len(rounds):
            both = (rounds[at], chips - rounds[at])
            greet(known_sem.at[at], [chip(offset, core) for offset in both for core in (c, 1 - c)])

    def round_end(at):
        if at < len(rounds):
            pl.semaphore_wait(known_sem.at[at], 4)

    def local(src, dst, at):
        copy = pltpu.make_async_copy(src, dst, local_sem.at[at])
        copy.start()
        return copy

    cot_own = local(cot_ref.at[0], cot_all.at[x], 0)
    out_copies = [local(w_out_ref.at[k], w_out.at[:, pl.ds(k * states, states)], 1 + k) for k in range(2)]
    inp_own = local(inp_ref.at[0], inp_all.at[x], 3)
    small = ((step_hbm, step_ref), (resets_hbm, resets_ref), (rate_hbm, rate_ref))
    small_copies = [local(*pair, 8 + k) for k, pair in enumerate(small)]
    saved_copies = [local(saved_hbm, saved_ref, 11), local(index_hbm, index_ref, 12)]
    in_copies = [local(w_in_ref.at[k], w_in.at[:, pl.ds(k * states, states)], 4 + k) for k in range(2)]

    pl.semaphore_wait(barrier, len(peers))
    round_start(0)

    low, high = pl.ds(0, half), pl.ds(half, half)

    def ring(ref, whole, at):
        def send(part, device, sem):
            copy = remote(
                ref.at[0, part], whole.at[x, part], ring_send.at[at, sem], ring_recv.at[at, sem], device
            )
            copy.start()
            return copy

        return [
            send(low, block(1), 0),
            send(high, block(blocks - 1), 1),
            send(high, block(1), 2),
            send(low, block(blocks - 1), 3),
        ]

    def forward(whole, at, way):
        owner, part, device = ((left, low, block(1)), (right, high, block(blocks - 1)))[way]
        copy = remote(
            whole.at[owner, part], whole.at[owner, part], ring_send.at[at, 4 + way], ring_recv.at[at, 4 + way], device
        )
        copy.start()
        return copy

    cot_ring = ring(cot_ref, cot_all, 0)

    for copy in small_copies:
        copy.wait()
    step = step_ref[...]
    keep = (1 - resets_ref[...]).astype(F32)
    wide = column(step)
    magnitude = column(keep) * small_exp(wide * rate_ref[0:1, :])
    cosine, sine = cos_sin(wide * rate_ref[1:2, :])
    dec_re[...] = magnitude * cosine
    dec_im[...] = magnitude * sine
    step_col[...] = wide

    def part_dot(whole, weights, owner):
        return dot(whole[owner], weights[pl.ds(pl.multiple_of(owner * width, width), width), :], 1, 0)

    cot_own.wait()
    for copy in out_copies:
        copy.wait()
    round_end(0)
    round_start(1)
    inject = part_dot(cot_all, w_out, x)
    cot_ring[0].wait_recv()
    cot_on = [forward(cot_all, 0, 0)]
    cot_ring[1].wait_recv()
    cot_on.append(forward(cot_all, 0, 1))
    round_end(1)
    round_start(2)
    inp_ring = ring(inp_ref, inp_all, 1)
    cot_ring[2].wait_recv()
    inject += part_dot(cot_all, w_out, left)
    cot_ring[3].wait_recv()
    inject += part_dot(cot_all, w_out, right)
    round_end(2)
    greet(known_sem.at[3], [row(i) for i in range(1, batches)])
    for copy in cot_on:
        copy.wait_recv()
    inject += part_dot(cot_all, w_out, across)
    inj_re[...] = inject[:, :states]
    inj_im[...] = -inject[:, states:]

    def at_step(j):
        return pl.ds(j, GROUPS, stride=length)

    zero8 = jnp.zeros((GROUPS, states), F32)
    one8 = jnp.ones((GROUPS, states), F32)

    def leave(i, carry):
        prod_re, prod_im, sum_re, sum_im = carry
        at = at_step(length - 1 - i)
        d_re, d_im = dec_re[at, :], dec_im[at, :]
        prod_re, prod_im = conj_times(d_re, d_im, prod_re, prod_im)
        sum_re, sum_im = conj_times(d_re, d_im, inj_re[at, :] + sum_re, inj_im[at, :] + sum_im)
        return prod_re, prod_im, sum_re, sum_im

    grp = lax.fori_loop(0, length, leave, (one8, zero8, zero8, zero8), unroll=True)

    def pass_on(prod_re, prod_im, sum_re, sum_im, at_re, at_im):
        move_re, move_im = complex_times(prod_re, prod_im, at_re, at_im)
        return move_re + sum_re, move_im + sum_im

    def compose(first, then):
        prod_re, prod_im = complex_times(then[0], then[1], first[0], first[1])
        sum_re, sum_im = pass_on(*then, first[2], first[3])
        return prod_re, prod_im, sum_re, sum_im

    grp_rows = [tuple(part[g : g + 1, :] for part in grp) for g in range(GROUPS)]
    own = grp_rows[GROUPS - 1]
    for g in range(GROUPS - 2, -1, -1):
        own = compose(own, grp_rows[g])
    z_sum[s] = jnp.concatenate(own, axis=0)

    def four(ref, at):
        return tuple(ref[at, k : k + 1, :] for k in range(4))

    def far_first(k):
        return chips // 2 + (k // 2) * (1 - 2 * (k % 2))

    def sum_start(k, carry):
        for core in range(2):
            remote(
                z_sum.at[s], z_sum.at[s], zs_send.at[SUMMARY], zs_recv.at[SUMMARY], chip(far_first(k), core)
            ).start()
        return carry

    lax.fori_loop(1, chips, sum_start, 0)
    remote(z_sum.at[s], z_sum.at[s], zs_send.at[SUMMARY], zs_recv.at[SUMMARY], partner).start()
    sum_part = z_sum.at[pl.ds(0, seqs - 1)]
    sum_all = remote(sum_part, sum_part, zs_send.at[SUMMARY], zs_recv.at[SUMMARY], partner)

    def z_start(src, dst, kind):
        def go(k, carry):
            i = far_first(k)
            remote(src(i), dst, zs_send.at[kind], zs_recv.at[kind], chip(i)).start()
            return carry

        lax.fori_loop(1, chips, go, 0)

    def z_all(buffer, kind):
        part = buffer.at[pl.ds(0, chips - 1)]
        return remote(part, part, zs_send.at[kind], zs_recv.at[kind], chip(1))

    inp_ring[0].wait_recv()
    inp_on = [forward(inp_all, 1, 0)]
    inp_ring[1].wait_recv()
    inp_on.append(forward(inp_all, 1, 1))
    inp_own.wait()
    for copy in in_copies:
        copy.wait()
    drive = part_dot(inp_all, w_in, x)

    columns = pl.ds(pl.multiple_of(c * steps, steps), steps)

    def turn(owner, at):
        there = inp_t.at[pl.ds(pl.multiple_of(owner * width, width), width), columns]
        there[...] = inp_all[owner].T
        copy = remote(there, there, pair_send.at[PAIR_INPUTS + at], pair_recv.at[PAIR_INPUTS + at], partner)
        copy.start()
        return copy

    turned = [turn(x, 0)]
    inp_ring[2].wait_recv()
    turned.append(turn(left, 1))
    drive += part_dot(inp_all, w_in, left)
    inp_ring[3].wait_recv()
    turned.append(turn(right, 2))
    drive += part_dot(inp_all, w_in, right)
    for copy in inp_on:
        copy.wait_recv()
    turned.append(turn(across, 3))

    sum_all.wait_recv()
    in_re, in_im = jnp.zeros((1, states), F32), jnp.zeros((1, states), F32)
    for j in range(seqs - 1, 0, -1):
        next_re, next_im = pass_on(*four(z_sum, j), in_re, in_im)
        in_re, in_im = jnp.where(j > s, next_re, in_re), jnp.where(j > s, next_im, in_im)
    enter = [None] * GROUPS
    for g in range(GROUPS - 1, -1, -1):
        enter[g] = (in_re, in_im)
        in_re, in_im = pass_on(*grp_rows[g], in_re, in_im)

    def back(i, carry):
        at = at_step(length - 1 - i)
        a_re, a_im = inj_re[at, :] + carry[0], inj_im[at, :] + carry[1]
        adj_re[at, :] = a_re
        adj_im[at, :] = a_im
        l_re, l_im = conj_times(dec_re[at, :], dec_im[at, :], a_re, a_im)
        left_re[at, :] = l_re
        left_im[at, :] = l_im
        return l_re, l_im

    lax.fori_loop(
        0,
        length,
        back,
        tuple(jnp.concatenate([pair[k] for pair in enter], axis=0) for k in range(2)),
        unroll=True,
    )
    bf_re, bf_im = adj_re[...].astype(BF16), adj_im[...].astype(BF16)
    adj_bf[:, :states] = bf_re
    adj_bf[:, states:] = bf_im
    first = (jnp.zeros((steps, states), jnp.int32) + c) == 0
    own_rows = pl.ds(pl.multiple_of(c * steps, steps), steps)
    adj_send[...] = jnp.where(first, adj_im[...], adj_re[...]).astype(BF16)
    adj_cat[own_rows, :] = jnp.where(first, adj_re[...], adj_im[...]).astype(BF16)
    adj_pair = remote(
        adj_send, adj_cat.at[own_rows], pair_send.at[PAIR_ADJOINT], pair_recv.at[PAIR_ADJOINT], partner
    )
    adj_pair.start()

    adj_pair.wait_recv()
    pl.semaphore_wait(known_sem.at[3], batches - 1)
    kind = z % CLASSES
    around = (2, -2, 1, -1, 0)

    def class_rows(of, at):
        start = of * piece + (piece // 2 if at == -2 else 0)
        size = piece // 2 if abs(at) == 2 else piece
        return pl.ds(pl.multiple_of(start, size), size)

    def near_copy(offset, at):
        src = g_send.at[offset, class_rows((z + at + chips) % CLASSES, at)]
        place = around.index(at)
        dst = g_half.at[offset, place] if abs(at) == 2 else g_full.at[offset, place - 2]
        device = {"seq": 2 * ((z + at + chips) % chips) + c, "batch": (b + offset) % batches}
        return remote(src, dst, gs_send.at[offset, place], gs_recv.at[offset, place], device)

    for copy in turned:
        copy.wait_recv()
    for place, offset in enumerate((2, 1, 3, 0)):
        owner = (b + offset) % batches
        here = pl.ds(pl.multiple_of(owner * width, width), width)
        part = dot(inp_t[here, :], adj_cat[...], 1, 0)
        g_send[offset] = part.astype(BF16)
        for distance in around[:-1]:
            near_copy(offset, distance).start()

        if place == 3:
            z_own[...] = part
        else:
            near_copy(offset, 0).start()

    g_copies = {
        (offset, distance): near_copy(offset, distance)
        for offset in range(batches)
        for distance in around
        if offset or distance
    }

    def gi_part(owner):
        return dot(adj_bf[...], w_in[pl.ds(pl.multiple_of(owner * width, width), width), :], 1, 1)

    gi_copies = []
    for i in range(1, blocks):
        gi_send[i - 1] = gi_part((x + i) % blocks).astype(BF16)
        copy = remote(gi_send.at[i - 1], gi_recv.at[i - 1], gi_ssem.at[i - 1], gi_rsem.at[i - 1], block(i))
        copy.start()
        gi_copies.append(copy)

    drive += part_dot(inp_all, w_in, across)
    drv_re[...] = drive[:, :states]
    drv_im[...] = drive[:, states:]

    def run(i, carry):
        prod_re, prod_im, sum_re, sum_im = carry
        at = at_step(i)
        d_re, d_im = dec_re[at, :], dec_im[at, :]
        prod_re, prod_im = complex_times(d_re, d_im, prod_re, prod_im)
        sum_re, sum_im = pass_on(d_re, d_im, drv_re[at, :], drv_im[at, :], sum_re, sum_im)
        return prod_re, prod_im, sum_re, sum_im

    fwd = lax.fori_loop(0, length, run, (one8, zero8, zero8, zero8), unroll=True)
    fwd_rows = [tuple(part[g : g + 1, :] for part in fwd) for g in range(GROUPS)]
    for copy in saved_copies:
        copy.wait()
    spans = saved_ref.shape[1]
    begin = [None] * GROUPS
    for span in range(spans):
        slot = jnp.zeros((1, states), jnp.int32) + index_ref[0, span]
        at_re, at_im = jnp.zeros((1, states), F32), jnp.zeros((1, states), F32)
        for k in range(spans):
            at_re = jnp.where(slot == k, saved_ref[0, k, 0:1, :], at_re)
            at_im = jnp.where(slot == k, saved_ref[0, k, 1:2, :], at_im)
        for g in range(span * GROUPS // spans, (span + 1) * GROUPS // spans):
            begin[g] = (at_re, at_im)
            at_re, at_im = pass_on(*fwd_rows[g], at_re, at_im)

    def rerun(i, carry):
        at = at_step(i)
        pri_re[at, :] = carry[0]
        pri_im[at, :] = carry[1]
        return pass_on(dec_re[at, :], dec_im[at, :], drv_re[at, :], drv_im[at, :], *carry)

    lax.fori_loop(
        0,
        length,
        rerun,
        tuple(jnp.concatenate([pair[k] for pair in begin], axis=0) for k in range(2)),
        unroll=True,
    )
    wide_re, wide_im = conj_times(pri_re[...], pri_im[...], left_re[...], left_im[...])
    weight = step_col[...]
    z_dec[z] = jnp.concatenate(
        [jnp.sum(weight * part, axis=0, keepdims=True) for part in (wide_re, wide_im)], axis=0
    )
    z_start(lambda i: z_dec.at[z], z_dec.at[z], DECAY)

    for copy in g_copies.values():
        copy.wait_recv()
    total = z_own[class_rows(kind, 0), :]
    for offset in range(batches):
        if offset:
            total += g_full[offset, 2].astype(F32)
        total += g_full[offset, 0].astype(F32) + g_full[offset, 1].astype(F32)
        total += jnp.concatenate([g_half[offset, 0], g_half[offset, 1]], axis=0).astype(F32)
    z_mem[z // CLASSES] = total.astype(BF16)
    member = z_mem.at[z // CLASSES]
    members = []
    for i in range(chips // CLASSES - 1):
        copy = remote(member, member, zm_send.at[i], zm_recv.at[i], chip(CLASSES * (i + 1)))
        copy.start()
        members.append(copy)

    z_all(z_dec, DECAY).wait_recv()
    part = z_dec[0]
    for j in range(1, chips):
        part += z_dec[j]
    y_dec[b] = part
    dec_copies = []
    for i in range(1, batches):
        copy = remote(y_dec.at[b], y_dec.at[b], yd_send.at[i - 1], yd_recv.at[i - 1], row(i))
        copy.start()
        dec_copies.append(copy)

    for copy in members:
        copy.wait_recv()
    total = z_mem[0].astype(F32)
    for i in range(1, chips // CLASSES):
        total += z_mem[i].astype(F32)
    scale = 1.0 / math.sqrt(batches * seqs * steps)
    gp_bf[c, kind] = (total * scale).astype(BF16)

    def spread(at, core, place):
        rows_of = pl.ds(piece // 2 if at == -2 else 0, piece // 2 if abs(at) == 2 else piece)
        mine = gp_bf.at[c, kind, rows_of]
        copy = remote(mine, mine, sp_send.at[place], sp_recv.at[place], chip(at + chips, core))
        copy.start()
        return copy

    def hand(of, place):
        there = gp_bf.at[c, of]
        copy = remote(there, there, pair_send.at[place], pair_recv.at[place], partner)
        copy.start()
        return copy

    halves = [spread(at, core, place) for place, (at, core) in enumerate(((2, c), (-2, c), (2, 1 - c), (-2, 1 - c)))]
    wholes = [spread(1, c, 4), spread(-1, c, 5)]
    hands = [hand(kind, PAIR_PROJ)]

    own_gi = gi_part(x)
    for i in range(blocks - 1):
        gi_copies[i].wait_recv()
        own_gi += gi_recv[i].astype(F32)
    gi_bf[...] = own_gi.astype(BF16)
    gi_out = local(gi_bf, gi_ref.at[0], 6)

    wholes[0].wait_recv()
    hands.append(hand((kind + CLASSES - 1) % CLASSES, PAIR_PROJ + 1))
    wholes[1].wait_recv()
    hands.append(hand((kind + 1) % CLASSES, PAIR_PROJ + 2))
    for copy in dec_copies:
        copy.wait_recv()
    part = y_dec[0]
    for j in range(1, batches):
        part += y_dec[j]
    pair_dec[c] = part
    dec_pair = remote(pair_dec.at[c], pair_dec.at[c], pair_send.at[PAIR_DECAY], pair_recv.at[PAIR_DECAY], partner)
    dec_pair.start()
    dec_pair.wait_recv()
    gd_own[...] = (pair_dec[0] + pair_dec[1]) / (batches * seqs * steps)
    gd_out = local(gd_own, gd_ref, 13)

    for copy in halves[:2]:
        copy.wait_recv()
    gp_outs = [local(gp_bf.at[c], gp_ref.at[c], 7)]
    for copy in halves[2:] + hands:
        copy.wait_recv()
    gp_outs.append(local(gp_bf.at[1 - c], gp_ref.at[1 - c], 14))

    for copy in cot_ring + cot_on + inp_ring + inp_on + turned + gi_copies + dec_copies:
        copy.wait_send()
    for copy in (sum_all, adj_pair, dec_pair, *g_copies.values(), *members, *halves, *wholes, *hands):
        copy.wait_send()
    z_all(z_dec, DECAY).wait_send()
    for copy in (gi_out, gd_out, *gp_outs):
        copy.wait()


def hand_out(gi_in, gp_in, gd_in, gi_out, gp_out, gd_out, gi, gp, gd, wide, sems):
    parts = [(gp_in.at[k], gp.at[k], wide.at[k], gp_out.at[k]) for k in range(2)]
    parts += [(gi_in, gi, gi, gi_out), (gd_in, gd, gd, gd_out)]
    come = [pltpu.make_async_copy(part[0], part[1], sems.at[0, i]) for i, part in enumerate(parts)]
    go = [pltpu.make_async_copy(part[2], part[3], sems.at[1, i]) for i, part in enumerate(parts)]
    for copy in come:
        copy.start()
    for i in range(len(parts)):
        come[i].wait()
        if i < 2:
            wide[i] = gp[i].astype(F32)
        go[i].start()
    for copy in go:
        copy.wait()


def local(sizes, inputs, cotangent, step_size, resets, log_decay, in_proj, out_proj, saved_states, saved_index):
    seqs, batches, blocks = sizes
    chips = seqs // 2
    _, steps, width = inputs.shape
    _, features, states = in_proj.shape
    rows = features // batches
    piece = rows // CLASSES
    hbm_spec = pl.BlockSpec(memory_space=pltpu.HBM)
    per_step = pltpu.VMEM((steps, states), F32)
    dma = pltpu.SemaphoreType.DMA
    grad_inputs, grad_proj, grad_decay = pl.pallas_call(
        functools.partial(kernel, sizes),
        out_shape=(
            jax.ShapeDtypeStruct((1, steps, width), BF16),
            jax.ShapeDtypeStruct((2, CLASSES, piece, states), BF16),
            jax.ShapeDtypeStruct((2, states), F32),
        ),
        in_specs=[hbm_spec] * 9,
        out_specs=(hbm_spec, hbm_spec, hbm_spec),
        scratch_shapes=[
            pltpu.VMEM((blocks, steps, width), BF16),
            pltpu.VMEM((blocks, steps, width), BF16),
            pltpu.VMEM((features, 2 * states), BF16),
            pltpu.VMEM((features, 2 * states), BF16),
            pltpu.VMEM((features, 2 * steps), BF16),
            *([per_step] * 13),
            pltpu.VMEM((steps, 2 * states), BF16),
            pltpu.VMEM((steps, states), BF16),
            pltpu.VMEM((2 * steps, states), BF16),
            pltpu.VMEM((seqs, 4, states), F32),
            pltpu.VMEM((blocks - 1, steps, width), BF16),
            pltpu.VMEM((blocks - 1, steps, width), BF16),
            pltpu.VMEM((steps, width), BF16),
            pltpu.VMEM((batches, rows, states), BF16),
            pltpu.VMEM((batches, 3, piece, states), BF16),
            pltpu.VMEM((batches, 2, piece // 2, states), BF16),
            pltpu.VMEM((rows, states), F32),
            pltpu.VMEM((chips // CLASSES, piece, states), BF16),
            pltpu.VMEM((2, CLASSES, piece, states), BF16),
            pltpu.VMEM((chips, 2, states), F32),
            pltpu.VMEM((batches, 2, states), F32),
            pltpu.VMEM((2, 2, states), F32),
            pltpu.VMEM(step_size.shape, F32),
            pltpu.VMEM(resets.shape, jnp.int32),
            pltpu.VMEM(log_decay.shape, F32),
            pltpu.VMEM(saved_states.shape, F32),
            pltpu.SMEM(saved_index.shape, jnp.int32),
            pltpu.VMEM((2, states), F32),
            pltpu.SemaphoreType.REGULAR((4,)),
            dma((15,)),
            dma((2, 6)),
            dma((2, 6)),
            dma((PAIR_INPUTS + blocks,)),
            dma((PAIR_INPUTS + blocks,)),
            dma((2,)),
            dma((2,)),
            dma((batches, 5)),
            dma((batches, 5)),
            dma((chips // CLASSES,)),
            dma((chips // CLASSES,)),
            dma((6,)),
            dma((6,)),
            dma((batches - 1,)),
            dma((batches - 1,)),
            dma((blocks - 1,)),
            dma((blocks - 1,)),
        ],
        compiler_params=pltpu.CompilerParams(
            collective_id=0, has_side_effects=True, vmem_limit_bytes=60 * 1024 * 1024
        ),
    )(cotangent, inputs, step_size, resets, log_decay, in_proj, out_proj, saved_states, saved_index)
    results = (grad_inputs, grad_proj.reshape(2, rows, states), grad_decay)
    return pl.pallas_call(
        hand_out,
        out_shape=[
            jax.ShapeDtypeStruct(grad_inputs.shape, BF16),
            jax.ShapeDtypeStruct((2, rows, states), F32),
            jax.ShapeDtypeStruct(grad_decay.shape, F32),
        ],
        in_specs=[hbm_spec] * 3,
        out_specs=[hbm_spec] * 3,
        scratch_shapes=[
            *(pltpu.VMEM(part.shape, part.dtype) for part in results),
            pltpu.VMEM((2, rows, states), F32),
            dma((2, 4)),
        ],
        compiler_params=pltpu.CompilerParams(vmem_limit_bytes=60 * 1024 * 1024),
    )(*results)


def solution(mesh):
    in_specs = (
        P("batch", "seq", "state"),
        P("batch", "seq", "state"),
        P("batch", "seq"),
        P("batch", "seq"),
        P(None, "state"),
        P(None, None, "state"),
        P(None, None, "state"),
        P("batch", "seq", None, "state"),
        P("batch", "seq"),
    )
    out_specs = (P("batch", "seq", "state"), P(None, "batch", "state"), P(None, "state"))
    sizes = (mesh.shape["seq"], mesh.shape["batch"], mesh.shape["state"])
    return jax.shard_map(
        functools.partial(local, sizes), mesh=mesh, in_specs=in_specs, out_specs=out_specs, check_vma=False
    )
```

```python
import functools
import math

import jax
import jax.numpy as jnp
from jax import lax
from jax.experimental import pallas as pl
from jax.experimental.pallas import tpu as pltpu
from jax.sharding import PartitionSpec as P

MESH = pl.DeviceIdType.MESH
F32 = jnp.float32
BF16 = jnp.bfloat16
GROUPS = 8
CLASSES = 4
SUMMARY, DECAY = range(2)
PAIR_ADJOINT, PAIR_DECAY, PAIR_PROJ = range(3)
PAIR_INPUTS = PAIR_PROJ + 3


def complex_times(left_re, left_im, right_re, right_im):
    return (left_re * right_re - left_im * right_im, left_re * right_im + left_im * right_re)


def conj_times(left_re, left_im, right_re, right_im):
    return (left_re * right_re + left_im * right_im, left_re * right_im - left_im * right_re)


def dot(left, right, left_dim, right_dim):
    return lax.dot_general(
        left, right, (((left_dim,), (right_dim,)), ((), ())), preferred_element_type=F32
    )


def small_exp(x):
    total = jnp.full_like(x, 1.0 / 5040.0)
    for factor in (1.0 / 720.0, 1.0 / 120.0, 1.0 / 24.0, 1.0 / 6.0, 0.5):
        total = total * x + factor
    near = 1.0 + (x + x * x * total)
    return jnp.where(x > -0.4, near, jnp.exp(x))


def cos_sin(angle):
    turns = jnp.floor(angle * (2.0 / math.pi) + 0.5)
    rest = angle - turns * 1.5703125
    rest = rest - turns * 4.837512969970703125e-4
    rest = rest - turns * 7.54978995489188216e-8
    square = rest * rest
    sine = ((-1.9515295891e-4 * square + 8.3321608736e-3) * square - 1.6666654611e-1) * square
    sine = sine * rest + rest
    cosine = (2.443315711809948e-5 * square - 1.388731625493765e-3) * square + 4.166664568298827e-2
    cosine = cosine * square * square - 0.5 * square + 1.0
    half = jnp.floor(turns * 0.5)
    odd = turns - 2.0 * half
    negative = half - 2.0 * jnp.floor(half * 0.5)
    sign = 1.0 - 2.0 * negative
    swap = odd > 0.5
    return (
        sign * jnp.where(swap, -sine, cosine),
        sign * jnp.where(swap, cosine, sine),
    )


def column(row):
    steps = row.shape[1]
    return jnp.concatenate(
        [
            jnp.broadcast_to(row[:, at : at + 128], (128, 128)).T
            for at in range(0, steps, 128)
        ],
        axis=0,
    )


def kernel(
    sizes,
    cot_ref,
    inp_ref,
    step_hbm,
    resets_hbm,
    rate_hbm,
    w_in_ref,
    w_out_ref,
    saved_hbm,
    index_hbm,
    gi_ref,
    gp_ref,
    gd_ref,
    cot_all,
    inp_all,
    w_in,
    w_out,
    inp_t,
    dec_re,
    dec_im,
    step_col,
    inj_re,
    inj_im,
    drv_re,
    drv_im,
    adj_re,
    adj_im,
    left_re,
    left_im,
    pri_re,
    pri_im,
    adj_bf,
    adj_send,
    adj_cat,
    z_sum,
    gi_send,
    gi_recv,
    gi_bf,
    g_send,
    g_full,
    g_half,
    z_own,
    z_mem,
    gp_bf,
    z_dec,
    y_dec,
    pair_dec,
    step_ref,
    resets_ref,
    rate_ref,
    saved_ref,
    index_ref,
    gd_own,
    known_sem,
    local_sem,
    ring_send,
    ring_recv,
    pair_send,
    pair_recv,
    zs_send,
    zs_recv,
    gs_send,
    gs_recv,
    zm_send,
    zm_recv,
    sp_send,
    sp_recv,
    yd_send,
    yd_recv,
    gi_ssem,
    gi_rsem,
):
    seqs, batches, blocks = sizes
    chips = seqs // 2
    steps, width = cot_all.shape[1], cot_all.shape[2]
    half = steps // 2
    length = steps // GROUPS
    states = dec_re.shape[1]
    piece = z_mem.shape[1]
    s, b, x = lax.axis_index("seq"), lax.axis_index("batch"), lax.axis_index("state")
    z, c = s // 2, s % 2
    partner = {"seq": 2 * z + (1 - c)}
    right, left = (x + 1) % blocks, (x + blocks - 1) % blocks
    across = (x + 2) % blocks

    def chip(offset, core=c):
        return {"seq": 2 * ((z + offset) % chips) + core}

    def row(offset):
        return {"batch": (b + offset) % batches}

    def block(offset):
        return {"state": (x + offset) % blocks}

    def remote(src, dst, send, recv, device):
        return pltpu.make_async_remote_copy(
            src_ref=src, dst_ref=dst, send_sem=send, recv_sem=recv, device_id=device, device_id_type=MESH
        )

    barrier = pltpu.get_barrier_semaphore()
    peers = [partner]
    peers += [block(i) for i in range(1, blocks)]
    peers += [row(i) for i in range(1, batches)]
    peers += [chip(offset, core) for offset in (1, chips - 1) for core in (c, 1 - c)]

    def greet(semaphore, devices):
        for device in devices:
            pl.semaphore_signal(semaphore, inc=1, device_id=device, device_id_type=MESH)

    greet(barrier, peers)

    rounds = [1 << i for i in range(chips.bit_length() - 2)]

    def round_start(at):
        if at < len(rounds):
            both = (rounds[at], chips - rounds[at])
            greet(known_sem.at[at], [chip(offset, core) for offset in both for core in (c, 1 - c)])

    def round_end(at):
        if at < len(rounds):
            pl.semaphore_wait(known_sem.at[at], 4)

    def local(src, dst, at):
        copy = pltpu.make_async_copy(src, dst, local_sem.at[at])
        copy.start()
        return copy

    cot_own = local(cot_ref.at[0], cot_all.at[x], 0)
    out_copies = [local(w_out_ref.at[k], w_out.at[:, pl.ds(k * states, states)], 1 + k) for k in range(2)]
    pl.semaphore_wait(barrier, len(peers))
    round_start(0)

    low, high = pl.ds(0, half), pl.ds(half, half)

    def ring(ref, whole, at):
        def send(part, device, sem):
            copy = remote(
                ref.at[0, part], whole.at[x, part], ring_send.at[at, sem], ring_recv.at[at, sem], device
            )
            copy.start()
            return copy

        return [
            send(low, block(1), 0),
            send(high, block(blocks - 1), 1),
            send(high, block(1), 2),
            send(low, block(blocks - 1), 3),
        ]

    def forward(whole, at, way):
        owner, part, device = ((left, low, block(1)), (right, high, block(blocks - 1)))[way]
        copy = remote(
            whole.at[owner, part], whole.at[owner, part], ring_send.at[at, 4 + way], ring_recv.at[at, 4 + way], device
        )
        copy.start()
        return copy

    cot_ring = ring(cot_ref, cot_all, 0)
    inp_own = local(inp_ref.at[0], inp_all.at[x], 3)
    small = ((step_hbm, step_ref), (resets_hbm, resets_ref), (rate_hbm, rate_ref))
    small_copies = [local(*pair, 8 + k) for k, pair in enumerate(small)]
    saved_copies = [local(saved_hbm, saved_ref, 11), local(index_hbm, index_ref, 12)]
    in_copies = [local(w_in_ref.at[k], w_in.at[:, pl.ds(k * states, states)], 4 + k) for k in range(2)]

    for copy in small_copies:
        copy.wait()
    step = step_ref[...]
    keep = (1 - resets_ref[...]).astype(F32)
    wide = column(step)
    magnitude = column(keep) * small_exp(wide * rate_ref[0:1, :])
    cosine, sine = cos_sin(wide * rate_ref[1:2, :])
    dec_re[...] = magnitude * cosine
    dec_im[...] = magnitude * sine
    step_col[...] = wide

    def part_dot(whole, weights, owner):
        return dot(whole[owner], weights[pl.ds(pl.multiple_of(owner * width, width), width), :], 1, 0)

    cot_own.wait()
    for copy in out_copies:
        copy.wait()
    round_end(0)
    round_start(1)
    inject = part_dot(cot_all, w_out, x)
    cot_ring[0].wait_recv()
    cot_on = [forward(cot_all, 0, 0)]
    cot_ring[1].wait_recv()
    cot_on.append(forward(cot_all, 0, 1))
    round_end(1)
    round_start(2)
    inp_ring = ring(inp_ref, inp_all, 1)
    cot_ring[2].wait_recv()
    inject += part_dot(cot_all, w_out, left)
    cot_ring[3].wait_recv()
    inject += part_dot(cot_all, w_out, right)
    round_end(2)
    greet(known_sem.at[3], [row(i) for i in range(1, batches)])
    for copy in cot_on:
        copy.wait_recv()
    inject += part_dot(cot_all, w_out, across)
    inj_re[...] = inject[:, :states]
    inj_im[...] = -inject[:, states:]

    def at_step(j):
        return pl.ds(j, GROUPS, stride=length)

    zero8 = jnp.zeros((GROUPS, states), F32)
    one8 = jnp.ones((GROUPS, states), F32)

    def leave(i, carry):
        prod_re, prod_im, sum_re, sum_im = carry
        at = at_step(length - 1 - i)
        d_re, d_im = dec_re[at, :], dec_im[at, :]
        prod_re, prod_im = conj_times(d_re, d_im, prod_re, prod_im)
        sum_re, sum_im = conj_times(d_re, d_im, inj_re[at, :] + sum_re, inj_im[at, :] + sum_im)
        return prod_re, prod_im, sum_re, sum_im

    grp = lax.fori_loop(0, length, leave, (one8, zero8, zero8, zero8), unroll=True)

    def pass_on(prod_re, prod_im, sum_re, sum_im, at_re, at_im):
        move_re, move_im = complex_times(prod_re, prod_im, at_re, at_im)
        return move_re + sum_re, move_im + sum_im

    def compose(first, then):
        prod_re, prod_im = complex_times(then[0], then[1], first[0], first[1])
        sum_re, sum_im = pass_on(*then, first[2], first[3])
        return prod_re, prod_im, sum_re, sum_im

    grp_rows = [tuple(part[g : g + 1, :] for part in grp) for g in range(GROUPS)]
    own = grp_rows[GROUPS - 1]
    for g in range(GROUPS - 2, -1, -1):
        own = compose(own, grp_rows[g])
    z_sum[s] = jnp.concatenate(own, axis=0)

    def four(ref, at):
        return tuple(ref[at, k : k + 1, :] for k in range(4))

    def far_first(k):
        return chips // 2 + (k // 2) * (1 - 2 * (k % 2))

    def sum_start(k, carry):
        for core in range(2):
            remote(
                z_sum.at[s], z_sum.at[s], zs_send.at[SUMMARY], zs_recv.at[SUMMARY], chip(far_first(k), core)
            ).start()
        return carry

    lax.fori_loop(1, chips, sum_start, 0)
    remote(z_sum.at[s], z_sum.at[s], zs_send.at[SUMMARY], zs_recv.at[SUMMARY], partner).start()
    sum_part = z_sum.at[pl.ds(0, seqs - 1)]
    sum_all = remote(sum_part, sum_part, zs_send.at[SUMMARY], zs_recv.at[SUMMARY], partner)

    def z_start(src, dst, kind):
        def go(k, carry):
            i = far_first(k)
            remote(src(i), dst, zs_send.at[kind], zs_recv.at[kind], chip(i)).start()
            return carry

        lax.fori_loop(1, chips, go, 0)

    def z_all(buffer, kind):
        part = buffer.at[pl.ds(0, chips - 1)]
        return remote(part, part, zs_send.at[kind], zs_recv.at[kind], chip(1))

    inp_ring[0].wait_recv()
    inp_on = [forward(inp_all, 1, 0)]
    inp_ring[1].wait_recv()
    inp_on.append(forward(inp_all, 1, 1))
    inp_own.wait()
    for copy in in_copies:
        copy.wait()
    drive = part_dot(inp_all, w_in, x)

    columns = pl.ds(pl.multiple_of(c * steps, steps), steps)

    def turn(owner, at):
        there = inp_t.at[pl.ds(pl.multiple_of(owner * width, width), width), columns]
        there[...] = inp_all[owner].T
        copy = remote(there, there, pair_send.at[PAIR_INPUTS + at], pair_recv.at[PAIR_INPUTS + at], partner)
        copy.start()
        return copy

    turned = [turn(x, 0)]
    inp_ring[2].wait_recv()
    turned.append(turn(left, 1))
    drive += part_dot(inp_all, w_in, left)
    inp_ring[3].wait_recv()
    turned.append(turn(right, 2))
    drive += part_dot(inp_all, w_in, right)
    for copy in inp_on:
        copy.wait_recv()
    turned.append(turn(across, 3))

    sum_all.wait_recv()
    in_re, in_im = jnp.zeros((1, states), F32), jnp.zeros((1, states), F32)
    for j in range(seqs - 1, 0, -1):
        next_re, next_im = pass_on(*four(z_sum, j), in_re, in_im)
        in_re, in_im = jnp.where(j > s, next_re, in_re), jnp.where(j > s, next_im, in_im)
    enter = [None] * GROUPS
    for g in range(GROUPS - 1, -1, -1):
        enter[g] = (in_re, in_im)
        in_re, in_im = pass_on(*grp_rows[g], in_re, in_im)

    def back(i, carry):
        at = at_step(length - 1 - i)
        a_re, a_im = inj_re[at, :] + carry[0], inj_im[at, :] + carry[1]
        adj_re[at, :] = a_re
        adj_im[at, :] = a_im
        l_re, l_im = conj_times(dec_re[at, :], dec_im[at, :], a_re, a_im)
        left_re[at, :] = l_re
        left_im[at, :] = l_im
        return l_re, l_im

    lax.fori_loop(
        0,
        length,
        back,
        tuple(jnp.concatenate([pair[k] for pair in enter], axis=0) for k in range(2)),
        unroll=True,
    )
    bf_re, bf_im = adj_re[...].astype(BF16), adj_im[...].astype(BF16)
    first = (jnp.zeros((steps, states), jnp.int32) + c) == 0
    own_rows = pl.ds(pl.multiple_of(c * steps, steps), steps)
    adj_send[...] = jnp.where(first, adj_im[...], adj_re[...]).astype(BF16)
    adj_cat[own_rows, :] = jnp.where(first, adj_re[...], adj_im[...]).astype(BF16)
    adj_pair = remote(
        adj_send, adj_cat.at[own_rows], pair_send.at[PAIR_ADJOINT], pair_recv.at[PAIR_ADJOINT], partner
    )
    adj_pair.start()
    adj_bf[:, :states] = bf_re
    adj_bf[:, states:] = bf_im

    adj_pair.wait_recv()
    pl.semaphore_wait(known_sem.at[3], batches - 1)
    kind = z % CLASSES
    around = (2, -2, 1, -1, 0)

    def class_rows(of, at):
        start = of * piece + (piece // 2 if at == -2 else 0)
        size = piece // 2 if abs(at) == 2 else piece
        return pl.ds(pl.multiple_of(start, size), size)

    def near_copy(offset, at):
        src = g_send.at[offset, class_rows((z + at + chips) % CLASSES, at)]
        place = around.index(at)
        dst = g_half.at[offset, place] if abs(at) == 2 else g_full.at[offset, place - 2]
        device = {"seq": 2 * ((z + at + chips) % chips) + c, "batch": (b + offset) % batches}
        return remote(src, dst, gs_send.at[offset, place], gs_recv.at[offset, place], device)

    for copy in turned:
        copy.wait_recv()
    for place, offset in enumerate((2, 1, 3, 0)):
        owner = (b + offset) % batches
        here = pl.ds(pl.multiple_of(owner * width, width), width)
        part = dot(inp_t[here, :], adj_cat[...], 1, 0)
        g_send[offset] = part.astype(BF16)
        for distance in around[:-1]:
            near_copy(offset, distance).start()

        if place == 3:
            z_own[...] = part
        else:
            near_copy(offset, 0).start()

    g_copies = {
        (offset, distance): near_copy(offset, distance)
        for offset in range(batches)
        for distance in around
        if offset or distance
    }

    def gi_part(owner):
        return dot(adj_bf[...], w_in[pl.ds(pl.multiple_of(owner * width, width), width), :], 1, 1)

    gi_copies = []
    for i in range(1, blocks):
        gi_send[i - 1] = gi_part((x + i) % blocks).astype(BF16)
        copy = remote(gi_send.at[i - 1], gi_recv.at[i - 1], gi_ssem.at[i - 1], gi_rsem.at[i - 1], block(i))
        copy.start()
        gi_copies.append(copy)

    drive += part_dot(inp_all, w_in, across)
    drv_re[...] = drive[:, :states]
    drv_im[...] = drive[:, states:]

    def run(i, carry):
        prod_re, prod_im, sum_re, sum_im = carry
        at = at_step(i)
        d_re, d_im = dec_re[at, :], dec_im[at, :]
        prod_re, prod_im = complex_times(d_re, d_im, prod_re, prod_im)
        sum_re, sum_im = pass_on(d_re, d_im, drv_re[at, :], drv_im[at, :], sum_re, sum_im)
        return prod_re, prod_im, sum_re, sum_im

    fwd = lax.fori_loop(0, length, run, (one8, zero8, zero8, zero8), unroll=True)
    fwd_rows = [tuple(part[g : g + 1, :] for part in fwd) for g in range(GROUPS)]
    for copy in saved_copies:
        copy.wait()
    spans = saved_ref.shape[1]
    begin = [None] * GROUPS
    for span in range(spans):
        slot = jnp.zeros((1, states), jnp.int32) + index_ref[0, span]
        at_re, at_im = jnp.zeros((1, states), F32), jnp.zeros((1, states), F32)
        for k in range(spans):
            at_re = jnp.where(slot == k, saved_ref[0, k, 0:1, :], at_re)
            at_im = jnp.where(slot == k, saved_ref[0, k, 1:2, :], at_im)
        for g in range(span * GROUPS // spans, (span + 1) * GROUPS // spans):
            begin[g] = (at_re, at_im)
            at_re, at_im = pass_on(*fwd_rows[g], at_re, at_im)

    def rerun(i, carry):
        at = at_step(i)
        pri_re[at, :] = carry[0]
        pri_im[at, :] = carry[1]
        return pass_on(dec_re[at, :], dec_im[at, :], drv_re[at, :], drv_im[at, :], *carry)

    lax.fori_loop(
        0,
        length,
        rerun,
        tuple(jnp.concatenate([pair[k] for pair in begin], axis=0) for k in range(2)),
        unroll=True,
    )
    wide_re, wide_im = conj_times(pri_re[...], pri_im[...], left_re[...], left_im[...])
    weight = step_col[...]
    z_dec[z] = jnp.concatenate(
        [jnp.sum(weight * part, axis=0, keepdims=True) for part in (wide_re, wide_im)], axis=0
    )
    z_start(lambda i: z_dec.at[z], z_dec.at[z], DECAY)

    for copy in g_copies.values():
        copy.wait_recv()
    total = z_own[class_rows(kind, 0), :]
    for offset in range(batches):
        if offset:
            total += g_full[offset, 2].astype(F32)
        total += g_full[offset, 0].astype(F32) + g_full[offset, 1].astype(F32)
        total += jnp.concatenate([g_half[offset, 0], g_half[offset, 1]], axis=0).astype(F32)
    z_mem[z // CLASSES] = total.astype(BF16)
    member = z_mem.at[z // CLASSES]
    members = []
    for i in range(chips // CLASSES - 1):
        copy = remote(member, member, zm_send.at[i], zm_recv.at[i], chip(CLASSES * (i + 1)))
        copy.start()
        members.append(copy)

    z_all(z_dec, DECAY).wait_recv()
    part = z_dec[0]
    for j in range(1, chips):
        part += z_dec[j]
    y_dec[b] = part
    dec_copies = []
    for i in range(1, batches):
        copy = remote(y_dec.at[b], y_dec.at[b], yd_send.at[i - 1], yd_recv.at[i - 1], row(i))
        copy.start()
        dec_copies.append(copy)

    for copy in members:
        copy.wait_recv()
    total = z_mem[0].astype(F32)
    for i in range(1, chips // CLASSES):
        total += z_mem[i].astype(F32)
    scale = 1.0 / math.sqrt(batches * seqs * steps)
    gp_bf[c, kind] = (total * scale).astype(BF16)

    def spread(at, core, place):
        rows_of = pl.ds(piece // 2 if at == -2 else 0, piece // 2 if abs(at) == 2 else piece)
        there = gp_ref if abs(at) == 2 else gp_bf
        mine, target = gp_bf.at[c, kind, rows_of], there.at[c, kind, rows_of]
        copy = remote(mine, target, sp_send.at[place], sp_recv.at[place], chip(at + chips, core))
        copy.start()
        return copy

    def hand(of, place):
        gp_outs.append(local(gp_bf.at[c, of], gp_ref.at[c, of], 15 + place - PAIR_PROJ))
        copy = remote(gp_bf.at[c, of], gp_ref.at[c, of], pair_send.at[place], pair_recv.at[place], partner)
        copy.start()
        return copy

    gp_outs = []
    wholes = [spread(1, c, 4), spread(-1, c, 5)]
    halves = [spread(at, core, place) for place, (at, core) in enumerate(((2, c), (-2, c), (2, 1 - c), (-2, 1 - c)))]
    hands = [hand(kind, PAIR_PROJ)]

    own_gi = gi_part(x)
    for i in range(blocks - 1):
        gi_copies[i].wait_recv()
        own_gi += gi_recv[i].astype(F32)
    gi_bf[...] = own_gi.astype(BF16)
    gi_out = local(gi_bf, gi_ref.at[0], 6)

    wholes[0].wait_recv()
    hands.append(hand((kind + CLASSES - 1) % CLASSES, PAIR_PROJ + 1))
    wholes[1].wait_recv()
    hands.append(hand((kind + 1) % CLASSES, PAIR_PROJ + 2))
    for copy in dec_copies:
        copy.wait_recv()
    part = y_dec[0]
    for j in range(1, batches):
        part += y_dec[j]
    pair_dec[c] = part
    dec_pair = remote(pair_dec.at[c], pair_dec.at[c], pair_send.at[PAIR_DECAY], pair_recv.at[PAIR_DECAY], partner)
    dec_pair.start()
    dec_pair.wait_recv()
    gd_own[...] = (pair_dec[0] + pair_dec[1]) / (batches * seqs * steps)
    gd_out = local(gd_own, gd_ref, 13)

    for copy in halves + hands:
        copy.wait_recv()

    for copy in cot_ring + cot_on + inp_ring + inp_on + turned + gi_copies + dec_copies:
        copy.wait_send()
    for copy in (sum_all, adj_pair, dec_pair, *g_copies.values(), *members, *halves, *wholes, *hands):
        copy.wait_send()
    z_all(z_dec, DECAY).wait_send()
    for copy in (gi_out, gd_out, *gp_outs):
        copy.wait()


def hand_out(gi_in, gp_in, gd_in, gi_out, gp_out, gd_out, gi, gp, gd, wide, sems):
    parts = [(gp_in.at[k], gp.at[k], wide.at[k], gp_out.at[k]) for k in range(2)]
    parts += [(gi_in, gi, gi, gi_out), (gd_in, gd, gd, gd_out)]
    come = [pltpu.make_async_copy(part[0], part[1], sems.at[0, i]) for i, part in enumerate(parts)]
    go = [pltpu.make_async_copy(part[2], part[3], sems.at[1, i]) for i, part in enumerate(parts)]
    for copy in come:
        copy.start()
    for i in range(len(parts)):
        come[i].wait()
        if i < 2:
            wide[i] = gp[i].astype(F32)
        go[i].start()
    for copy in go:
        copy.wait()


def local(sizes, inputs, cotangent, step_size, resets, log_decay, in_proj, out_proj, saved_states, saved_index):
    seqs, batches, blocks = sizes
    chips = seqs // 2
    _, steps, width = inputs.shape
    _, features, states = in_proj.shape
    rows = features // batches
    piece = rows // CLASSES
    hbm_spec = pl.BlockSpec(memory_space=pltpu.HBM)
    per_step = pltpu.VMEM((steps, states), F32)
    dma = pltpu.SemaphoreType.DMA
    grad_inputs, grad_proj, grad_decay = pl.pallas_call(
        functools.partial(kernel, sizes),
        out_shape=(
            jax.ShapeDtypeStruct((1, steps, width), BF16),
            jax.ShapeDtypeStruct((2, CLASSES, piece, states), BF16),
            jax.ShapeDtypeStruct((2, states), F32),
        ),
        in_specs=[hbm_spec] * 9,
        out_specs=(hbm_spec, hbm_spec, hbm_spec),
        scratch_shapes=[
            pltpu.VMEM((blocks, steps, width), BF16),
            pltpu.VMEM((blocks, steps, width), BF16),
            pltpu.VMEM((features, 2 * states), BF16),
            pltpu.VMEM((features, 2 * states), BF16),
            pltpu.VMEM((features, 2 * steps), BF16),
            *([per_step] * 13),
            pltpu.VMEM((steps, 2 * states), BF16),
            pltpu.VMEM((steps, states), BF16),
            pltpu.VMEM((2 * steps, states), BF16),
            pltpu.VMEM((seqs, 4, states), F32),
            pltpu.VMEM((blocks - 1, steps, width), BF16),
            pltpu.VMEM((blocks - 1, steps, width), BF16),
            pltpu.VMEM((steps, width), BF16),
            pltpu.VMEM((batches, rows, states), BF16),
            pltpu.VMEM((batches, 3, piece, states), BF16),
            pltpu.VMEM((batches, 2, piece // 2, states), BF16),
            pltpu.VMEM((rows, states), F32),
            pltpu.VMEM((chips // CLASSES, piece, states), BF16),
            pltpu.VMEM((2, CLASSES, piece, states), BF16),
            pltpu.VMEM((chips, 2, states), F32),
            pltpu.VMEM((batches, 2, states), F32),
            pltpu.VMEM((2, 2, states), F32),
            pltpu.VMEM(step_size.shape, F32),
            pltpu.VMEM(resets.shape, jnp.int32),
            pltpu.VMEM(log_decay.shape, F32),
            pltpu.VMEM(saved_states.shape, F32),
            pltpu.SMEM(saved_index.shape, jnp.int32),
            pltpu.VMEM((2, states), F32),
            pltpu.SemaphoreType.REGULAR((4,)),
            dma((18,)),
            dma((2, 6)),
            dma((2, 6)),
            dma((PAIR_INPUTS + blocks,)),
            dma((PAIR_INPUTS + blocks,)),
            dma((2,)),
            dma((2,)),
            dma((batches, 5)),
            dma((batches, 5)),
            dma((chips // CLASSES,)),
            dma((chips // CLASSES,)),
            dma((6,)),
            dma((6,)),
            dma((batches - 1,)),
            dma((batches - 1,)),
            dma((blocks - 1,)),
            dma((blocks - 1,)),
        ],
        compiler_params=pltpu.CompilerParams(
            collective_id=0, has_side_effects=True, vmem_limit_bytes=60 * 1024 * 1024
        ),
    )(cotangent, inputs, step_size, resets, log_decay, in_proj, out_proj, saved_states, saved_index)
    results = (grad_inputs, grad_proj.reshape(2, rows, states), grad_decay)
    return pl.pallas_call(
        hand_out,
        out_shape=[
            jax.ShapeDtypeStruct(grad_inputs.shape, BF16),
            jax.ShapeDtypeStruct((2, rows, states), F32),
            jax.ShapeDtypeStruct(grad_decay.shape, F32),
        ],
        in_specs=[hbm_spec] * 3,
        out_specs=[hbm_spec] * 3,
        scratch_shapes=[
            *(pltpu.VMEM(part.shape, part.dtype) for part in results),
            pltpu.VMEM((2, rows, states), F32),
            dma((2, 4)),
        ],
        compiler_params=pltpu.CompilerParams(vmem_limit_bytes=60 * 1024 * 1024),
    )(*results)


def solution(mesh):
    in_specs = (
        P("batch", "seq", "state"),
        P("batch", "seq", "state"),
        P("batch", "seq"),
        P("batch", "seq"),
        P(None, "state"),
        P(None, None, "state"),
        P(None, None, "state"),
        P("batch", "seq", None, "state"),
        P("batch", "seq"),
    )
    out_specs = (P("batch", "seq", "state"), P(None, "batch", "state"), P(None, "state"))
    sizes = (mesh.shape["seq"], mesh.shape["batch"], mesh.shape["state"])
    return jax.shard_map(
        functools.partial(local, sizes), mesh=mesh, in_specs=in_specs, out_specs=out_specs, check_vma=False
    )
```

```python
import functools
import math

import jax
import jax.numpy as jnp
from jax import lax
from jax.experimental import pallas as pl
from jax.experimental.pallas import tpu as pltpu
from jax.sharding import PartitionSpec as P

MESH = pl.DeviceIdType.MESH
F32 = jnp.float32
BF16 = jnp.bfloat16
GROUPS = 8
CLASSES = 4
SUMMARY, DECAY = range(2)
PAIR_DECAY, PAIR_STEPS, PAIR_PROJ = 0, 1, 6
PAIR_INPUTS = PAIR_PROJ + 3


def complex_times(left_re, left_im, right_re, right_im):
    return (left_re * right_re - left_im * right_im, left_re * right_im + left_im * right_re)


def conj_times(left_re, left_im, right_re, right_im):
    return (left_re * right_re + left_im * right_im, left_re * right_im - left_im * right_re)


def dot(left, right, left_dim, right_dim):
    return lax.dot_general(
        left, right, (((left_dim,), (right_dim,)), ((), ())), preferred_element_type=F32
    )


def small_exp(x):
    total = jnp.full_like(x, 1.0 / 5040.0)
    for factor in (1.0 / 720.0, 1.0 / 120.0, 1.0 / 24.0, 1.0 / 6.0, 0.5):
        total = total * x + factor
    near = 1.0 + (x + x * x * total)
    return jnp.where(x > -0.4, near, jnp.exp(x))


def cos_sin(angle):
    turns = jnp.floor(angle * (2.0 / math.pi) + 0.5)
    rest = angle - turns * 1.5703125
    rest = rest - turns * 4.837512969970703125e-4
    rest = rest - turns * 7.54978995489188216e-8
    square = rest * rest
    sine = ((-1.9515295891e-4 * square + 8.3321608736e-3) * square - 1.6666654611e-1) * square
    sine = sine * rest + rest
    cosine = (2.443315711809948e-5 * square - 1.388731625493765e-3) * square + 4.166664568298827e-2
    cosine = cosine * square * square - 0.5 * square + 1.0
    half = jnp.floor(turns * 0.5)
    odd = turns - 2.0 * half
    negative = half - 2.0 * jnp.floor(half * 0.5)
    sign = 1.0 - 2.0 * negative
    swap = odd > 0.5
    return (
        sign * jnp.where(swap, -sine, cosine),
        sign * jnp.where(swap, cosine, sine),
    )


def column(row):
    steps = row.shape[1]
    return jnp.concatenate(
        [
            jnp.broadcast_to(row[:, at : at + 128], (128, 128)).T
            for at in range(0, steps, 128)
        ],
        axis=0,
    )


def kernel(
    sizes,
    cot_ref,
    inp_ref,
    step_hbm,
    resets_hbm,
    rate_hbm,
    w_in_ref,
    w_out_ref,
    saved_hbm,
    index_hbm,
    gi_ref,
    gp_ref,
    gd_ref,
    cot_all,
    inp_all,
    w_in,
    w_out,
    inp_t,
    dec_re,
    dec_im,
    step_col,
    inj_re,
    inj_im,
    drv_re,
    drv_im,
    adj_re,
    adj_im,
    left_re,
    left_im,
    pri_re,
    pri_im,
    adj_bf,
    other_adj,
    other_dec_re,
    other_dec_im,
    other_inj_re,
    other_inj_im,
    grp_own,
    grp_other,
    adj_cat,
    z_sum,
    gi_send,
    gi_recv,
    gi_bf,
    g_send,
    g_full,
    g_half,
    z_own,
    z_mem,
    gp_bf,
    z_dec,
    y_dec,
    pair_dec,
    step_ref,
    resets_ref,
    rate_ref,
    saved_ref,
    index_ref,
    gd_own,
    known_sem,
    local_sem,
    ring_send,
    ring_recv,
    pair_send,
    pair_recv,
    zs_send,
    zs_recv,
    gs_send,
    gs_recv,
    zm_send,
    zm_recv,
    sp_send,
    sp_recv,
    yd_send,
    yd_recv,
    gi_ssem,
    gi_rsem,
):
    seqs, batches, blocks = sizes
    chips = seqs // 2
    steps, width = cot_all.shape[1], cot_all.shape[2]
    half = steps // 2
    length = steps // GROUPS
    states = dec_re.shape[1]
    piece = z_mem.shape[1]
    s, b, x = lax.axis_index("seq"), lax.axis_index("batch"), lax.axis_index("state")
    z, c = s // 2, s % 2
    partner = {"seq": 2 * z + (1 - c)}
    right, left = (x + 1) % blocks, (x + blocks - 1) % blocks
    across = (x + 2) % blocks

    def chip(offset, core=c):
        return {"seq": 2 * ((z + offset) % chips) + core}

    def row(offset):
        return {"batch": (b + offset) % batches}

    def block(offset):
        return {"state": (x + offset) % blocks}

    def remote(src, dst, send, recv, device):
        return pltpu.make_async_remote_copy(
            src_ref=src, dst_ref=dst, send_sem=send, recv_sem=recv, device_id=device, device_id_type=MESH
        )

    barrier = pltpu.get_barrier_semaphore()
    peers = [partner]
    peers += [block(i) for i in range(1, blocks)]
    peers += [row(i) for i in range(1, batches)]
    peers += [chip(offset, core) for offset in (1, chips - 1) for core in (c, 1 - c)]

    def greet(semaphore, devices):
        for device in devices:
            pl.semaphore_signal(semaphore, inc=1, device_id=device, device_id_type=MESH)

    greet(barrier, peers)

    rounds = [1 << i for i in range(chips.bit_length() - 2)]

    def round_start(at):
        if at < len(rounds):
            both = (rounds[at], chips - rounds[at])
            greet(known_sem.at[at], [chip(offset, core) for offset in both for core in (c, 1 - c)])

    def round_end(at):
        if at < len(rounds):
            pl.semaphore_wait(known_sem.at[at], 4)

    def local(src, dst, at):
        copy = pltpu.make_async_copy(src, dst, local_sem.at[at])
        copy.start()
        return copy

    cot_own = local(cot_ref.at[0], cot_all.at[x], 0)
    out_copies = [local(w_out_ref.at[k], w_out.at[:, pl.ds(k * states, states)], 1 + k) for k in range(2)]
    pl.semaphore_wait(barrier, len(peers))
    round_start(0)

    low, high = pl.ds(0, half), pl.ds(half, half)

    def ring(ref, whole, at):
        def send(part, device, sem):
            copy = remote(
                ref.at[0, part], whole.at[x, part], ring_send.at[at, sem], ring_recv.at[at, sem], device
            )
            copy.start()
            return copy

        return [
            send(low, block(1), 0),
            send(high, block(blocks - 1), 1),
            send(high, block(1), 2),
            send(low, block(blocks - 1), 3),
        ]

    def forward(whole, at, way):
        owner, part, device = ((left, low, block(1)), (right, high, block(blocks - 1)))[way]
        copy = remote(
            whole.at[owner, part], whole.at[owner, part], ring_send.at[at, 4 + way], ring_recv.at[at, 4 + way], device
        )
        copy.start()
        return copy

    cot_ring = ring(cot_ref, cot_all, 0)
    inp_own = local(inp_ref.at[0], inp_all.at[x], 3)
    small = ((step_hbm, step_ref), (resets_hbm, resets_ref), (rate_hbm, rate_ref))
    small_copies = [local(*pair, 8 + k) for k, pair in enumerate(small)]
    saved_copies = [local(saved_hbm, saved_ref, 11), local(index_hbm, index_ref, 12)]
    in_copies = [local(w_in_ref.at[k], w_in.at[:, pl.ds(k * states, states)], 4 + k) for k in range(2)]

    for copy in small_copies:
        copy.wait()
    step = step_ref[...]
    keep = (1 - resets_ref[...]).astype(F32)
    wide = column(step)
    magnitude = column(keep) * small_exp(wide * rate_ref[0:1, :])
    cosine, sine = cos_sin(wide * rate_ref[1:2, :])
    dec_re[...] = magnitude * cosine
    dec_im[...] = magnitude * sine
    step_col[...] = wide

    def share(src, dst, at):
        copy = remote(src, dst, pair_send.at[PAIR_STEPS + at], pair_recv.at[PAIR_STEPS + at], partner)
        copy.start()
        return copy

    shared = [share(dec_re, other_dec_re, 0), share(dec_im, other_dec_im, 1)]

    def part_dot(whole, weights, owner):
        return dot(whole[owner], weights[pl.ds(pl.multiple_of(owner * width, width), width), :], 1, 0)

    cot_own.wait()
    for copy in out_copies:
        copy.wait()
    round_end(0)
    round_start(1)
    inject = part_dot(cot_all, w_out, x)
    cot_ring[0].wait_recv()
    cot_on = [forward(cot_all, 0, 0)]
    cot_ring[1].wait_recv()
    cot_on.append(forward(cot_all, 0, 1))
    round_end(1)
    round_start(2)
    inp_ring = ring(inp_ref, inp_all, 1)
    cot_ring[2].wait_recv()
    inject += part_dot(cot_all, w_out, left)
    cot_ring[3].wait_recv()
    inject += part_dot(cot_all, w_out, right)
    round_end(2)
    greet(known_sem.at[3], [row(i) for i in range(1, batches)])
    for copy in cot_on:
        copy.wait_recv()
    inject += part_dot(cot_all, w_out, across)
    inj_re[...] = inject[:, :states]
    inj_im[...] = -inject[:, states:]
    shared += [share(inj_re, other_inj_re, 2), share(inj_im, other_inj_im, 3)]

    def at_step(j):
        return pl.ds(j, GROUPS, stride=length)

    zero8 = jnp.zeros((GROUPS, states), F32)
    one8 = jnp.ones((GROUPS, states), F32)

    def leave(i, carry):
        prod_re, prod_im, sum_re, sum_im = carry
        at = at_step(length - 1 - i)
        d_re, d_im = dec_re[at, :], dec_im[at, :]
        prod_re, prod_im = conj_times(d_re, d_im, prod_re, prod_im)
        sum_re, sum_im = conj_times(d_re, d_im, inj_re[at, :] + sum_re, inj_im[at, :] + sum_im)
        return prod_re, prod_im, sum_re, sum_im

    grp = lax.fori_loop(0, length, leave, (one8, zero8, zero8, zero8), unroll=True)

    def pass_on(prod_re, prod_im, sum_re, sum_im, at_re, at_im):
        move_re, move_im = complex_times(prod_re, prod_im, at_re, at_im)
        return move_re + sum_re, move_im + sum_im

    def compose(first, then):
        prod_re, prod_im = complex_times(then[0], then[1], first[0], first[1])
        sum_re, sum_im = pass_on(*then, first[2], first[3])
        return prod_re, prod_im, sum_re, sum_im

    grp_rows = [tuple(part[g : g + 1, :] for part in grp) for g in range(GROUPS)]
    own = grp_rows[GROUPS - 1]
    for g in range(GROUPS - 2, -1, -1):
        own = compose(own, grp_rows[g])
    z_sum[s] = jnp.concatenate(own, axis=0)
    for k in range(4):
        grp_own[k] = grp[k]

    def four(ref, at):
        return tuple(ref[at, k : k + 1, :] for k in range(4))

    def far_first(k):
        return chips // 2 + (k // 2) * (1 - 2 * (k % 2))

    def sum_start(k, carry):
        for core in range(2):
            remote(
                z_sum.at[s], z_sum.at[s], zs_send.at[SUMMARY], zs_recv.at[SUMMARY], chip(far_first(k), core)
            ).start()
        return carry

    lax.fori_loop(1, chips, sum_start, 0)
    remote(z_sum.at[s], z_sum.at[s], zs_send.at[SUMMARY], zs_recv.at[SUMMARY], partner).start()
    shared.append(share(grp_own, grp_other, 4))
    sum_part = z_sum.at[pl.ds(0, seqs - 1)]
    sum_all = remote(sum_part, sum_part, zs_send.at[SUMMARY], zs_recv.at[SUMMARY], partner)

    def z_start(src, dst, kind):
        def go(k, carry):
            i = far_first(k)
            remote(src(i), dst, zs_send.at[kind], zs_recv.at[kind], chip(i)).start()
            return carry

        lax.fori_loop(1, chips, go, 0)

    def z_all(buffer, kind):
        part = buffer.at[pl.ds(0, chips - 1)]
        return remote(part, part, zs_send.at[kind], zs_recv.at[kind], chip(1))

    inp_ring[0].wait_recv()
    inp_on = [forward(inp_all, 1, 0)]
    inp_ring[1].wait_recv()
    inp_on.append(forward(inp_all, 1, 1))
    inp_own.wait()
    for copy in in_copies:
        copy.wait()
    drive = part_dot(inp_all, w_in, x)

    columns = pl.ds(pl.multiple_of(c * steps, steps), steps)

    def turn(owner, at):
        there = inp_t.at[pl.ds(pl.multiple_of(owner * width, width), width), columns]
        there[...] = inp_all[owner].T
        copy = remote(there, there, pair_send.at[PAIR_INPUTS + at], pair_recv.at[PAIR_INPUTS + at], partner)
        copy.start()
        return copy

    turned = [turn(x, 0)]
    inp_ring[2].wait_recv()
    turned.append(turn(left, 1))
    drive += part_dot(inp_all, w_in, left)
    inp_ring[3].wait_recv()
    turned.append(turn(right, 2))
    drive += part_dot(inp_all, w_in, right)
    for copy in inp_on:
        copy.wait_recv()
    turned.append(turn(across, 3))

    sum_all.wait_recv()
    end = 2 * z + 1
    in_re, in_im = jnp.zeros((1, states), F32), jnp.zeros((1, states), F32)
    for j in range(seqs - 1, 1, -1):
        next_re, next_im = pass_on(*four(z_sum, j), in_re, in_im)
        in_re, in_im = jnp.where(j > end, next_re, in_re), jnp.where(j > end, next_im, in_im)
    mid_re, mid_im = pass_on(*four(z_sum, end), in_re, in_im)
    is_first = c == 0

    def enter(rows, at_re, at_im):
        found = [None] * GROUPS
        for g in range(GROUPS - 1, -1, -1):
            found[g] = (at_re, at_im)
            at_re, at_im = pass_on(*rows[g], at_re, at_im)
        return tuple(jnp.concatenate([pair[k] for pair in found], axis=0) for k in range(2))

    for copy in shared:
        copy.wait_recv()
    other_rows = [tuple(grp_other[k, g : g + 1, :] for k in range(4)) for g in range(GROUPS)]
    own_enter = enter(grp_rows, jnp.where(is_first, mid_re, in_re), jnp.where(is_first, mid_im, in_im))
    other_enter = enter(other_rows, jnp.where(is_first, in_re, mid_re), jnp.where(is_first, in_im, mid_im))
    first8 = (jnp.zeros((GROUPS, states), jnp.int32) + c) == 0

    def back(i, carry):
        at = at_step(length - 1 - i)
        a_re, a_im = inj_re[at, :] + carry[0], inj_im[at, :] + carry[1]
        adj_re[at, :] = a_re
        adj_im[at, :] = a_im
        l_re, l_im = conj_times(dec_re[at, :], dec_im[at, :], a_re, a_im)
        left_re[at, :] = l_re
        left_im[at, :] = l_im
        o_re, o_im = other_inj_re[at, :] + carry[2], other_inj_im[at, :] + carry[3]
        other_adj[at, :] = jnp.where(first8, o_re, o_im)
        return (l_re, l_im, *conj_times(other_dec_re[at, :], other_dec_im[at, :], o_re, o_im))

    lax.fori_loop(0, length, back, (*own_enter, *other_enter), unroll=True)
    bf_re, bf_im = adj_re[...].astype(BF16), adj_im[...].astype(BF16)
    first = (jnp.zeros((steps, states), jnp.int32) + c) == 0
    own_rows = pl.ds(pl.multiple_of(c * steps, steps), steps)
    adj_cat[own_rows, :] = jnp.where(first, adj_re[...], adj_im[...]).astype(BF16)
    other_steps = pl.ds(pl.multiple_of((1 - c) * steps, steps), steps)
    adj_cat[other_steps, :] = other_adj[...].astype(BF16)
    adj_bf[:, :states] = bf_re
    adj_bf[:, states:] = bf_im

    pl.semaphore_wait(known_sem.at[3], batches - 1)
    kind = z % CLASSES
    around = (2, -2, 1, -1, 0)

    def class_rows(of, at):
        start = of * piece + (piece // 2 if at == -2 else 0)
        size = piece // 2 if abs(at) == 2 else piece
        return pl.ds(pl.multiple_of(start, size), size)

    def near_copy(offset, at):
        src = g_send.at[offset, class_rows((z + at + chips) % CLASSES, at)]
        place = around.index(at)
        dst = g_half.at[offset, place] if abs(at) == 2 else g_full.at[offset, place - 2]
        device = {"seq": 2 * ((z + at + chips) % chips) + c, "batch": (b + offset) % batches}
        return remote(src, dst, gs_send.at[offset, place], gs_recv.at[offset, place], device)

    for copy in turned:
        copy.wait_recv()
    for place, offset in enumerate((2, 1, 3, 0)):
        owner = (b + offset) % batches
        here = pl.ds(pl.multiple_of(owner * width, width), width)
        part = dot(inp_t[here, :], adj_cat[...], 1, 0)
        g_send[offset] = part.astype(BF16)
        for distance in around[:-1]:
            near_copy(offset, distance).start()

        if place == 3:
            z_own[...] = part
        else:
            near_copy(offset, 0).start()

    g_copies = {
        (offset, distance): near_copy(offset, distance)
        for offset in range(batches)
        for distance in around
        if offset or distance
    }

    def gi_part(owner):
        return dot(adj_bf[...], w_in[pl.ds(pl.multiple_of(owner * width, width), width), :], 1, 1)

    gi_copies = []
    for i in range(1, blocks):
        gi_send[i - 1] = gi_part((x + i) % blocks).astype(BF16)
        copy = remote(gi_send.at[i - 1], gi_recv.at[i - 1], gi_ssem.at[i - 1], gi_rsem.at[i - 1], block(i))
        copy.start()
        gi_copies.append(copy)

    drive += part_dot(inp_all, w_in, across)
    drv_re[...] = drive[:, :states]
    drv_im[...] = drive[:, states:]

    def run(i, carry):
        prod_re, prod_im, sum_re, sum_im = carry
        at = at_step(i)
        d_re, d_im = dec_re[at, :], dec_im[at, :]
        prod_re, prod_im = complex_times(d_re, d_im, prod_re, prod_im)
        sum_re, sum_im = pass_on(d_re, d_im, drv_re[at, :], drv_im[at, :], sum_re, sum_im)
        return prod_re, prod_im, sum_re, sum_im

    fwd = lax.fori_loop(0, length, run, (one8, zero8, zero8, zero8), unroll=True)
    fwd_rows = [tuple(part[g : g + 1, :] for part in fwd) for g in range(GROUPS)]
    for copy in saved_copies:
        copy.wait()
    spans = saved_ref.shape[1]
    begin = [None] * GROUPS
    for span in range(spans):
        slot = jnp.zeros((1, states), jnp.int32) + index_ref[0, span]
        at_re, at_im = jnp.zeros((1, states), F32), jnp.zeros((1, states), F32)
        for k in range(spans):
            at_re = jnp.where(slot == k, saved_ref[0, k, 0:1, :], at_re)
            at_im = jnp.where(slot == k, saved_ref[0, k, 1:2, :], at_im)
        for g in range(span * GROUPS // spans, (span + 1) * GROUPS // spans):
            begin[g] = (at_re, at_im)
            at_re, at_im = pass_on(*fwd_rows[g], at_re, at_im)

    def rerun(i, carry):
        at = at_step(i)
        pri_re[at, :] = carry[0]
        pri_im[at, :] = carry[1]
        return pass_on(dec_re[at, :], dec_im[at, :], drv_re[at, :], drv_im[at, :], *carry)

    lax.fori_loop(
        0,
        length,
        rerun,
        tuple(jnp.concatenate([pair[k] for pair in begin], axis=0) for k in range(2)),
        unroll=True,
    )
    wide_re, wide_im = conj_times(pri_re[...], pri_im[...], left_re[...], left_im[...])
    weight = step_col[...]
    z_dec[z] = jnp.concatenate(
        [jnp.sum(weight * part, axis=0, keepdims=True) for part in (wide_re, wide_im)], axis=0
    )
    z_start(lambda i: z_dec.at[z], z_dec.at[z], DECAY)

    for copy in g_copies.values():
        copy.wait_recv()
    total = z_own[class_rows(kind, 0), :]
    for offset in range(batches):
        if offset:
            total += g_full[offset, 2].astype(F32)
        total += g_full[offset, 0].astype(F32) + g_full[offset, 1].astype(F32)
        total += jnp.concatenate([g_half[offset, 0], g_half[offset, 1]], axis=0).astype(F32)
    z_mem[z // CLASSES] = total.astype(BF16)
    member = z_mem.at[z // CLASSES]
    members = []
    for i in range(chips // CLASSES - 1):
        copy = remote(member, member, zm_send.at[i], zm_recv.at[i], chip(CLASSES * (i + 1)))
        copy.start()
        members.append(copy)

    z_all(z_dec, DECAY).wait_recv()
    part = z_dec[0]
    for j in range(1, chips):
        part += z_dec[j]
    y_dec[b] = part
    dec_copies = []
    for i in range(1, batches):
        copy = remote(y_dec.at[b], y_dec.at[b], yd_send.at[i - 1], yd_recv.at[i - 1], row(i))
        copy.start()
        dec_copies.append(copy)

    for copy in members:
        copy.wait_recv()
    total = z_mem[0].astype(F32)
    for i in range(1, chips // CLASSES):
        total += z_mem[i].astype(F32)
    scale = 1.0 / math.sqrt(batches * seqs * steps)
    gp_bf[c, kind] = (total * scale).astype(BF16)

    def spread(at, core, place):
        rows_of = pl.ds(piece // 2 if at == -2 else 0, piece // 2 if abs(at) == 2 else piece)
        there = gp_ref if abs(at) == 2 else gp_bf
        mine, target = gp_bf.at[c, kind, rows_of], there.at[c, kind, rows_of]
        copy = remote(mine, target, sp_send.at[place], sp_recv.at[place], chip(at + chips, core))
        copy.start()
        return copy

    def hand(of, place):
        gp_outs.append(local(gp_bf.at[c, of], gp_ref.at[c, of], 15 + place - PAIR_PROJ))
        copy = remote(gp_bf.at[c, of], gp_ref.at[c, of], pair_send.at[place], pair_recv.at[place], partner)
        copy.start()
        return copy

    gp_outs = []
    wholes = [spread(1, c, 4), spread(-1, c, 5)]
    halves = [spread(at, core, place) for place, (at, core) in enumerate(((2, c), (-2, c), (2, 1 - c), (-2, 1 - c)))]
    hands = [hand(kind, PAIR_PROJ)]

    own_gi = gi_part(x)
    for i in range(blocks - 1):
        gi_copies[i].wait_recv()
        own_gi += gi_recv[i].astype(F32)
    gi_bf[...] = own_gi.astype(BF16)
    gi_out = local(gi_bf, gi_ref.at[0], 6)

    wholes[0].wait_recv()
    hands.append(hand((kind + CLASSES - 1) % CLASSES, PAIR_PROJ + 1))
    wholes[1].wait_recv()
    hands.append(hand((kind + 1) % CLASSES, PAIR_PROJ + 2))
    for copy in dec_copies:
        copy.wait_recv()
    part = y_dec[0]
    for j in range(1, batches):
        part += y_dec[j]
    pair_dec[c] = part
    dec_pair = remote(pair_dec.at[c], pair_dec.at[c], pair_send.at[PAIR_DECAY], pair_recv.at[PAIR_DECAY], partner)
    dec_pair.start()
    dec_pair.wait_recv()
    gd_own[...] = (pair_dec[0] + pair_dec[1]) / (batches * seqs * steps)
    gd_out = local(gd_own, gd_ref, 13)

    for copy in halves + hands:
        copy.wait_recv()

    for copy in cot_ring + cot_on + inp_ring + inp_on + turned + gi_copies + dec_copies:
        copy.wait_send()
    for copy in (sum_all, dec_pair, *shared, *g_copies.values(), *members, *halves, *wholes, *hands):
        copy.wait_send()
    z_all(z_dec, DECAY).wait_send()
    for copy in (gi_out, gd_out, *gp_outs):
        copy.wait()


def hand_out(gi_in, gp_in, gd_in, gi_out, gp_out, gd_out, gi, gp, gd, wide, sems):
    parts = [(gp_in.at[k], gp.at[k], wide.at[k], gp_out.at[k]) for k in range(2)]
    parts += [(gi_in, gi, gi, gi_out), (gd_in, gd, gd, gd_out)]
    come = [pltpu.make_async_copy(part[0], part[1], sems.at[0, i]) for i, part in enumerate(parts)]
    go = [pltpu.make_async_copy(part[2], part[3], sems.at[1, i]) for i, part in enumerate(parts)]
    for copy in come:
        copy.start()
    for i in range(len(parts)):
        come[i].wait()
        if i < 2:
            wide[i] = gp[i].astype(F32)
        go[i].start()
    for copy in go:
        copy.wait()


def local(sizes, inputs, cotangent, step_size, resets, log_decay, in_proj, out_proj, saved_states, saved_index):
    seqs, batches, blocks = sizes
    chips = seqs // 2
    _, steps, width = inputs.shape
    _, features, states = in_proj.shape
    rows = features // batches
    piece = rows // CLASSES
    hbm_spec = pl.BlockSpec(memory_space=pltpu.HBM)
    per_step = pltpu.VMEM((steps, states), F32)
    dma = pltpu.SemaphoreType.DMA
    grad_inputs, grad_proj, grad_decay = pl.pallas_call(
        functools.partial(kernel, sizes),
        out_shape=(
            jax.ShapeDtypeStruct((1, steps, width), BF16),
            jax.ShapeDtypeStruct((2, CLASSES, piece, states), BF16),
            jax.ShapeDtypeStruct((2, states), F32),
        ),
        in_specs=[hbm_spec] * 9,
        out_specs=(hbm_spec, hbm_spec, hbm_spec),
        scratch_shapes=[
            pltpu.VMEM((blocks, steps, width), BF16),
            pltpu.VMEM((blocks, steps, width), BF16),
            pltpu.VMEM((features, 2 * states), BF16),
            pltpu.VMEM((features, 2 * states), BF16),
            pltpu.VMEM((features, 2 * steps), BF16),
            *([per_step] * 13),
            pltpu.VMEM((steps, 2 * states), BF16),
            *([per_step] * 5),
            pltpu.VMEM((4, GROUPS, states), F32),
            pltpu.VMEM((4, GROUPS, states), F32),
            pltpu.VMEM((2 * steps, states), BF16),
            pltpu.VMEM((seqs, 4, states), F32),
            pltpu.VMEM((blocks - 1, steps, width), BF16),
            pltpu.VMEM((blocks - 1, steps, width), BF16),
            pltpu.VMEM((steps, width), BF16),
            pltpu.VMEM((batches, rows, states), BF16),
            pltpu.VMEM((batches, 3, piece, states), BF16),
            pltpu.VMEM((batches, 2, piece // 2, states), BF16),
            pltpu.VMEM((rows, states), F32),
            pltpu.VMEM((chips // CLASSES, piece, states), BF16),
            pltpu.VMEM((2, CLASSES, piece, states), BF16),
            pltpu.VMEM((chips, 2, states), F32),
            pltpu.VMEM((batches, 2, states), F32),
            pltpu.VMEM((2, 2, states), F32),
            pltpu.VMEM(step_size.shape, F32),
            pltpu.VMEM(resets.shape, jnp.int32),
            pltpu.VMEM(log_decay.shape, F32),
            pltpu.VMEM(saved_states.shape, F32),
            pltpu.SMEM(saved_index.shape, jnp.int32),
            pltpu.VMEM((2, states), F32),
            pltpu.SemaphoreType.REGULAR((4,)),
            dma((18,)),
            dma((2, 6)),
            dma((2, 6)),
            dma((PAIR_INPUTS + blocks,)),
            dma((PAIR_INPUTS + blocks,)),
            dma((2,)),
            dma((2,)),
            dma((batches, 5)),
            dma((batches, 5)),
            dma((chips // CLASSES,)),
            dma((chips // CLASSES,)),
            dma((6,)),
            dma((6,)),
            dma((batches - 1,)),
            dma((batches - 1,)),
            dma((blocks - 1,)),
            dma((blocks - 1,)),
        ],
        compiler_params=pltpu.CompilerParams(
            collective_id=0, has_side_effects=True, vmem_limit_bytes=60 * 1024 * 1024
        ),
    )(cotangent, inputs, step_size, resets, log_decay, in_proj, out_proj, saved_states, saved_index)
    results = (grad_inputs, grad_proj.reshape(2, rows, states), grad_decay)
    return pl.pallas_call(
        hand_out,
        out_shape=[
            jax.ShapeDtypeStruct(grad_inputs.shape, BF16),
            jax.ShapeDtypeStruct((2, rows, states), F32),
            jax.ShapeDtypeStruct(grad_decay.shape, F32),
        ],
        in_specs=[hbm_spec] * 3,
        out_specs=[hbm_spec] * 3,
        scratch_shapes=[
            *(pltpu.VMEM(part.shape, part.dtype) for part in results),
            pltpu.VMEM((2, rows, states), F32),
            dma((2, 4)),
        ],
        compiler_params=pltpu.CompilerParams(vmem_limit_bytes=60 * 1024 * 1024),
    )(*results)


def solution(mesh):
    in_specs = (
        P("batch", "seq", "state"),
        P("batch", "seq", "state"),
        P("batch", "seq"),
        P("batch", "seq"),
        P(None, "state"),
        P(None, None, "state"),
        P(None, None, "state"),
        P("batch", "seq", None, "state"),
        P("batch", "seq"),
    )
    out_specs = (P("batch", "seq", "state"), P(None, "batch", "state"), P(None, "state"))
    sizes = (mesh.shape["seq"], mesh.shape["batch"], mesh.shape["state"])
    return jax.shard_map(
        functools.partial(local, sizes), mesh=mesh, in_specs=in_specs, out_specs=out_specs, check_vma=False
    )
```

```python
import functools
import math

import jax
import jax.numpy as jnp
from jax import lax
from jax.experimental import pallas as pl
from jax.experimental.pallas import tpu as pltpu
from jax.sharding import PartitionSpec as P

MESH = pl.DeviceIdType.MESH
F32 = jnp.float32
BF16 = jnp.bfloat16
GROUPS = 8
CLASSES = 4
SUMMARY, DECAY = range(2)
PAIR_DECAY, PAIR_STEPS, PAIR_PROJ = 0, 1, 6
PAIR_INPUTS = PAIR_PROJ + 3


def complex_times(left_re, left_im, right_re, right_im):
    return (left_re * right_re - left_im * right_im, left_re * right_im + left_im * right_re)


def conj_times(left_re, left_im, right_re, right_im):
    return (left_re * right_re + left_im * right_im, left_re * right_im - left_im * right_re)


def dot(left, right, left_dim, right_dim):
    return lax.dot_general(
        left, right, (((left_dim,), (right_dim,)), ((), ())), preferred_element_type=F32
    )


def small_exp(x):
    total = jnp.full_like(x, 1.0 / 5040.0)
    for factor in (1.0 / 720.0, 1.0 / 120.0, 1.0 / 24.0, 1.0 / 6.0, 0.5):
        total = total * x + factor
    near = 1.0 + (x + x * x * total)
    return jnp.where(x > -0.4, near, jnp.exp(x))


def cos_sin(angle):
    turns = jnp.floor(angle * (2.0 / math.pi) + 0.5)
    rest = angle - turns * 1.5703125
    rest = rest - turns * 4.837512969970703125e-4
    rest = rest - turns * 7.54978995489188216e-8
    square = rest * rest
    sine = ((-1.9515295891e-4 * square + 8.3321608736e-3) * square - 1.6666654611e-1) * square
    sine = sine * rest + rest
    cosine = (2.443315711809948e-5 * square - 1.388731625493765e-3) * square + 4.166664568298827e-2
    cosine = cosine * square * square - 0.5 * square + 1.0
    half = jnp.floor(turns * 0.5)
    odd = turns - 2.0 * half
    negative = half - 2.0 * jnp.floor(half * 0.5)
    sign = 1.0 - 2.0 * negative
    swap = odd > 0.5
    return (
        sign * jnp.where(swap, -sine, cosine),
        sign * jnp.where(swap, cosine, sine),
    )


def column(row):
    steps = row.shape[1]
    return jnp.concatenate(
        [
            jnp.broadcast_to(row[:, at : at + 128], (128, 128)).T
            for at in range(0, steps, 128)
        ],
        axis=0,
    )


def kernel(
    sizes,
    cot_ref,
    inp_ref,
    step_hbm,
    resets_hbm,
    rate_hbm,
    w_in_ref,
    w_out_ref,
    saved_hbm,
    index_hbm,
    gi_ref,
    gp_ref,
    gd_ref,
    cot_all,
    inp_all,
    w_in,
    w_out,
    inp_t,
    dec_re,
    dec_im,
    step_col,
    inj_re,
    inj_im,
    drv_re,
    drv_im,
    adj_re,
    adj_im,
    left_re,
    left_im,
    pri_re,
    pri_im,
    adj_bf,
    other_adj,
    other_dec_re,
    other_dec_im,
    other_inj_re,
    other_inj_im,
    grp_own,
    grp_other,
    adj_cat,
    z_sum,
    gi_send,
    gi_recv,
    gi_bf,
    g_send,
    g_full,
    g_half,
    z_own,
    z_mem,
    gp_bf,
    z_dec,
    y_dec,
    pair_dec,
    step_ref,
    resets_ref,
    rate_ref,
    saved_ref,
    index_ref,
    gd_own,
    known_sem,
    local_sem,
    ring_send,
    ring_recv,
    pair_send,
    pair_recv,
    zs_send,
    zs_recv,
    gs_send,
    gs_recv,
    zm_send,
    zm_recv,
    sp_send,
    sp_recv,
    yd_send,
    yd_recv,
    gi_ssem,
    gi_rsem,
):
    seqs, batches, blocks = sizes
    chips = seqs // 2
    steps, width = cot_all.shape[1], cot_all.shape[2]
    half = steps // 2
    length = steps // GROUPS
    states = dec_re.shape[1]
    piece = z_mem.shape[1]
    s, b, x = lax.axis_index("seq"), lax.axis_index("batch"), lax.axis_index("state")
    z, c = s // 2, s % 2
    partner = {"seq": 2 * z + (1 - c)}
    right, left = (x + 1) % blocks, (x + blocks - 1) % blocks
    across = (x + 2) % blocks

    def chip(offset, core=c):
        return {"seq": 2 * ((z + offset) % chips) + core}

    def row(offset):
        return {"batch": (b + offset) % batches}

    def block(offset):
        return {"state": (x + offset) % blocks}

    def remote(src, dst, send, recv, device):
        return pltpu.make_async_remote_copy(
            src_ref=src, dst_ref=dst, send_sem=send, recv_sem=recv, device_id=device, device_id_type=MESH
        )

    barrier = pltpu.get_barrier_semaphore()
    peers = [partner]
    peers += [block(i) for i in range(1, blocks)]
    peers += [row(i) for i in range(1, batches)]
    peers += [chip(offset, core) for offset in (1, chips - 1) for core in (c, 1 - c)]

    def greet(semaphore, devices):
        for device in devices:
            pl.semaphore_signal(semaphore, inc=1, device_id=device, device_id_type=MESH)

    greet(barrier, peers)

    rounds = [1 << i for i in range(chips.bit_length() - 2)]

    def round_start(at):
        if at < len(rounds):
            both = (rounds[at], chips - rounds[at])
            greet(known_sem.at[at], [chip(offset, core) for offset in both for core in (c, 1 - c)])

    def round_end(at):
        if at < len(rounds):
            pl.semaphore_wait(known_sem.at[at], 4)

    def local(src, dst, at):
        copy = pltpu.make_async_copy(src, dst, local_sem.at[at])
        copy.start()
        return copy

    cot_own = local(cot_ref.at[0], cot_all.at[x], 0)
    out_copies = [local(w_out_ref.at[k], w_out.at[:, pl.ds(k * states, states)], 1 + k) for k in range(2)]
    pl.semaphore_wait(barrier, len(peers))
    round_start(0)

    low, high = pl.ds(0, half), pl.ds(half, half)

    def ring(ref, whole, at):
        def send(part, device, sem):
            copy = remote(
                ref.at[0, part], whole.at[x, part], ring_send.at[at, sem], ring_recv.at[at, sem], device
            )
            copy.start()
            return copy

        return [
            send(low, block(1), 0),
            send(high, block(blocks - 1), 1),
            send(high, block(1), 2),
            send(low, block(blocks - 1), 3),
        ]

    def forward(whole, at, way):
        owner, part, device = ((left, low, block(1)), (right, high, block(blocks - 1)))[way]
        copy = remote(
            whole.at[owner, part], whole.at[owner, part], ring_send.at[at, 4 + way], ring_recv.at[at, 4 + way], device
        )
        copy.start()
        return copy

    cot_ring = ring(cot_ref, cot_all, 0)
    inp_own = local(inp_ref.at[0], inp_all.at[x], 3)
    small = ((step_hbm, step_ref), (resets_hbm, resets_ref), (rate_hbm, rate_ref))
    small_copies = [local(*pair, 8 + k) for k, pair in enumerate(small)]
    saved_copies = [local(saved_hbm, saved_ref, 11), local(index_hbm, index_ref, 12)]
    in_copies = [local(w_in_ref.at[k], w_in.at[:, pl.ds(k * states, states)], 4 + k) for k in range(2)]

    for copy in small_copies:
        copy.wait()
    step = step_ref[...]
    keep = (1 - resets_ref[...]).astype(F32)
    wide = column(step)
    magnitude = column(keep) * small_exp(wide * rate_ref[0:1, :])
    cosine, sine = cos_sin(wide * rate_ref[1:2, :])
    dec_re[...] = magnitude * cosine
    dec_im[...] = magnitude * sine
    step_col[...] = wide

    def share(src, dst, at):
        copy = remote(src, dst, pair_send.at[PAIR_STEPS + at], pair_recv.at[PAIR_STEPS + at], partner)
        copy.start()
        return copy

    shared = [share(dec_re, other_dec_re, 0), share(dec_im, other_dec_im, 1)]

    def part_dot(whole, weights, owner):
        return dot(whole[owner], weights[pl.ds(pl.multiple_of(owner * width, width), width), :], 1, 0)

    cot_own.wait()
    for copy in out_copies:
        copy.wait()
    round_end(0)
    round_start(1)
    inject = part_dot(cot_all, w_out, x)
    cot_ring[0].wait_recv()
    cot_on = [forward(cot_all, 0, 0)]
    cot_ring[1].wait_recv()
    cot_on.append(forward(cot_all, 0, 1))
    round_end(1)
    round_start(2)
    inp_ring = ring(inp_ref, inp_all, 1)
    cot_ring[2].wait_recv()
    inject += part_dot(cot_all, w_out, left)
    cot_ring[3].wait_recv()
    inject += part_dot(cot_all, w_out, right)
    round_end(2)
    greet(known_sem.at[3], [row(i) for i in range(1, batches)])
    for copy in cot_on:
        copy.wait_recv()
    inject += part_dot(cot_all, w_out, across)
    inj_re[...] = inject[:, :states]
    inj_im[...] = -inject[:, states:]
    shared += [share(inj_re, other_inj_re, 2), share(inj_im, other_inj_im, 3)]

    def at_step(j):
        return pl.ds(j, GROUPS, stride=length)

    zero8 = jnp.zeros((GROUPS, states), F32)
    one8 = jnp.ones((GROUPS, states), F32)

    def leave(i, carry):
        prod_re, prod_im, sum_re, sum_im = carry
        at = at_step(length - 1 - i)
        d_re, d_im = dec_re[at, :], dec_im[at, :]
        prod_re, prod_im = conj_times(d_re, d_im, prod_re, prod_im)
        sum_re, sum_im = conj_times(d_re, d_im, inj_re[at, :] + sum_re, inj_im[at, :] + sum_im)
        return prod_re, prod_im, sum_re, sum_im

    grp = lax.fori_loop(0, length, leave, (one8, zero8, zero8, zero8), unroll=True)

    def pass_on(prod_re, prod_im, sum_re, sum_im, at_re, at_im):
        move_re, move_im = complex_times(prod_re, prod_im, at_re, at_im)
        return move_re + sum_re, move_im + sum_im

    def compose(first, then):
        prod_re, prod_im = complex_times(then[0], then[1], first[0], first[1])
        sum_re, sum_im = pass_on(*then, first[2], first[3])
        return prod_re, prod_im, sum_re, sum_im

    grp_rows = [tuple(part[g : g + 1, :] for part in grp) for g in range(GROUPS)]
    own = grp_rows[GROUPS - 1]
    for g in range(GROUPS - 2, -1, -1):
        own = compose(own, grp_rows[g])
    z_sum[s] = jnp.concatenate(own, axis=0)
    for k in range(4):
        grp_own[k] = grp[k]

    def four(ref, at):
        return tuple(ref[at, k : k + 1, :] for k in range(4))

    def far_first(k):
        return chips // 2 + (k // 2) * (1 - 2 * (k % 2))

    def sum_start(k, carry):
        for core in range(2):
            remote(
                z_sum.at[s], z_sum.at[s], zs_send.at[SUMMARY], zs_recv.at[SUMMARY], chip(far_first(k), core)
            ).start()
        return carry

    lax.fori_loop(1, chips, sum_start, 0)
    remote(z_sum.at[s], z_sum.at[s], zs_send.at[SUMMARY], zs_recv.at[SUMMARY], partner).start()
    shared.append(share(grp_own, grp_other, 4))
    sum_part = z_sum.at[pl.ds(0, seqs - 1)]
    sum_all = remote(sum_part, sum_part, zs_send.at[SUMMARY], zs_recv.at[SUMMARY], partner)

    def z_start(src, dst, kind):
        def go(k, carry):
            i = far_first(k)
            remote(src(i), dst, zs_send.at[kind], zs_recv.at[kind], chip(i)).start()
            return carry

        lax.fori_loop(1, chips, go, 0)

    def z_all(buffer, kind):
        part = buffer.at[pl.ds(0, chips - 1)]
        return remote(part, part, zs_send.at[kind], zs_recv.at[kind], chip(1))

    inp_ring[0].wait_recv()
    inp_on = [forward(inp_all, 1, 0)]
    inp_ring[1].wait_recv()
    inp_on.append(forward(inp_all, 1, 1))
    inp_own.wait()
    for copy in in_copies:
        copy.wait()
    drive = part_dot(inp_all, w_in, x)

    columns = pl.ds(pl.multiple_of(c * steps, steps), steps)

    def turn(owner, at):
        there = inp_t.at[pl.ds(pl.multiple_of(owner * width, width), width), columns]
        there[...] = inp_all[owner].T
        copy = remote(there, there, pair_send.at[PAIR_INPUTS + at], pair_recv.at[PAIR_INPUTS + at], partner)
        copy.start()
        return copy

    turned = [turn(x, 0)]
    inp_ring[2].wait_recv()
    turned.append(turn(left, 1))
    drive += part_dot(inp_all, w_in, left)
    inp_ring[3].wait_recv()
    turned.append(turn(right, 2))
    drive += part_dot(inp_all, w_in, right)
    for copy in inp_on:
        copy.wait_recv()
    turned.append(turn(across, 3))

    sum_all.wait_recv()
    end = 2 * z + 1
    in_re, in_im = jnp.zeros((1, states), F32), jnp.zeros((1, states), F32)
    for j in range(seqs - 1, 1, -1):
        next_re, next_im = pass_on(*four(z_sum, j), in_re, in_im)
        in_re, in_im = jnp.where(j > end, next_re, in_re), jnp.where(j > end, next_im, in_im)
    mid_re, mid_im = pass_on(*four(z_sum, end), in_re, in_im)
    is_first = c == 0

    def enter(rows, at_re, at_im):
        found = [None] * GROUPS
        for g in range(GROUPS - 1, -1, -1):
            found[g] = (at_re, at_im)
            at_re, at_im = pass_on(*rows[g], at_re, at_im)
        return tuple(jnp.concatenate([pair[k] for pair in found], axis=0) for k in range(2))

    for copy in shared:
        copy.wait_recv()
    other_rows = [tuple(grp_other[k, g : g + 1, :] for k in range(4)) for g in range(GROUPS)]
    own_enter = enter(grp_rows, jnp.where(is_first, mid_re, in_re), jnp.where(is_first, mid_im, in_im))
    other_enter = enter(other_rows, jnp.where(is_first, in_re, mid_re), jnp.where(is_first, in_im, mid_im))
    first8 = (jnp.zeros((GROUPS, states), jnp.int32) + c) == 0

    def back(i, carry):
        at = at_step(length - 1 - i)
        a_re, a_im = inj_re[at, :] + carry[0], inj_im[at, :] + carry[1]
        adj_re[at, :] = a_re
        adj_im[at, :] = a_im
        l_re, l_im = conj_times(dec_re[at, :], dec_im[at, :], a_re, a_im)
        left_re[at, :] = l_re
        left_im[at, :] = l_im
        o_re, o_im = other_inj_re[at, :] + carry[2], other_inj_im[at, :] + carry[3]
        other_adj[at, :] = jnp.where(first8, o_re, o_im)
        return (l_re, l_im, *conj_times(other_dec_re[at, :], other_dec_im[at, :], o_re, o_im))

    lax.fori_loop(0, length, back, (*own_enter, *other_enter), unroll=True)
    bf_re, bf_im = adj_re[...].astype(BF16), adj_im[...].astype(BF16)
    first = (jnp.zeros((steps, states), jnp.int32) + c) == 0
    own_rows = pl.ds(pl.multiple_of(c * steps, steps), steps)
    adj_cat[own_rows, :] = jnp.where(first, adj_re[...], adj_im[...]).astype(BF16)
    other_steps = pl.ds(pl.multiple_of((1 - c) * steps, steps), steps)
    adj_cat[other_steps, :] = other_adj[...].astype(BF16)
    adj_bf[:, :states] = bf_re
    adj_bf[:, states:] = bf_im

    pl.semaphore_wait(known_sem.at[3], batches - 1)
    kind = z % CLASSES
    around = (2, -2, 1, -1, 0)

    def class_rows(of, at):
        start = of * piece + (piece // 2 if at == -2 else 0)
        size = piece // 2 if abs(at) == 2 else piece
        return pl.ds(pl.multiple_of(start, size), size)

    def near_copy(offset, at):
        src = g_send.at[offset, class_rows((z + at + chips) % CLASSES, at)]
        place = around.index(at)
        dst = g_half.at[offset, place] if abs(at) == 2 else g_full.at[offset, place - 2]
        device = {"seq": 2 * ((z + at + chips) % chips) + c, "batch": (b + offset) % batches}
        return remote(src, dst, gs_send.at[offset, place], gs_recv.at[offset, place], device)

    for copy in turned:
        copy.wait_recv()
    for place, offset in enumerate((2, 1, 3, 0)):
        owner = (b + offset) % batches
        here = pl.ds(pl.multiple_of(owner * width, width), width)
        part = dot(inp_t[here, :], adj_cat[...], 1, 0)
        g_send[offset] = part.astype(BF16)
        for distance in around[:-1]:
            near_copy(offset, distance).start()

        if place == 3:
            z_own[...] = part
        else:
            near_copy(offset, 0).start()

    g_copies = {
        (offset, distance): near_copy(offset, distance)
        for offset in range(batches)
        for distance in around
        if offset or distance
    }

    def gi_part(owner):
        return dot(adj_bf[...], w_in[pl.ds(pl.multiple_of(owner * width, width), width), :], 1, 1)

    gi_copies = []
    for i in range(1, blocks):
        gi_send[i - 1] = gi_part((x + i) % blocks).astype(BF16)
        copy = remote(gi_send.at[i - 1], gi_recv.at[i - 1], gi_ssem.at[i - 1], gi_rsem.at[i - 1], block(i))
        copy.start()
        gi_copies.append(copy)

    drive += part_dot(inp_all, w_in, across)
    drv_re[...] = drive[:, :states]
    drv_im[...] = drive[:, states:]

    def run(i, carry):
        prod_re, prod_im, sum_re, sum_im = carry
        at = at_step(i)
        d_re, d_im = dec_re[at, :], dec_im[at, :]
        prod_re, prod_im = complex_times(d_re, d_im, prod_re, prod_im)
        sum_re, sum_im = pass_on(d_re, d_im, drv_re[at, :], drv_im[at, :], sum_re, sum_im)
        return prod_re, prod_im, sum_re, sum_im

    fwd = lax.fori_loop(0, length, run, (one8, zero8, zero8, zero8), unroll=True)
    fwd_rows = [tuple(part[g : g + 1, :] for part in fwd) for g in range(GROUPS)]
    for copy in saved_copies:
        copy.wait()
    spans = saved_ref.shape[1]
    begin = [None] * GROUPS
    for span in range(spans):
        slot = jnp.zeros((1, states), jnp.int32) + index_ref[0, span]
        at_re, at_im = jnp.zeros((1, states), F32), jnp.zeros((1, states), F32)
        for k in range(spans):
            at_re = jnp.where(slot == k, saved_ref[0, k, 0:1, :], at_re)
            at_im = jnp.where(slot == k, saved_ref[0, k, 1:2, :], at_im)
        for g in range(span * GROUPS // spans, (span + 1) * GROUPS // spans):
            begin[g] = (at_re, at_im)
            at_re, at_im = pass_on(*fwd_rows[g], at_re, at_im)

    def rerun(i, carry):
        at = at_step(i)
        pri_re[at, :] = carry[0]
        pri_im[at, :] = carry[1]
        return pass_on(dec_re[at, :], dec_im[at, :], drv_re[at, :], drv_im[at, :], *carry)

    lax.fori_loop(
        0,
        length,
        rerun,
        tuple(jnp.concatenate([pair[k] for pair in begin], axis=0) for k in range(2)),
        unroll=True,
    )
    wide_re, wide_im = conj_times(pri_re[...], pri_im[...], left_re[...], left_im[...])
    weight = step_col[...]
    z_dec[z] = jnp.concatenate(
        [jnp.sum(weight * part, axis=0, keepdims=True) for part in (wide_re, wide_im)], axis=0
    )
    z_start(lambda i: z_dec.at[z], z_dec.at[z], DECAY)

    for copy in g_copies.values():
        copy.wait_recv()
    total = z_own[class_rows(kind, 0), :]
    for offset in range(batches):
        if offset:
            total += g_full[offset, 2].astype(F32)
        total += g_full[offset, 0].astype(F32) + g_full[offset, 1].astype(F32)
        total += jnp.concatenate([g_half[offset, 0], g_half[offset, 1]], axis=0).astype(F32)
    z_mem[z // CLASSES] = total.astype(BF16)
    member = z_mem.at[z // CLASSES]
    members = []
    for i in sorted(range(chips // CLASSES - 1), key=lambda i: abs(CLASSES * (i + 1) - chips // 2)):
        copy = remote(member, member, zm_send.at[i], zm_recv.at[i], chip(CLASSES * (i + 1)))
        copy.start()
        members.append(copy)

    z_all(z_dec, DECAY).wait_recv()
    part = z_dec[0]
    for j in range(1, chips):
        part += z_dec[j]
    y_dec[b] = part
    dec_copies = []
    for i in range(1, batches):
        copy = remote(y_dec.at[b], y_dec.at[b], yd_send.at[i - 1], yd_recv.at[i - 1], row(i))
        copy.start()
        dec_copies.append(copy)

    for copy in members:
        copy.wait_recv()
    total = z_mem[0].astype(F32)
    for i in range(1, chips // CLASSES):
        total += z_mem[i].astype(F32)
    scale = 1.0 / math.sqrt(batches * seqs * steps)
    gp_bf[c, kind] = (total * scale).astype(BF16)

    def spread(at, core, place):
        rows_of = pl.ds(piece // 2 if at == -2 else 0, piece // 2 if abs(at) == 2 else piece)
        there = gp_ref if abs(at) == 2 else gp_bf
        mine, target = gp_bf.at[c, kind, rows_of], there.at[c, kind, rows_of]
        copy = remote(mine, target, sp_send.at[place], sp_recv.at[place], chip(at + chips, core))
        copy.start()
        return copy

    def hand(of, place):
        gp_outs.append(local(gp_bf.at[c, of], gp_ref.at[c, of], 15 + place - PAIR_PROJ))
        copy = remote(gp_bf.at[c, of], gp_ref.at[c, of], pair_send.at[place], pair_recv.at[place], partner)
        copy.start()
        return copy

    gp_outs = []
    wholes = [spread(1, c, 4), spread(-1, c, 5)]
    halves = [spread(at, core, place) for place, (at, core) in enumerate(((2, c), (-2, c), (2, 1 - c), (-2, 1 - c)))]
    hands = [hand(kind, PAIR_PROJ)]

    own_gi = gi_part(x)
    for i in range(blocks - 1):
        gi_copies[i].wait_recv()
        own_gi += gi_recv[i].astype(F32)
    gi_bf[...] = own_gi.astype(BF16)
    gi_out = local(gi_bf, gi_ref.at[0], 6)

    wholes[0].wait_recv()
    hands.append(hand((kind + CLASSES - 1) % CLASSES, PAIR_PROJ + 1))
    wholes[1].wait_recv()
    hands.append(hand((kind + 1) % CLASSES, PAIR_PROJ + 2))
    for copy in dec_copies:
        copy.wait_recv()
    part = y_dec[0]
    for j in range(1, batches):
        part += y_dec[j]
    pair_dec[c] = part
    dec_pair = remote(pair_dec.at[c], pair_dec.at[c], pair_send.at[PAIR_DECAY], pair_recv.at[PAIR_DECAY], partner)
    dec_pair.start()
    dec_pair.wait_recv()
    gd_own[...] = (pair_dec[0] + pair_dec[1]) / (batches * seqs * steps)
    gd_out = local(gd_own, gd_ref, 13)

    for copy in halves + hands:
        copy.wait_recv()

    for copy in cot_ring + cot_on + inp_ring + inp_on + turned + gi_copies + dec_copies:
        copy.wait_send()
    for copy in (sum_all, dec_pair, *shared, *g_copies.values(), *members, *halves, *wholes, *hands):
        copy.wait_send()
    z_all(z_dec, DECAY).wait_send()
    for copy in (gi_out, gd_out, *gp_outs):
        copy.wait()


def hand_out(gi_in, gp_in, gd_in, gi_out, gp_out, gd_out, gi, gp, gd, wide, sems):
    parts = [(gp_in.at[k], gp.at[k], wide.at[k], gp_out.at[k]) for k in range(2)]
    parts += [(gi_in, gi, gi, gi_out), (gd_in, gd, gd, gd_out)]
    come = [pltpu.make_async_copy(part[0], part[1], sems.at[0, i]) for i, part in enumerate(parts)]
    go = [pltpu.make_async_copy(part[2], part[3], sems.at[1, i]) for i, part in enumerate(parts)]
    for copy in come:
        copy.start()
    for i in range(len(parts)):
        come[i].wait()
        if i < 2:
            wide[i] = gp[i].astype(F32)
        go[i].start()
    for copy in go:
        copy.wait()


def local(sizes, inputs, cotangent, step_size, resets, log_decay, in_proj, out_proj, saved_states, saved_index):
    seqs, batches, blocks = sizes
    chips = seqs // 2
    _, steps, width = inputs.shape
    _, features, states = in_proj.shape
    rows = features // batches
    piece = rows // CLASSES
    hbm_spec = pl.BlockSpec(memory_space=pltpu.HBM)
    per_step = pltpu.VMEM((steps, states), F32)
    dma = pltpu.SemaphoreType.DMA
    grad_inputs, grad_proj, grad_decay = pl.pallas_call(
        functools.partial(kernel, sizes),
        out_shape=(
            jax.ShapeDtypeStruct((1, steps, width), BF16),
            jax.ShapeDtypeStruct((2, CLASSES, piece, states), BF16),
            jax.ShapeDtypeStruct((2, states), F32),
        ),
        in_specs=[hbm_spec] * 9,
        out_specs=(hbm_spec, hbm_spec, hbm_spec),
        scratch_shapes=[
            pltpu.VMEM((blocks, steps, width), BF16),
            pltpu.VMEM((blocks, steps, width), BF16),
            pltpu.VMEM((features, 2 * states), BF16),
            pltpu.VMEM((features, 2 * states), BF16),
            pltpu.VMEM((features, 2 * steps), BF16),
            *([per_step] * 13),
            pltpu.VMEM((steps, 2 * states), BF16),
            *([per_step] * 5),
            pltpu.VMEM((4, GROUPS, states), F32),
            pltpu.VMEM((4, GROUPS, states), F32),
            pltpu.VMEM((2 * steps, states), BF16),
            pltpu.VMEM((seqs, 4, states), F32),
            pltpu.VMEM((blocks - 1, steps, width), BF16),
            pltpu.VMEM((blocks - 1, steps, width), BF16),
            pltpu.VMEM((steps, width), BF16),
            pltpu.VMEM((batches, rows, states), BF16),
            pltpu.VMEM((batches, 3, piece, states), BF16),
            pltpu.VMEM((batches, 2, piece // 2, states), BF16),
            pltpu.VMEM((rows, states), F32),
            pltpu.VMEM((chips // CLASSES, piece, states), BF16),
            pltpu.VMEM((2, CLASSES, piece, states), BF16),
            pltpu.VMEM((chips, 2, states), F32),
            pltpu.VMEM((batches, 2, states), F32),
            pltpu.VMEM((2, 2, states), F32),
            pltpu.VMEM(step_size.shape, F32),
            pltpu.VMEM(resets.shape, jnp.int32),
            pltpu.VMEM(log_decay.shape, F32),
            pltpu.VMEM(saved_states.shape, F32),
            pltpu.SMEM(saved_index.shape, jnp.int32),
            pltpu.VMEM((2, states), F32),
            pltpu.SemaphoreType.REGULAR((4,)),
            dma((18,)),
            dma((2, 6)),
            dma((2, 6)),
            dma((PAIR_INPUTS + blocks,)),
            dma((PAIR_INPUTS + blocks,)),
            dma((2,)),
            dma((2,)),
            dma((batches, 5)),
            dma((batches, 5)),
            dma((chips // CLASSES,)),
            dma((chips // CLASSES,)),
            dma((6,)),
            dma((6,)),
            dma((batches - 1,)),
            dma((batches - 1,)),
            dma((blocks - 1,)),
            dma((blocks - 1,)),
        ],
        compiler_params=pltpu.CompilerParams(
            collective_id=0, has_side_effects=True, vmem_limit_bytes=60 * 1024 * 1024
        ),
    )(cotangent, inputs, step_size, resets, log_decay, in_proj, out_proj, saved_states, saved_index)
    results = (grad_inputs, grad_proj.reshape(2, rows, states), grad_decay)
    return pl.pallas_call(
        hand_out,
        out_shape=[
            jax.ShapeDtypeStruct(grad_inputs.shape, BF16),
            jax.ShapeDtypeStruct((2, rows, states), F32),
            jax.ShapeDtypeStruct(grad_decay.shape, F32),
        ],
        in_specs=[hbm_spec] * 3,
        out_specs=[hbm_spec] * 3,
        scratch_shapes=[
            *(pltpu.VMEM(part.shape, part.dtype) for part in results),
            pltpu.VMEM((2, rows, states), F32),
            dma((2, 4)),
        ],
        compiler_params=pltpu.CompilerParams(vmem_limit_bytes=60 * 1024 * 1024),
    )(*results)


def solution(mesh):
    in_specs = (
        P("batch", "seq", "state"),
        P("batch", "seq", "state"),
        P("batch", "seq"),
        P("batch", "seq"),
        P(None, "state"),
        P(None, None, "state"),
        P(None, None, "state"),
        P("batch", "seq", None, "state"),
        P("batch", "seq"),
    )
    out_specs = (P("batch", "seq", "state"), P(None, "batch", "state"), P(None, "state"))
    sizes = (mesh.shape["seq"], mesh.shape["batch"], mesh.shape["state"])
    return jax.shard_map(
        functools.partial(local, sizes), mesh=mesh, in_specs=in_specs, out_specs=out_specs, check_vma=False
    )
```
